32 devices in a mesh: wide: 8 (over z, x), narrow: 4 (over y, core).
Axes of the slice: x: 2, y: 2, z: 4, core: 2. Of those that a mesh axis runs over, the one named last changes fastest.
Arguments:
- layer_input: bfloat16 [8, 1024, 2048], P('wide', 'narrow'), may hold values from -6 to 6
- out_grad: bfloat16 [8, 1024, 2048], P('wide', 'narrow'), may hold values from -6 to 6
- lengths: int32 [8], P('wide'), may hold values from 769 to 1024, as said below
- query_weight: float32 [2048, 2048], P('wide', 'narrow'), may hold values from -0.125 to 0.125
- query_mean: float32 [2048, 2048], P('wide', 'narrow'), may hold values from -256 to 256
- query_square: float32 [2048, 2048], P('wide', 'narrow'), may hold values from 2048 to 8192
- keyval_weight: float32 [2, 2048, 1024], P(None, 'wide', 'narrow'), may hold values from -0.125 to 0.125
- keyval_mean: float32 [2, 2048, 1024], P(None, 'wide', 'narrow'), may hold values from -256 to 256
- keyval_square: float32 [2, 2048, 1024], P(None, 'wide', 'narrow'), may hold values from 2048 to 8192
- output_weight: float32 [2048, 2048], P('narrow', 'wide'), may hold values from -1 to 1
- output_mean: float32 [2048, 2048], P('narrow', 'wide'), may hold values from -56 to 56
- output_square: float32 [2048, 2048], P('narrow', 'wide'), may hold values from 81.92 to 327.68
- gateup_weight: float32 [2, 2048, 6144], P(None, 'wide', 'narrow'), may hold values from -0.125 to 0.125
- gateup_mean: float32 [2, 2048, 6144], P(None, 'wide', 'narrow'), may hold values from -160 to 160
- gateup_square: float32 [2, 2048, 6144], P(None, 'wide', 'narrow'), may hold values from 737.28 to 2949.12
- down_weight: float32 [6144, 2048], P('narrow', 'wide'), may hold values from -0.078125 to 0.078125
- down_mean: float32 [6144, 2048], P('narrow', 'wide'), may hold values from -256 to 256
- down_square: float32 [6144, 2048], P('narrow', 'wide'), may hold values from 2048 to 8192
- norm_gains: float32 [2, 2048], P(None, 'wide'), may hold values from 0.5 to 1.5
- norm_mean: float32 [2, 2048], P(None, 'wide'), may hold values from -512 to 512
- norm_square: float32 [2, 2048], P(None, 'wide'), may hold values from 8192 to 32768
- head_gains: float32 [2, 128], P(None, 'wide'), may hold values from 0.5 to 1.5
- head_mean: float32 [2, 128], P(None, 'wide'), may hold values from -2048 to 2048
- head_square: float32 [2, 128], P(None, 'wide'), may hold values from 131072 to 524288
Outputs:
- layer_out: bfloat16 [8, 1024, 2048], P('wide', 'narrow')
- input_grad: float32 [8, 1024, 2048], P('wide', 'narrow')
- query_new: float32 [2048, 2048], P('wide', 'narrow')
- query_first: float32 [2048, 2048], P('wide', 'narrow')
- query_second: float32 [2048, 2048], P('wide', 'narrow')
- keyval_new: float32 [2, 2048, 1024], P(None, 'wide', 'narrow')
- keyval_first: float32 [2, 2048, 1024], P(None, 'wide', 'narrow')
- keyval_second: float32 [2, 2048, 1024], P(None, 'wide', 'narrow')
- output_new: float32 [2048, 2048], P('narrow', 'wide')
- output_first: float32 [2048, 2048], P('narrow', 'wide')
- output_second: float32 [2048, 2048], P('narrow', 'wide')
- gateup_new: float32 [2, 2048, 6144], P(None, 'wide', 'narrow')
- gateup_first: float32 [2, 2048, 6144], P(None, 'wide', 'narrow')
- gateup_second: float32 [2, 2048, 6144], P(None, 'wide', 'narrow')
- down_new: float32 [6144, 2048], P('narrow', 'wide')
- down_first: float32 [6144, 2048], P('narrow', 'wide')
- down_second: float32 [6144, 2048], P('narrow', 'wide')
- norm_new: float32 [2, 2048], P(None, 'wide')
- norm_first: float32 [2, 2048], P(None, 'wide')
- norm_second: float32 [2, 2048], P(None, 'wide')
- head_new: float32 [2, 128], P(None, 'wide')
- head_first: float32 [2, 128], P(None, 'wide')
- head_second: float32 [2, 128], P(None, 'wide')
The draws below stay inside these ranges and needn't reach their ends.
Inputs may be any that keep to these rules, and one draw needn't show every extreme that they name: `lengths`: each row's count of valid tokens from its start; one row has exactly 1024 and one exactly 769.
All inputs are finite; a program needn't handle non-finite values.
Results may differ from the reference program's by a relative error of at most 0.015.
The reference program's roundings to bfloat16 on the way count: a program that leaves them out, or rounds other values in their place, can miss the bound.
Values may be sent and summed in bfloat16 or wider, within the bound.
A program may use at most 256 MiB of HBM per device.

```python
import math
import jax
import jax.numpy as jnp
from jax import lax

D = 2048
H = 16
KV = 8
HD = 128
FF = 6144
L = 1024
STEP = 5
SEQS = 8


def draw_lengths(key, part):
    key = jax.random.fold_in(key, 11)
    first_key, second_key = jax.random.split(key)
    lowest = 3 * L // 4 + 1
    drawn = jax.random.randint(first_key, (SEQS,), lowest, L + 1)
    order = jax.random.permutation(second_key, SEQS)
    places = jnp.arange(SEQS)
    drawn = jnp.where(places == order[0], L, drawn)
    drawn = jnp.where(places == order[1], lowest, drawn)
    return drawn.astype(jnp.int32)


def levels(own_key, shape, cuts, low, high):
    gain, own = 1.0, jax.random.fold_in(own_key, 6)
    for position, shards_of in cuts:
        heights = jnp.exp(jax.random.uniform(jax.random.fold_in(own, position), (shards_of,), jnp.float32, low / len(cuts), high / len(cuts)))
        gain = gain * jnp.repeat(heights, shape[position] // shards_of).reshape([-1 if axis == position else 1 for axis in range(len(shape))])
    return gain


def gaussian(rng, shape, deviation, bound, cuts=(), held_as=jnp.bfloat16):
    result = deviation * jax.random.normal(rng, shape, jnp.float32)
    if cuts:
        result = result * levels(rng, shape, cuts, -0.22, 0.18)
    return jnp.clip(result, -bound, bound).astype(held_as)


def setup_inputs(seed: int = 0) -> dict:
    streams_of = jax.random.split(jax.random.key(seed), 25)
    layer_input = gaussian(streams_of[0], (SEQS, L, D), 1.0, 6.0, ((0, 8), (1, 4)))
    out_grad = gaussian(streams_of[1], (SEQS, L, D), 1.0, 6.0, ((0, 8), (1, 4)))
    lengths = draw_lengths(jax.random.fold_in(streams_of[24], 71), 0)
    query_weight = gaussian(streams_of[3], (D, H * HD), D ** -0.5, 0.125, ((0, 8), (1, 4)), jnp.float32)
    query_mean = gaussian(streams_of[4], (D, H * HD), (0.5 * (SEQS * L) ** 0.5), 256.0, ((0, 8), (1, 4)), jnp.float32)
    query_square = jnp.clip(jnp.exp(math.log(8192.0) - 1.3862944 * jax.random.uniform(streams_of[5], (D, H * HD), jnp.float32) ** levels(streams_of[5], (D, H * HD), ((0, 8), (1, 4)), -0.2, 0.2)), 2048.0, 8192.0)
    keyval_weight = gaussian(streams_of[6], (2, D, KV * HD), D ** -0.5, 0.125, ((1, 8), (2, 4)), jnp.float32)
    keyval_mean = gaussian(streams_of[7], (2, D, KV * HD), (0.5 * (SEQS * L) ** 0.5), 256.0, ((1, 8), (2, 4)), jnp.float32)
    keyval_square = jnp.clip(jnp.exp(math.log(8192.0) - 1.3862944 * jax.random.uniform(streams_of[8], (2, D, KV * HD), jnp.float32) ** levels(streams_of[8], (2, D, KV * HD), ((1, 8), (2, 4)), -0.2, 0.2)), 2048.0, 8192.0)
    output_weight = gaussian(streams_of[9], (H * HD, D), (H * HD // 64) ** -0.5, 1.0, ((0, 4), (1, 8)), jnp.float32)
    output_mean = gaussian(streams_of[10], (H * HD, D), (0.1 * (SEQS * L) ** 0.5), 56.0, ((0, 4), (1, 8)), jnp.float32)
    output_square = jnp.clip(jnp.exp(math.log(327.68) - 1.3862944 * jax.random.uniform(streams_of[11], (H * HD, D), jnp.float32) ** levels(streams_of[11], (H * HD, D), ((0, 4), (1, 8)), -0.2, 0.2)), 81.92, 327.68)
    gateup_weight = gaussian(streams_of[12], (2, D, FF), D ** -0.5, 0.125, ((1, 8), (2, 4)), jnp.float32)
    gateup_mean = gaussian(streams_of[13], (2, D, FF), (0.3 * (SEQS * L) ** 0.5), 160.0, ((1, 8), (2, 4)), jnp.float32)
    gateup_square = jnp.clip(jnp.exp(math.log(2949.12) - 1.3862944 * jax.random.uniform(streams_of[14], (2, D, FF), jnp.float32) ** levels(streams_of[14], (2, D, FF), ((1, 8), (2, 4)), -0.2, 0.2)), 737.28, 2949.12)
    down_weight = gaussian(streams_of[15], (FF, D), FF ** -0.5, 0.078125, ((0, 4), (1, 8)), jnp.float32)
    down_mean = gaussian(streams_of[16], (FF, D), (0.5 * (SEQS * L) ** 0.5), 256.0, ((0, 4), (1, 8)), jnp.float32)
    down_square = jnp.clip(jnp.exp(math.log(8192.0) - 1.3862944 * jax.random.uniform(streams_of[17], (FF, D), jnp.float32) ** levels(streams_of[17], (FF, D), ((0, 4), (1, 8)), -0.2, 0.2)), 2048.0, 8192.0)
    norm_gains = jnp.clip(1.0 + 0.1 * jax.random.normal(streams_of[18], (2, D), jnp.float32), 0.5, 1.5)
    norm_mean = gaussian(streams_of[19], (2, D), ((SEQS * L) ** 0.5), 512.0, ((1, 8),), jnp.float32)
    norm_square = jnp.clip(jnp.exp(math.log(32768.0) - 1.3862944 * jax.random.uniform(streams_of[20], (2, D), jnp.float32) ** levels(streams_of[20], (2, D), ((1, 8),), -0.2, 0.2)), 8192.0, 32768.0)
    head_gains = jnp.clip(1.0 + 0.1 * jax.random.normal(streams_of[21], (2, HD), jnp.float32), 0.5, 1.5)
    head_mean = gaussian(streams_of[22], (2, HD), ((SEQS * L * H) ** 0.5), 2048.0, ((1, 8),), jnp.float32)
    head_square = jnp.clip(jnp.exp(math.log(524288.0) - 1.3862944 * jax.random.uniform(streams_of[23], (2, HD), jnp.float32) ** levels(streams_of[23], (2, HD), ((1, 8),), -0.2, 0.2)), 131072.0, 524288.0)
    return dict(layer_input=layer_input, out_grad=out_grad, lengths=lengths, query_weight=query_weight, query_mean=query_mean, query_square=query_square, keyval_weight=keyval_weight, keyval_mean=keyval_mean, keyval_square=keyval_square, output_weight=output_weight, output_mean=output_mean, output_square=output_square, gateup_weight=gateup_weight, gateup_mean=gateup_mean, gateup_square=gateup_square, down_weight=down_weight, down_mean=down_mean, down_square=down_square, norm_gains=norm_gains, norm_mean=norm_mean, norm_square=norm_square, head_gains=head_gains, head_mean=head_mean, head_square=head_square)


@jax.custom_vjp
def low(v):
    return lax.optimization_barrier(v.astype(jnp.bfloat16)).astype(jnp.float32)

@jax.custom_vjp
def low_back(v):
    return v

def low_keep(v):
    return (low(v), None)

def low_pass(kept, grad):
    return (grad,)

def back_keep(v):
    return (v, None)

def back_low(kept, grad):
    return (low(grad),)
low.defvjp(low_keep, low_pass)
low_back.defvjp(back_keep, back_low)
norm_eps = 1e-06
rope_base = 1000000.0
beta_first = 0.5
beta_second = 0.5
adam_eps = 1e-08
weight_decay = 0.1
masked_fill = -1e+30
highest = lax.Precision.HIGHEST

def row_scale(values):
    return lax.rsqrt(lax.optimization_barrier(jnp.mean(values * values, axis=-1, keepdims=True)) + norm_eps)

def rope_tables(length):
    half = HD // 2
    freqs = rope_base ** (-(jnp.arange(half, dtype=jnp.float32) * 2.0) / HD)
    angles = jnp.arange(length, dtype=jnp.float32)[:, None] * freqs[None, :]
    cosine = jnp.cos(angles)
    sine = jnp.sin(angles)
    return (jnp.concatenate([cosine, cosine], axis=-1)[:, None, :], jnp.concatenate([sine, sine], axis=-1)[:, None, :])

def rotate(values, cosine, sine):
    half = values.shape[-1] // 2
    turned = jnp.concatenate([-values[..., half:], values[..., :half]], axis=-1)
    return values * cosine + turned * sine

def matmul(left, right):
    return jnp.matmul(left, right, precision=highest)

def attend(queries, keys, values, row_lengths):
    batch = queries.shape[0]
    block_rows = min(512, L)
    count = L // block_rows
    groups = H // KV
    blocks = queries.reshape(batch, count, block_rows, KV, groups, HD).transpose(1, 0, 2, 3, 4, 5)
    starts = (jnp.arange(count) * block_rows).astype(jnp.int32)

    def one_block(carry, pieces):
        query_block, start = pieces
        scores = jnp.einsum('bqkgd,btkd->bkgqt', query_block, keys, precision=highest) * HD ** (-0.5)
        scores = low_back(scores)
        rows = start + jnp.arange(block_rows).astype(jnp.int32)
        columns = jnp.arange(L).astype(jnp.int32)
        allowed = (columns[None, None, :] <= rows[None, :, None]) & (columns[None, None, :] < row_lengths[:, None, None])
        scores = jnp.where(allowed[:, None, None], scores, masked_fill)
        weights = low(jax.nn.softmax(scores, axis=-1))
        return (carry, jnp.einsum('bkgqt,btkd->bqkgd', weights, values, precision=highest))
    unused, outputs = lax.scan(jax.checkpoint(one_block), jnp.zeros((), jnp.float32), (blocks, starts))
    return outputs.transpose(1, 0, 2, 3, 4, 5).reshape(batch, L, H, HD)

def layer(params, inputs, row_lengths):
    query_matrix, key_value_matrix, output_matrix, gate_up_matrix, down_matrix, gain_norm, gain_head = [low(item) for item in params]
    batch = inputs.shape[0]
    normed_rows = low(inputs * row_scale(inputs) * gain_norm[0])
    query_raw = low_back(matmul(normed_rows, query_matrix)).reshape(batch, L, H, HD)
    key_raw = low_back(matmul(normed_rows, key_value_matrix[0])).reshape(batch, L, KV, HD)
    value_raw = low_back(matmul(normed_rows, key_value_matrix[1])).reshape(batch, L, KV, HD)
    cosine, sine = rope_tables(L)
    queries = low(rotate(query_raw * row_scale(query_raw) * gain_head[0], cosine, sine))
    keys = low(rotate(key_raw * row_scale(key_raw) * gain_head[1], cosine, sine))
    values = low(value_raw)
    context_rows = attend(queries, keys, values, row_lengths)
    context_rows = low(low_back(context_rows)).reshape(batch, L, H * HD)
    resid = inputs + low_back(matmul(context_rows, output_matrix))
    mixed_rows = low(resid * row_scale(resid) * gain_norm[1])
    gate_rows = low_back(matmul(mixed_rows, gate_up_matrix[0]))
    up_rows = low_back(matmul(mixed_rows, gate_up_matrix[1]))
    hidden_rows = low(jax.nn.silu(gate_rows) * up_rows)
    return resid + low_back(matmul(hidden_rows, down_matrix))

def adamw(weight, first, second, grad, rate):
    first_new = beta_first * first + (1.0 - beta_first) * grad
    second_new = beta_second * second + (1.0 - beta_second) * grad * grad
    first_hat = first_new / (1.0 - beta_first ** STEP)
    second_hat = second_new / (1.0 - beta_second ** STEP)
    weight_new = weight - rate * (first_hat / (jnp.sqrt(second_hat) + adam_eps) + weight_decay * weight)
    return (weight_new, first_new, second_new)

def reference(layer_input, out_grad, lengths, query_weight, query_mean, query_square, keyval_weight, keyval_mean, keyval_square, output_weight, output_mean, output_square, gateup_weight, gateup_mean, gateup_square, down_weight, down_mean, down_square, norm_gains, norm_mean, norm_square, head_gains, head_mean, head_square):
    masters = (query_weight, keyval_weight, output_weight, gateup_weight, down_weight, norm_gains, head_gains)
    group = min(SEQS, max(1, 4096 // L))
    count = SEQS // group
    inputs = layer_input.astype(jnp.float32).reshape(count, group, L, D)
    cotangent = out_grad.astype(jnp.float32).reshape(count, group, L, D)
    grouped_lengths = lengths.reshape(count, group)

    def one_group(totals, pieces):
        block_input, block_cot, block_lengths = pieces

        def forward(params, values):
            return layer(params, values, block_lengths)
        outputs, pullback = jax.vjp(forward, masters, block_input)
        valid = (jnp.arange(L).astype(jnp.int32)[None, :] < block_lengths[:, None]).astype(jnp.float32)
        param_grads, input_grads = pullback(block_cot * valid[:, :, None])
        totals = jax.tree.map(lambda left, right: left + right, totals, param_grads)
        return (totals, (outputs.astype(jnp.bfloat16), input_grads))
    zeros = jax.tree.map(jnp.zeros_like, masters)
    grads, (results, input_grads) = lax.scan(one_group, zeros, (inputs, cotangent, grouped_lengths))
    layer_out = results.reshape(SEQS, L, D)
    input_grad = input_grads.reshape(SEQS, L, D)
    query_new, query_first, query_second = adamw(query_weight, query_mean, query_square, grads[0], 0.04)
    keyval_new, keyval_first, keyval_second = adamw(keyval_weight, keyval_mean, keyval_square, grads[1], 0.04)
    output_new, output_first, output_second = adamw(output_weight, output_mean, output_square, grads[2], 0.3)
    gateup_new, gateup_first, gateup_second = adamw(gateup_weight, gateup_mean, gateup_square, grads[3], 0.04)
    down_new, down_first, down_second = adamw(down_weight, down_mean, down_square, grads[4], 0.025)
    norm_new, norm_first, norm_second = adamw(norm_gains, norm_mean, norm_square, grads[5], 0.4)
    head_new, head_first, head_second = adamw(head_gains, head_mean, head_square, grads[6], 0.4)
    return (layer_out, input_grad, query_new, query_first, query_second, keyval_new, keyval_first, keyval_second, output_new, output_first, output_second, gateup_new, gateup_first, gateup_second, down_new, down_first, down_second, norm_new, norm_first, norm_second, head_new, head_first, head_second)
```

```python
import functools

import jax
import jax.numpy as jnp
from jax import lax
from jax.experimental import pallas as pl
from jax.experimental.pallas import tpu as pltpu
from jax.sharding import PartitionSpec as P

HD = 128
STEP = 5
MESH = pl.DeviceIdType.MESH
MIB = 2**20

norm_eps = 1e-06
rope_base = 1000000.0
beta_first = 0.5
beta_second = 0.5
adam_eps = 1e-08
weight_decay = 0.1
masked_fill = -1e30
f32 = jnp.float32
bf16 = jnp.bfloat16


def row_scale(values):
    return lax.rsqrt(jnp.mean(values * values, axis=-1, keepdims=True) + norm_eps)


def norm_back(grad, unit, scale, gain):
    scaled = grad * gain
    return scale * (scaled - unit * jnp.mean(scaled * unit, axis=-1, keepdims=True))


def adamw(weight, first, second, grad, rate):
    first_new = beta_first * first + (1.0 - beta_first) * grad
    second_new = beta_second * second + (1.0 - beta_second) * grad * grad
    first_hat = first_new / (1.0 - beta_first**STEP)
    second_hat = second_new / (1.0 - beta_second**STEP)
    weight_new = weight - rate * (
        first_hat / (jnp.sqrt(second_hat) + adam_eps) + weight_decay * weight
    )
    return (weight_new, first_new, second_new)


def rope_tables(length):
    half = HD // 2
    freqs = rope_base ** (-(jnp.arange(half, dtype=f32) * 2.0) / HD)
    angles = jnp.arange(length, dtype=f32)[:, None] * freqs[None, :]
    cosine = jnp.cos(angles)
    sine = jnp.sin(angles)
    return (
        jnp.concatenate([cosine, cosine], axis=-1),
        jnp.concatenate([-sine, sine], axis=-1),
    )


def dot_nn(left, right):
    return lax.dot_general(left, right, (((1,), (0,)), ((), ())), preferred_element_type=f32)


def dot_nt(left, right):
    return lax.dot_general(left, right, (((1,), (1,)), ((), ())), preferred_element_type=f32)


def dot_tn(left, right):
    return lax.dot_general(left, right, (((0,), (0,)), ((), ())), preferred_element_type=f32)


def loop(count, step):
    def body(index, carry):
        step(index)
        return carry

    lax.fori_loop(0, count, body, 0)


def rows(index, size):
    return pl.ds(pl.multiple_of(index * size, size), size)


class Place:
    def __init__(self, wide, narrow):
        self.depth = wide // 2
        w = lax.axis_index("wide")
        n = lax.axis_index("narrow")
        self.w, self.n = w, n
        self.z = w // 2
        self.x = w - 2 * self.z
        self.y = n // 2
        self.c = n - 2 * self.y

    def far(self, k, dx):
        x = self.x if dx == 0 else 1 - self.x
        return (lax.rem(self.z + k, self.depth) * 2 + x, self.n)

    def side(self, dy, dc):
        y = self.y if dy == 0 else 1 - self.y
        c = self.c if dc == 0 else 1 - self.c
        return (self.w, y * 2 + c)

    def slot(self, block):
        ay, ac = block // 2, block % 2
        dy = lax.rem(self.y + ay, 2)
        dc = lax.rem(self.c + ac, 2)
        return dc * 2 + dy


def remote(src, dst, send, recv, device):
    return pltpu.make_async_remote_copy(
        src_ref=src,
        dst_ref=dst,
        send_sem=send,
        recv_sem=recv,
        device_id=device,
        device_id_type=MESH,
    )


class Side:
    def __init__(self, place, send, recv):
        self.place, self.send, self.recv = place, send, recv
        self.used = 0
        self.sent = []

    def copy(self, src, dst, dy, dc):
        i = self.used
        self.used += 1
        made = remote(src, dst, self.send.at[i], self.recv.at[i], self.place.side(dy, dc))
        made.start()
        self.sent.append(made)
        return made

    def drain(self):
        for made in self.sent:
            made.wait_send()


class Gather:
    def __init__(self, side, own, buf, size):
        self.side, self.buf, self.size = side, buf, size
        self.across = side.copy(own, buf.at[pl.ds(size, size)], 1, 0)
        self.core = side.copy(own, buf.at[pl.ds(2 * size, size)], 0, 1)

    def forward(self):
        size = self.size
        self.across.wait_recv()
        self.last = self.side.copy(
            self.buf.at[pl.ds(size, size)], self.buf.at[pl.ds(3 * size, size)], 0, 1
        )

    def done(self):
        self.core.wait_recv()
        self.last.wait_recv()


class Wide:
    def __init__(self, place, block, chunks, own, full, zs, zr, xs, xr):
        self.place, self.block, self.chunks, self.own, self.full = place, block, chunks, own, full
        self.zs, self.zr, self.xs, self.xr = zs, zr, xs, xr
        self.near = place.depth == 4

    def slot(self, i, index):
        g, a, b = self.chunks[i]
        return self.full[g].at[pl.ds(index * self.block, self.block), pl.ds(a, b - a)]

    def mine(self, i):
        g, a, b = self.chunks[i]
        return self.own[g].at[:, pl.ds(a, b - a)]

    def along(self, i, k):
        depth = self.place.depth
        return remote(
            self.mine(i),
            self.slot(i, k),
            self.zs.at[i, k],
            self.zr.at[i, k],
            self.place.far(depth - k, 0),
        )

    def beyond(self, i, k):
        depth = self.place.depth
        return remote(
            self.slot(i, 2),
            self.slot(i, k),
            self.zs.at[i, depth + k],
            self.zr.at[i, k],
            self.place.far(1 if k == 1 else depth - 1, 0),
        )

    def across(self, i, k):
        depth = self.place.depth
        src = self.mine(i) if k == 0 else self.slot(i, k)
        return remote(
            src, self.slot(i, depth + k), self.xs.at[i, k], self.xr.at[i, k], self.place.far(0, 1)
        )

    def each(self, i, k, act):
        place = self.place
        if self.near and k in (1, 3):
            at_end = (place.z == 0) if k == 1 else (place.z == 3)

            @pl.when(jnp.logical_not(at_end))
            def _():
                act(self.along(i, k))
        else:
            act(self.along(i, k))

    def order(self):
        depth = self.place.depth
        return (2, 1, 3) if self.near else tuple(range(1, depth))

    def issue(self, i):
        if i >= len(self.chunks):
            return
        self.across(i, 0).start()
        for k in self.order():
            self.each(i, k, lambda made: made.start())

    def hand_on(self, i):
        z = self.place.z
        for k in self.order():
            self.along(i, k).wait_recv()
            if self.near and k == 2:

                @pl.when(z == 2)
                def _():
                    self.beyond(i, 1).start()

                @pl.when(z == 1)
                def _():
                    self.beyond(i, 3).start()

            self.across(i, k).start()

    def arrived(self, i):
        for k in range(self.place.depth):
            self.across(i, k).wait_recv()

    def drain(self):
        z = self.place.z
        for i in range(len(self.chunks)):
            for k in range(self.place.depth):
                if k:
                    self.each(i, k, lambda made: made.wait_send())
                if self.near and k in (1, 3):

                    @pl.when(z == (2 if k == 1 else 1))
                    def _():
                        self.beyond(i, k).wait_send()

                self.across(i, k).wait_send()


def greet(place):
    depth = place.depth
    peers = [place.far(k, dx) for dx in (0, 1) for k in range(depth) if k or dx]
    peers += [place.side(1, 0), place.side(0, 1)]
    barrier = pltpu.get_barrier_semaphore()
    for peer in peers:
        pl.semaphore_signal(barrier, inc=1, device_id=peer, device_id_type=MESH)
    pl.semaphore_wait(barrier, len(peers))


def turn(values):
    return pltpu.roll(values, HD // 2, 1)


def rope(values, cosine, sine):
    return values * cosine + turn(values) * sine


def rope_back(grads, cosine, sine):
    return grads * cosine - turn(grads) * sine


def softmax_block(query, keys, block, size, count, length):
    scores = dot_nt(query, keys) * HD ** (-0.5)
    shape = scores.shape
    at = block * size + lax.broadcasted_iota(jnp.int32, shape, 0)
    to = lax.broadcasted_iota(jnp.int32, shape, 1)
    scores = jnp.where((to <= at) & (to < length), scores, masked_fill)
    lifted = jnp.exp(scores - jnp.max(scores, axis=-1, keepdims=True))
    return lifted / jnp.sum(lifted, axis=-1, keepdims=True)


def chunks_of(widths):
    qkv, out, gate, up, down = widths
    return [
        (0, 0, qkv // 2),
        (0, qkv // 2, qkv),
        (1, 0, out),
        (2, 0, gate // 2),
        (3, 0, up // 2),
        (2, gate // 2, gate),
        (3, up // 2, up),
        (4, 0, down // 2),
        (4, down // 2, down),
    ]


def forward_kernel(
    wide,
    heads,
    pairs,
    length_ref,
    x_ref,
    gain_ref,
    cos_ref,
    sin_ref,
    dyb_ref,
    own_qkv,
    own_out,
    own_gate,
    own_up,
    own_down,
    full_qkv,
    full_out,
    full_gate,
    full_up,
    full_down,
    o_dyb,
    o_normed,
    o_qkv,
    o_ctx,
    o_resid,
    o_mixed,
    o_gate,
    o_up,
    o_hidden,
    gains,
    head_gain,
    slots,
    normed,
    qkv,
    ctx,
    resid,
    mixed,
    gate,
    up,
    hidden,
    weights,
    k_act,
    v_act,
    half_out,
    half_in,
    cross_out,
    cross_in,
    zs,
    zr,
    xs,
    xr,
    ns,
    nr,
    gs,
    gr,
    ls,
):
    place = Place(wide, 4)
    depth = place.depth
    size, width = x_ref.shape
    block = width // wide
    ff = gate.shape[1]
    groups = heads // pairs
    span = 4 * size
    own = [own_qkv, own_out, own_gate, own_up, own_down]
    full = [full_qkv, full_out, full_gate, full_up, full_down]
    chunks = chunks_of([ref.shape[1] for ref in full])
    greet(place)
    ag = Wide(place, block, chunks, own, full, zs, zr, xs, xr)
    side = Side(place, ns, nr)

    gain_copies = []
    for dx in (0, 1):
        for k in range(depth):
            if k or dx:
                at = dx * depth + (depth - k) % depth
                made = remote(
                    gain_ref, slots.at[at], gs.at[at], gr.at[at], place.far(k, dx)
                )
                made.start()
                gain_copies.append(made)
    for i in range(3):
        ag.issue(i)
    local = []

    def keep(src, dst):
        made = pltpu.make_async_copy(src, dst, ls.at[len(local)])
        made.start()
        local.append(made)
        return made

    for g in range(5):
        keep(own[g], full[g].at[pl.ds(0, block)])
    keep(dyb_ref, o_dyb.at[pl.ds(0, size)])
    slots[0] = gain_ref[...]
    for made in gain_copies:
        made.wait_recv()
    gains[...] = jnp.concatenate([slots[b][:, :block] for b in range(wide)], axis=1)
    total = slots[0][:, :HD]
    for b in range(1, wide):
        total = total + slots[b][:, :HD]
    head_gain[...] = total

    def first_norm(i):
        at = rows(i, size // 4)
        x = x_ref[at, :].astype(f32)
        normed[at, :] = (x * row_scale(x) * gains[0:1, :]).astype(bf16)

    loop(4, first_norm)
    take_normed = Gather(side, normed.at[pl.ds(0, size)], normed, size)
    take_dyb = Gather(side, dyb_ref, o_dyb, size)
    take_normed.forward()
    ag.hand_on(0)
    ag.issue(3)
    take_dyb.forward()
    take_normed.done()
    keep(normed, o_normed)
    ag.hand_on(1)
    ag.issue(4)
    ag.arrived(0)
    ag.arrived(1)
    qkv_width = full_qkv.shape[1]
    out_width = full_out.shape[1]
    w_qkv = weights.at[:, pl.ds(0, qkv_width)]
    w_out = weights.at[:, pl.ds(qkv_width, out_width)]
    local[0].wait()
    get = pltpu.make_async_copy(full_qkv, w_qkv, ls.at[20])
    get.start()
    get.wait()

    def project(m):
        for n in range(qkv_width // 512):
            qkv[rows(m, size), pl.ds(n * 512, 512)] = dot_nn(
                normed[rows(m, size), :], weights[:, pl.ds(n * 512, 512)]
            )

    loop(4, project)
    keep(qkv, o_qkv)
    ag.hand_on(2)
    ag.issue(5)

    length = length_ref[0]

    def pair(p):
        def keys(a):
            at = rows(place.slot(a), size)
            to = pl.ds(a * size, size)
            raw = qkv[at, pl.ds(pl.multiple_of((heads + p) * HD, HD), HD)]
            unit = raw * row_scale(raw) * head_gain[3:4, :]
            k_act[to, :] = rope(unit, cos_ref[to, :], sin_ref[to, :]).astype(bf16)
            v_act[to, :] = qkv[
                at, pl.ds(pl.multiple_of((heads + pairs + p) * HD, HD), HD)
            ].astype(bf16)

        for a in range(4):
            keys(a)

        def head(g):
            column = pl.ds(pl.multiple_of((p * groups + g) * HD, HD), HD)
            for a in range(4):
                at = rows(place.slot(a), size)
                to = pl.ds(a * size, size)
                raw = qkv[at, column]
                unit = raw * row_scale(raw) * head_gain[2:3, :]
                query = rope(unit, cos_ref[to, :], sin_ref[to, :]).astype(bf16)
                last = (a + 1) * size
                probs = softmax_block(query, k_act[0:last, :], a, size, last, length)
                ctx[at, column] = dot_nn(probs.astype(bf16), v_act[0:last, :]).astype(bf16)

        loop(groups, head)

    loop(pairs, pair)
    keep(ctx, o_ctx)
    ag.hand_on(3)
    ag.issue(6)
    ag.arrived(2)
    local[1].wait()
    get = pltpu.make_async_copy(full_out, w_out, ls.at[21])
    get.start()
    get.wait()

    step = 512

    def to_core(n):
        at = rows(n, step)
        half_out[:, at] = dot_nt(
            ctx[pl.ds(2 * size, 2 * size), :], weights[at, pl.ds(qkv_width, out_width)]
        ).astype(bf16)

    loop(width // step, to_core)
    core = side.copy(half_out, half_in, 0, 1)
    core.wait_recv()

    def to_other(n):
        at = rows(n, step)
        cross_out[:, at] = (
            dot_nt(ctx[pl.ds(size, size), :], weights[at, pl.ds(qkv_width, out_width)])
            + half_in[pl.ds(size, size), at].astype(f32)
        ).astype(bf16)

    loop(width // step, to_other)
    other = side.copy(cross_out, cross_in, 1, 0)

    def to_self(n):
        at = rows(n, step)
        resid[:, at] = (
            dot_nt(ctx[pl.ds(0, size), :], weights[at, pl.ds(qkv_width, out_width)])
            + half_in[pl.ds(0, size), at].astype(f32)
            + x_ref[:, at].astype(f32)
        )

    loop(width // step, to_self)
    other.wait_recv()

    def second_norm(i):
        at = rows(i, size // 4)
        value = resid[at, :] + cross_in[at, :].astype(f32)
        resid[at, :] = value
        mixed[at, :] = (value * row_scale(value) * gains[1:2, :]).astype(bf16)

    loop(4, second_norm)
    take_mixed = Gather(side, mixed.at[pl.ds(0, size)], mixed, size)
    keep(resid, o_resid)
    ag.hand_on(4)
    ag.issue(7)
    take_mixed.forward()
    take_mixed.done()
    take_dyb.done()
    keep(mixed, o_mixed)
    ag.hand_on(5)
    ag.issue(8)
    half = ff // 2

    def feed(part):
        a = part * half
        get_gate = pltpu.make_async_copy(
            full_gate.at[:, pl.ds(a, half)], weights.at[:, pl.ds(0, half)], ls.at[22]
        )
        get_up = pltpu.make_async_copy(
            full_up.at[:, pl.ds(a, half)], weights.at[:, pl.ds(half, half)], ls.at[23]
        )
        get_gate.start()
        get_up.start()
        get_gate.wait()
        get_up.wait()
        tile = 256

        def columns(n):
            def body(m):
                at = rows(m, size)
                left = mixed[at, :]
                gate_part = dot_nn(left, weights[:, rows(n, tile)])
                up_part = dot_nn(
                    left, weights[:, pl.ds(pl.multiple_of(half + n * tile, tile), tile)]
                )
                to = pl.ds(pl.multiple_of(a + n * tile, tile), tile)
                gate[at, to] = gate_part
                up[at, to] = up_part
                hidden[at, to] = (gate_part * jax.nn.sigmoid(gate_part) * up_part).astype(bf16)

            loop(4, body)

        loop(half // tile, columns)

    local[2].wait()
    local[3].wait()
    ag.arrived(3)
    ag.arrived(4)
    feed(0)
    ag.hand_on(6)
    ag.arrived(5)
    ag.arrived(6)
    feed(1)
    keep(gate, o_gate)
    keep(up, o_up)
    keep(hidden, o_hidden)
    ag.hand_on(7)
    ag.hand_on(8)
    ag.arrived(7)
    ag.arrived(8)
    for i, made in enumerate(local):
        if i > 3:
            made.wait()
    for made in gain_copies:
        made.wait_send()
    side.drain()
    ag.drain()


def forward_call(lengths, x, gain, cosine, sine, dyb, own, heads, pairs):
    wide = lax.axis_size("wide")
    size, width = x.shape
    span = 4 * size
    block = width // wide
    ff = own[2].shape[1]
    qkv_width = own[0].shape[1]
    out_width = own[1].shape[1]
    lanes = gain.shape[1]
    shape = jax.ShapeDtypeStruct
    anywhere = pl.BlockSpec(memory_space=pl.ANY)
    vmem = pl.BlockSpec(memory_space=pltpu.VMEM)
    count = len(chunks_of([w.shape[1] for w in own]))
    depth = wide // 2
    outs = [shape((width, w.shape[1]), bf16) for w in own] + [
        shape((span, width), bf16),
        shape((span, width), bf16),
        shape((span, qkv_width), f32),
        shape((span, out_width), bf16),
        shape((size, width), f32),
        shape((span, width), bf16),
        shape((span, ff), f32),
        shape((span, ff), f32),
        shape((span, ff), bf16),
        shape((8, width), f32),
        shape((8, HD), f32),
    ]
    return pl.pallas_call(
        functools.partial(forward_kernel, wide, heads, pairs),
        out_shape=outs,
        in_specs=[pl.BlockSpec(memory_space=pltpu.SMEM)] + [vmem] * 4 + [anywhere] * 6,
        out_specs=[anywhere] * 14 + [vmem] * 2,
        scratch_shapes=[
            pltpu.VMEM((wide, 8, lanes), f32),
            pltpu.VMEM((span, width), bf16),
            pltpu.VMEM((span, qkv_width), f32),
            pltpu.VMEM((span, out_width), bf16),
            pltpu.VMEM((size, width), f32),
            pltpu.VMEM((span, width), bf16),
            pltpu.VMEM((span, ff), f32),
            pltpu.VMEM((span, ff), f32),
            pltpu.VMEM((span, ff), bf16),
            pltpu.VMEM((width, max(qkv_width + out_width, ff)), bf16),
            pltpu.VMEM((span, HD), bf16),
            pltpu.VMEM((span, HD), bf16),
            pltpu.VMEM((2 * size, width), bf16),
            pltpu.VMEM((2 * size, width), bf16),
            pltpu.VMEM((size, width), bf16),
            pltpu.VMEM((size, width), bf16),
            pltpu.SemaphoreType.DMA((count, 2 * depth)),
            pltpu.SemaphoreType.DMA((count, depth)),
            pltpu.SemaphoreType.DMA((count, depth)),
            pltpu.SemaphoreType.DMA((count, depth)),
            pltpu.SemaphoreType.DMA((16,)),
            pltpu.SemaphoreType.DMA((16,)),
            pltpu.SemaphoreType.DMA((wide,)),
            pltpu.SemaphoreType.DMA((wide,)),
            pltpu.SemaphoreType.DMA((24,)),
        ],
        compiler_params=pltpu.CompilerParams(
            collective_id=0, has_side_effects=True, vmem_limit_bytes=62 * MIB
        ),
    )(lengths, x, gain, cosine, sine, dyb, *own)


def owners(wide):
    depth = wide // 2
    w = lax.axis_index("wide")
    z, x = w // 2, w % 2
    return [
        ((z + k) % depth) * 2 + (x if dx == 0 else 1 - x) for dx in (0, 1) for k in range(depth)
    ]


def places(wide):
    depth = wide // 2
    w = lax.axis_index("wide")
    z, x = w // 2, w % 2
    return [
        jnp.where(x == o % 2, 0, depth) + (o // 2 - z) % depth for o in range(wide)
    ]


def reorder(values, order):
    block = values.shape[-1] // len(order)
    return jnp.concatenate(
        [lax.dynamic_slice_in_dim(values, at * block, block, axis=-1) for at in order], axis=-1
    )


def along_z(values, k):
    wide = lax.axis_size("wide")
    depth = wide // 2
    return lax.ppermute(
        values, "wide", [(w, ((w // 2 + k) % depth) * 2 + w % 2) for w in range(wide)]
    )


def along_x(values):
    return lax.ppermute(values, "wide", [(w, w ^ 1) for w in range(lax.axis_size("wide"))])


def side(values, flip):
    return lax.ppermute(values, "narrow", [(n, n ^ flip) for n in range(4)])


def scatter_wide(left, right):
    wide = lax.axis_size("wide")
    depth = wide // 2
    half = left.shape[1] // 2
    block = left.shape[1] // wide
    away = dot_tn(left[:, half:], right).astype(bf16)
    got = along_x(away)
    home = (dot_tn(left[:, :half], right) + got.astype(f32)).astype(bf16)
    total = home[:block].astype(f32)
    for k in range(1, depth):
        total = total + along_z(home[k * block : (k + 1) * block], k).astype(f32)
    return total


def scatter_side(values):
    half = values.shape[0] // 2
    size = half // 2
    kept = values[:half] + side(values[half:].astype(bf16), 1).astype(f32)
    return kept[:size] + side(kept[size:].astype(bf16), 2).astype(f32)


def gather_side(values):
    other = side(values, 2)
    return jnp.concatenate([values, other, side(values, 1), side(other, 1)], axis=0)


def per_device(
    layer_input,
    out_grad,
    lengths,
    query_weight,
    query_mean,
    query_square,
    keyval_weight,
    keyval_mean,
    keyval_square,
    output_weight,
    output_mean,
    output_square,
    gateup_weight,
    gateup_mean,
    gateup_square,
    down_weight,
    down_mean,
    down_square,
    norm_gains,
    norm_mean,
    norm_square,
    head_gains,
    head_mean,
    head_square,
):
    wide = lax.axis_size("wide")
    depth = wide // 2
    w = lax.axis_index("wide")
    n = lax.axis_index("narrow")
    _, size, width = layer_input.shape
    block = width // wide
    span = 4 * size
    heads = query_weight.shape[1] // HD
    pairs = keyval_weight.shape[2] // HD
    groups = heads // pairs
    owner, place = owners(wide), places(wide)
    x = reorder(layer_input[0], owner)
    positions = n * size + jnp.arange(size)
    valid = positions < lengths[0]
    dyb = reorder(jnp.where(valid[:, None], out_grad[0], 0).astype(bf16), owner)
    own = [
        jnp.concatenate([query_weight, keyval_weight[0], keyval_weight[1]], axis=1).astype(bf16),
        output_weight.astype(bf16).T,
        gateup_weight[0].astype(bf16),
        gateup_weight[1].astype(bf16),
        down_weight.astype(bf16).T,
    ]
    lanes = max(HD, block)
    part = HD // wide
    gain = jnp.zeros((8, lanes), f32)
    gain = gain.at[0:2, 0:block].set(norm_gains.astype(bf16).astype(f32))
    gain = lax.dynamic_update_slice(gain, head_gains.astype(bf16).astype(f32), (2, w * part))
    cosine, sine = rope_tables(span)
    (
        full_qkv,
        full_out,
        full_gate,
        full_up,
        full_down,
        row_gradients,
        normed,
        qkv,
        context,
        resid,
        mixed,
        gate,
        up,
        hidden,
        gains,
        head_gain,
    ) = forward_call(lengths, x, gain, cosine, sine, dyb, own, heads, pairs)
    inputs = x.astype(f32)
    scale_first = row_scale(inputs)
    unit_first = inputs * scale_first
    scale_second = row_scale(resid)
    unit_second = resid * scale_second
    result = resid + scatter_side(dot_nt(hidden, full_down))
    layer_out = reorder(result.astype(bf16), place)[None]
    sigma = jax.nn.sigmoid(gate)
    hidden_grad = dot_nn(row_gradients, full_down)
    gate_grad = (hidden_grad * up * sigma * (1.0 + gate * (1.0 - sigma))).astype(bf16)
    up_grad = (hidden_grad * gate * sigma).astype(bf16)
    down_total = scatter_wide(row_gradients, hidden)
    gate_total = scatter_wide(mixed, gate_grad)
    up_total = scatter_wide(mixed, up_grad)
    grad_mixed = scatter_side(dot_nt(gate_grad, full_gate) + dot_nt(up_grad, full_up))
    norm_second_grad = jnp.sum(grad_mixed * unit_second, axis=0)
    grad_resid = dyb.astype(f32) + norm_back(grad_mixed, unit_second, scale_second, gains[1:2])
    residual_rows = gather_side(grad_resid.astype(bf16))
    output_total = scatter_wide(residual_rows, context)
    grad_context = dot_nn(residual_rows, full_out).astype(bf16)
    position_rows = jnp.concatenate(
        [(n ^ flip) * size + jnp.arange(size) for flip in (0, 2, 1, 3)]
    )
    cos_rows = jnp.take(cosine, position_rows, axis=0)[:, None]
    sin_rows = jnp.take(sine, position_rows, axis=0)[:, None]

    def turned(v):
        return jnp.roll(v, HD // 2, axis=-1)

    query_raw = qkv[:, : heads * HD].reshape(span, heads, HD)
    key_raw = qkv[:, heads * HD : (heads + pairs) * HD].reshape(span, pairs, HD)
    values = qkv[:, (heads + pairs) * HD :].reshape(span, pairs, HD).astype(bf16)
    query_scale = row_scale(query_raw)
    key_scale = row_scale(key_raw)
    query_unit = query_raw * query_scale
    key_unit = key_raw * key_scale
    gq, gk = head_gain[2], head_gain[3]
    queries = (query_unit * gq * cos_rows + turned(query_unit * gq) * sin_rows).astype(bf16)
    keys = (key_unit * gk * cos_rows + turned(key_unit * gk) * sin_rows).astype(bf16)
    queries = queries.reshape(span, pairs, groups, HD)
    scores = jnp.einsum("qkgd,tkd->kgqt", queries, keys, preferred_element_type=f32) * HD ** (-0.5)
    allowed = (position_rows[None, :] <= position_rows[:, None]) & (
        position_rows[None, :] < lengths[0]
    )
    scores = jnp.where(allowed[None, None], scores, masked_fill)
    probs = jax.nn.softmax(scores, axis=-1)
    gctx = grad_context.reshape(span, pairs, groups, HD)
    grad_probs = jnp.einsum("qkgd,tkd->kgqt", gctx, values, preferred_element_type=f32)
    grad_values = jnp.einsum(
        "kgqt,qkgd->tkd", probs.astype(bf16), gctx, preferred_element_type=f32
    )
    delta = jnp.sum(probs * grad_probs, axis=-1, keepdims=True)
    grad_scores = (probs * (grad_probs - delta)).astype(bf16)
    grad_queries = jnp.einsum(
        "kgqt,tkd->qkgd", grad_scores, keys, preferred_element_type=f32
    ).reshape(span, heads, HD) * HD ** (-0.5)
    grad_keys = jnp.einsum(
        "kgqt,qkgd->tkd", grad_scores, queries, preferred_element_type=f32
    ) * HD ** (-0.5)
    grad_qnorm = grad_queries * cos_rows - turned(grad_queries) * sin_rows
    grad_knorm = grad_keys * cos_rows - turned(grad_keys) * sin_rows
    head_grad = jnp.stack(
        [
            jnp.sum(grad_qnorm * query_unit, axis=(0, 1)),
            jnp.sum(grad_knorm * key_unit, axis=(0, 1)),
        ]
    )
    qkv_grad = jnp.concatenate(
        [
            norm_back(grad_qnorm, query_unit, query_scale, gq).reshape(span, heads * HD),
            norm_back(grad_knorm, key_unit, key_scale, gk).reshape(span, pairs * HD),
            grad_values.reshape(span, pairs * HD),
        ],
        axis=1,
    ).astype(bf16)
    qkv_total = scatter_wide(normed, qkv_grad)
    grad_normed = scatter_side(dot_nt(qkv_grad, full_qkv))
    norm_first_grad = jnp.sum(grad_normed * unit_first, axis=0)
    input_grad = grad_resid + norm_back(grad_normed, unit_first, scale_first, gains[0:1])
    input_grad = reorder(input_grad, place)[None]
    norm_grads = reorder(jnp.stack([norm_first_grad, norm_second_grad]), place)
    norm_grads, head_grad = lax.psum((norm_grads, head_grad), ("wide", "narrow"))
    norm_total = lax.dynamic_slice_in_dim(norm_grads, w * block, block, axis=1)
    head_total = lax.dynamic_slice_in_dim(head_grad, w * part, part, axis=1)
    split = heads * HD
    key_split = split + pairs * HD
    query = adamw(query_weight, query_mean, query_square, qkv_total[:, :split], 0.04)
    keyval = adamw(
        keyval_weight,
        keyval_mean,
        keyval_square,
        jnp.stack([qkv_total[:, split:key_split], qkv_total[:, key_split:]]),
        0.04,
    )
    output = adamw(output_weight, output_mean, output_square, output_total.T, 0.3)
    gateup = adamw(
        gateup_weight, gateup_mean, gateup_square, jnp.stack([gate_total, up_total]), 0.04
    )
    down = adamw(down_weight, down_mean, down_square, down_total.T, 0.025)
    norm = adamw(norm_gains, norm_mean, norm_square, norm_total, 0.4)
    head = adamw(head_gains, head_mean, head_square, head_total, 0.4)
    return (layer_out, input_grad, *query, *keyval, *output, *gateup, *down, *norm, *head)


def solution(mesh):
    tokens = P("wide", "narrow", None)
    down = [P("wide", "narrow")] * 3
    pair = [P(None, "wide", "narrow")] * 3
    across = [P("narrow", "wide")] * 3
    gain = [P(None, "wide")] * 3
    weights = down + pair + across + pair + across + gain + gain
    return jax.shard_map(
        per_device,
        mesh=mesh,
        in_specs=(tokens, tokens, P("wide"), *weights),
        out_specs=(tokens, tokens, *weights),
        check_vma=False,
    )
```

```python
import functools

import jax
import jax.numpy as jnp
from jax import lax
from jax.experimental import pallas as pl
from jax.experimental.pallas import tpu as pltpu
from jax.sharding import PartitionSpec as P

HD = 128
STEP = 5
MESH = pl.DeviceIdType.MESH
MIB = 2**20

norm_eps = 1e-06
rope_base = 1000000.0
beta_first = 0.5
beta_second = 0.5
adam_eps = 1e-08
weight_decay = 0.1
masked_fill = -1e30
f32 = jnp.float32
bf16 = jnp.bfloat16


def row_scale(values):
    return lax.rsqrt(jnp.mean(values * values, axis=-1, keepdims=True) + norm_eps)


def norm_back(grad, unit, scale, gain):
    scaled = grad * gain
    return scale * (scaled - unit * jnp.mean(scaled * unit, axis=-1, keepdims=True))


def adamw(weight, first, second, grad, rate):
    first_new = beta_first * first + (1.0 - beta_first) * grad
    second_new = beta_second * second + (1.0 - beta_second) * grad * grad
    first_hat = first_new / (1.0 - beta_first**STEP)
    second_hat = second_new / (1.0 - beta_second**STEP)
    weight_new = weight - rate * (
        first_hat / (jnp.sqrt(second_hat) + adam_eps) + weight_decay * weight
    )
    return (weight_new, first_new, second_new)


def rope_tables(length):
    half = HD // 2
    freqs = rope_base ** (-(jnp.arange(half, dtype=f32) * 2.0) / HD)
    angles = jnp.arange(length, dtype=f32)[:, None] * freqs[None, :]
    cosine = jnp.cos(angles)
    sine = jnp.sin(angles)
    return (
        jnp.concatenate([cosine, cosine], axis=-1),
        jnp.concatenate([-sine, sine], axis=-1),
    )


def dot_nn(left, right):
    return lax.dot_general(left, right, (((1,), (0,)), ((), ())), preferred_element_type=f32)


def dot_nt(left, right):
    return lax.dot_general(left, right, (((1,), (1,)), ((), ())), preferred_element_type=f32)


def dot_tn(left, right):
    return lax.dot_general(left, right, (((0,), (0,)), ((), ())), preferred_element_type=f32)


def loop(count, step):
    def body(index, carry):
        step(index)
        return carry

    lax.fori_loop(0, count, body, 0)


def rows(index, size):
    return pl.ds(pl.multiple_of(index * size, size), size)


class Place:
    def __init__(self, wide, narrow):
        self.depth = wide // 2
        w = lax.axis_index("wide")
        n = lax.axis_index("narrow")
        self.w, self.n = w, n
        self.z = w // 2
        self.x = w - 2 * self.z
        self.y = n // 2
        self.c = n - 2 * self.y
        self.known = {(k, dx): self.reach(k, dx) for k in range(self.depth) for dx in (0, 1)}
        self.sides = {}
        for dy in (0, 1):
            for dc in (0, 1):
                y = self.y if dy == 0 else 1 - self.y
                c = self.c if dc == 0 else 1 - self.c
                self.sides[dy, dc] = (w, y * 2 + c)

    def reach(self, k, dx):
        x = self.x if dx == 0 else 1 - self.x
        return (lax.rem(self.z + k, self.depth) * 2 + x, self.n)

    def far(self, k, dx):
        return self.known[k, dx] if isinstance(k, int) else self.reach(k, dx)

    def side(self, dy, dc):
        return self.sides[dy, dc]

    def slot(self, block):
        ay, ac = block // 2, block % 2
        dy = lax.rem(self.y + ay, 2)
        dc = lax.rem(self.c + ac, 2)
        return dc * 2 + dy


def remote(src, dst, send, recv, device):
    return pltpu.make_async_remote_copy(
        src_ref=src,
        dst_ref=dst,
        send_sem=send,
        recv_sem=recv,
        device_id=device,
        device_id_type=MESH,
    )


class Side:
    def __init__(self, place, send, recv):
        self.place = place
        self.send = [send.at[i] for i in range(send.shape[0])]
        self.recv = [recv.at[i] for i in range(recv.shape[0])]
        self.used = 0
        self.sent = []

    def copy(self, src, dst, dy, dc):
        i = self.used
        self.used += 1
        made = remote(src, dst, self.send[i], self.recv[i], self.place.side(dy, dc))
        made.start()
        self.sent.append(made)
        return made

    def drain(self):
        for made in self.sent:
            made.wait_send()
        self.sent = []


class Gather:
    def __init__(self, side, own, buf, size):
        self.side, self.buf, self.size = side, buf, size
        self.across = side.copy(own, buf.at[pl.ds(size, size)], 1, 0)
        self.core = side.copy(own, buf.at[pl.ds(2 * size, size)], 0, 1)

    def forward(self):
        size = self.size
        self.across.wait_recv()
        self.last = self.side.copy(
            self.buf.at[pl.ds(size, size)], self.buf.at[pl.ds(3 * size, size)], 0, 1
        )

    def done(self):
        self.core.wait_recv()
        self.last.wait_recv()


class Wide:
    def __init__(self, place, block, chunks, own, full, zs, zr, xs, xr):
        self.place, self.block, self.chunks, self.own, self.full = place, block, chunks, own, full
        self.zs, self.zr, self.xs, self.xr = zs, zr, xs, xr
        self.near = place.depth == 4

    def slot(self, i, index):
        g, a, b = self.chunks[i]
        return self.full[g].at[pl.ds(index * self.block, self.block), pl.ds(a, b - a)]

    def mine(self, i):
        g, a, b = self.chunks[i]
        return self.own[g].at[:, pl.ds(a, b - a)]

    def along(self, i, k):
        depth = self.place.depth
        return remote(
            self.mine(i),
            self.slot(i, k),
            self.zs.at[i, k],
            self.zr.at[i, k],
            self.place.far(depth - k, 0),
        )

    def beyond(self, i, k):
        depth = self.place.depth
        return remote(
            self.slot(i, 2),
            self.slot(i, k),
            self.zs.at[i, depth + k],
            self.zr.at[i, k],
            self.place.far(1 if k == 1 else depth - 1, 0),
        )

    def across(self, i, k):
        depth = self.place.depth
        src = self.mine(i) if k == 0 else self.slot(i, k)
        return remote(
            src, self.slot(i, depth + k), self.xs.at[i, k], self.xr.at[i, k], self.place.far(0, 1)
        )

    def each(self, i, k, act):
        place = self.place
        if self.near and k in (1, 3):
            at_end = (place.z == 0) if k == 1 else (place.z == 3)

            @pl.when(jnp.logical_not(at_end))
            def _():
                act(self.along(i, k))
        else:
            act(self.along(i, k))

    def order(self):
        depth = self.place.depth
        return (2, 1, 3) if self.near else tuple(range(1, depth))

    def issue(self, i):
        if i >= len(self.chunks):
            return
        self.across(i, 0).start()
        for k in self.order():
            self.each(i, k, lambda made: made.start())

    def hand_on(self, i):
        z = self.place.z
        for k in self.order():
            self.along(i, k).wait_recv()
            if self.near and k == 2:

                @pl.when(z == 2)
                def _():
                    self.beyond(i, 1).start()

                @pl.when(z == 1)
                def _():
                    self.beyond(i, 3).start()

            self.across(i, k).start()

    def arrived(self, i):
        for k in range(self.place.depth):
            self.across(i, k).wait_recv()

    def drain(self):
        z = self.place.z
        for i in range(len(self.chunks)):
            for k in range(self.place.depth):
                if k:
                    self.each(i, k, lambda made: made.wait_send())
                if self.near and k in (1, 3):

                    @pl.when(z == (2 if k == 1 else 1))
                    def _():
                        self.beyond(i, k).wait_send()

                self.across(i, k).wait_send()


def greet(place):
    depth = place.depth
    peers = [place.far(k, dx) for dx in (0, 1) for k in range(depth) if k or dx]
    peers += [place.side(1, 0), place.side(0, 1)]
    barrier = pltpu.get_barrier_semaphore()
    for peer in peers:
        pl.semaphore_signal(barrier, inc=1, device_id=peer, device_id_type=MESH)
    pl.semaphore_wait(barrier, len(peers))


def turn(values):
    return pltpu.roll(values, HD // 2, 1)


def rope(values, cosine, sine):
    return values * cosine + turn(values) * sine


def rope_back(grads, cosine, sine):
    return grads * cosine - turn(grads) * sine


def softmax_block(query, keys, block, size, count, length):
    scores = dot_nt(query, keys) * HD ** (-0.5)
    shape = scores.shape
    at = block * size + lax.broadcasted_iota(jnp.int32, shape, 0)
    to = lax.broadcasted_iota(jnp.int32, shape, 1)
    scores = jnp.where((to <= at) & (to < length), scores, masked_fill)
    lifted = jnp.exp(scores - jnp.max(scores, axis=-1, keepdims=True))
    return lifted / jnp.sum(lifted, axis=-1, keepdims=True)


def chunks_of(widths):
    qkv, out, gate, up, down = widths
    return [
        (0, 0, qkv // 2),
        (0, qkv // 2, qkv),
        (1, 0, out),
        (2, 0, gate // 2),
        (3, 0, up // 2),
        (2, gate // 2, gate),
        (3, up // 2, up),
        (4, 0, down // 2),
        (4, down // 2, down),
    ]


def layer_kernel(
    wide,
    heads,
    pairs,
    length_ref,
    x_ref,
    gain_ref,
    cos_ref,
    sin_ref,
    dyb_ref,
    own_qkv,
    own_out,
    own_gate,
    own_up,
    own_down,
    o_out,
    o_grad,
    o_norm,
    o_head,
    home_qkv,
    home_out,
    home_gate,
    home_up,
    home_down,
    come_qkv,
    come_out,
    come_gate,
    come_up,
    come_down,
    full_qkv,
    full_out,
    full_gate,
    full_up,
    full_down,
    away_qkv,
    away_out,
    away_gate,
    away_up,
    away_down,
    got_qkv,
    got_out,
    got_gate,
    got_up,
    got_down,
    all_dyb,
    all_normed,
    all_qkv,
    all_dresb,
    slots,
    gains,
    head_gain,
    ctx,
    resid,
    total,
    mixed,
    hidden,
    weights,
    tokens,
    feed_grad,
    stage,
    arrived_tile,
    half_out,
    half_in,
    cross_out,
    cross_in,
    sums,
    sums_in,
    head_sums,
    head_sums_in,
    last_norm,
    last_head,
    zs,
    zr,
    xs,
    xr,
    ns,
    nr,
    gs,
    gr,
    ls,
    rxs,
    rxr,
    rzs,
    rzr,
    stage_sem,
    tile_sem,
    free_core,
    free_other,
):
    place = Place(wide, 4)
    depth = place.depth
    size, width = x_ref.shape
    block = width // wide
    ff = hidden.shape[1]
    groups = heads // pairs
    span = 4 * size
    own = [own_qkv, own_out, own_gate, own_up, own_down]
    full = [full_qkv, full_out, full_gate, full_up, full_down]
    away = [away_qkv, away_out, away_gate, away_up, away_down]
    got = [got_qkv, got_out, got_gate, got_up, got_down]
    home = [home_qkv, home_out, home_gate, home_up, home_down]
    come = [come_qkv, come_out, come_gate, come_up, come_down]
    qkv_width = full_qkv.shape[1]
    out_width = full_out.shape[1]
    chunks = chunks_of([ref.shape[1] for ref in full])
    greet(place)
    ag = Wide(place, block, chunks, own, full, zs, zr, xs, xr)
    side = Side(place, ns, nr)
    copies = []
    quarter = size // 4

    def keep(src, dst):
        made = pltpu.make_async_copy(src, dst, ls.at[len(copies)])
        made.start()
        copies.append(made)
        return made

    def fetch(*pairs_of):
        made = [keep(src, dst) for src, dst in pairs_of]
        for one in made:
            one.wait()

    gain_copies = []
    for dx in (0, 1):
        for k in range(depth):
            if k or dx:
                at = dx * depth + (depth - k) % depth
                made = remote(gain_ref, slots.at[at], gs.at[at], gr.at[at], place.far(k, dx))
                made.start()
                gain_copies.append(made)
    for i in range(3):
        ag.issue(i)
    own_copies = [keep(own[g], full[g].at[pl.ds(0, block)]) for g in range(5)]
    dyb_copy = keep(dyb_ref, all_dyb.at[pl.ds(0, size)])
    slots[0] = gain_ref[...]
    for made in gain_copies:
        made.wait_recv()
    gains[...] = jnp.concatenate([slots[b][:, :block] for b in range(wide)], axis=1)
    heads_row = slots[0][:, :HD]
    for b in range(1, wide):
        heads_row = heads_row + slots[b][:, :HD]
    head_gain[...] = heads_row

    def first_norm(i):
        at = rows(i, quarter)
        x = x_ref[at, :].astype(f32)
        cross_out[at, :] = (x * row_scale(x) * gains[0:1, :]).astype(bf16)

    loop(4, first_norm)
    take_normed = Gather(side, cross_out, all_normed, size)
    normed_copy = keep(cross_out, all_normed.at[pl.ds(0, size)])
    take_dyb = Gather(side, dyb_ref, all_dyb, size)
    take_normed.forward()
    ag.hand_on(0)
    ag.issue(3)
    take_dyb.forward()
    take_normed.done()
    normed_copy.wait()
    ag.hand_on(1)
    ag.issue(4)
    ag.arrived(0)
    ag.arrived(1)
    own_copies[0].wait()
    length = length_ref[0]

    def keys_of(p, qkv, k_act, v_act):
        for a in range(4):
            at = rows(place.slot(a), size)
            to = pl.ds(a * size, size)
            raw = qkv[at, pl.ds(pl.multiple_of((heads + p) * HD, HD), HD)]
            unit = raw * row_scale(raw) * head_gain[3:4, :]
            k_act[to, :] = rope(unit, cos_ref[to, :], sin_ref[to, :]).astype(bf16)
            v_act[to, :] = qkv[
                at, pl.ds(pl.multiple_of((heads + pairs + p) * HD, HD), HD)
            ].astype(bf16)

    def attention(normed, qkv, k_act, v_act):
        fetch((all_normed, normed), (full_qkv, weights.at[:, pl.ds(0, qkv_width)]))

        def project(m):
            for n in range(qkv_width // 512):
                qkv[rows(m, size), pl.ds(n * 512, 512)] = dot_nn(
                    normed[rows(m, size), :], weights[:, pl.ds(n * 512, 512)]
                )

        loop(4, project)
        qkv_copy = keep(qkv, all_qkv)
        ag.hand_on(2)
        ag.issue(5)

        def pair(p):
            keys_of(p, qkv, k_act, v_act)

            def head(g):
                column = pl.ds(pl.multiple_of((p * groups + g) * HD, HD), HD)
                for a in range(4):
                    at = rows(place.slot(a), size)
                    to = pl.ds(a * size, size)
                    raw = qkv[at, column]
                    unit = raw * row_scale(raw) * head_gain[2:3, :]
                    query = rope(unit, cos_ref[to, :], sin_ref[to, :]).astype(bf16)
                    last = (a + 1) * size
                    probs = softmax_block(query, k_act[0:last, :], a, size, last, length)
                    ctx[at, column] = dot_nn(probs.astype(bf16), v_act[0:last, :]).astype(bf16)

            loop(groups, head)

        loop(pairs, pair)
        qkv_copy.wait()

    pl.run_scoped(
        attention,
        pltpu.VMEM((span, width), bf16),
        pltpu.VMEM((span, qkv_width), f32),
        pltpu.VMEM((span, HD), bf16),
        pltpu.VMEM((span, HD), bf16),
    )
    ag.hand_on(3)
    ag.issue(6)
    ag.arrived(2)
    own_copies[1].wait()
    fetch((full_out, weights.at[:, pl.ds(0, out_width)]))
    step = 512

    def scatter(tile):
        def to_core(n):
            half_out[:, rows(n, step)] = tile(2 * size, 2 * size, n).astype(bf16)

        loop(width // step, to_core)
        core = side.copy(half_out, half_in, 0, 1)

        def to_self(n):
            total[:, rows(n, step)] = tile(0, size, n)

        loop(width // step, to_self)
        core.wait_recv()

        def to_other(n):
            at = rows(n, step)
            part = tile(size, size, n) + half_in[pl.ds(size, size), at].astype(f32)
            cross_out[:, at] = part.astype(bf16)

        loop(width // step, to_other)
        other = side.copy(cross_out, cross_in, 1, 0)
        total[...] += half_in[pl.ds(0, size), :].astype(f32)
        return other

    def out_tile(start, count, n):
        return dot_nt(ctx[pl.ds(start, count), :], weights[rows(n, step), pl.ds(0, out_width)])

    side.drain()
    other = scatter(out_tile)
    other.wait_recv()

    def second_norm(i):
        at = rows(i, quarter)
        value = x_ref[at, :].astype(f32) + total[at, :] + cross_in[at, :].astype(f32)
        resid[at, :] = value
        mixed[at, :] = (value * row_scale(value) * gains[1:2, :]).astype(bf16)

    loop(4, second_norm)
    take_mixed = Gather(side, mixed.at[pl.ds(0, size)], mixed, size)
    ag.hand_on(4)
    ag.issue(7)
    take_mixed.forward()
    take_mixed.done()
    take_dyb.done()
    dyb_copy.wait()
    fetch((all_dyb, tokens))
    ag.hand_on(5)
    ag.issue(8)
    half = ff // 2
    tile = 256

    piece = max(block, HD)
    steps = depth * block // piece
    held = piece // block

    def staged(g, slot, to):
        return pltpu.make_async_copy(
            stage.at[slot, :, pl.ds(0, full[g].shape[1])], to, stage_sem.at[slot]
        )

    def part_of(ref, t):
        return ref.at[rows(t, piece)]

    def cross(g, t):
        return remote(
            part_of(away[g], t), part_of(got[g], t), rxs.at[g, t], rxr.at[g, t], place.far(0, 1)
        )

    def hand_over(g, k):
        return remote(
            home[g].at[rows(k, block)],
            come[g].at[rows(k - 1, block)],
            rzs.at[g, k],
            rzr.at[g, k],
            place.far(k, 0),
        )

    def send_away(g, left, right):
        wide_g = full[g].shape[1]

        def finish(t):
            staged(g, lax.rem(t, 2), part_of(away[g], t)).wait()
            cross(g, t).start()

        def one(t):
            made = dot_tn(left[:, rows(steps + t, piece)], right())
            stage[lax.rem(t, 2), :, pl.ds(0, wide_g)] = made.astype(bf16)

            @pl.when(t > 0)
            def _():
                finish(t - 1)

            staged(g, lax.rem(t, 2), part_of(away[g], t)).start()

        loop(steps, one)
        finish(steps - 1)

    def send_home(g, left, right):
        wide_g = full[g].shape[1]

        def finish(j):
            t = lax.rem(j + 1, steps)
            staged(g, lax.rem(j, 2), part_of(home[g], t)).wait()
            for r in range(held):
                k = t * held + r

                @pl.when(k > 0)
                def _(k=k):
                    hand_over(g, k).start()

        def one(j):
            t = lax.rem(j + 1, steps)
            cross(g, t).wait_recv()
            get = pltpu.make_async_copy(
                part_of(got[g], t), arrived_tile.at[:, pl.ds(0, wide_g)], tile_sem
            )
            get.start()
            made = dot_tn(left[:, rows(t, piece)], right())
            get.wait()
            made = made + arrived_tile[:, pl.ds(0, wide_g)].astype(f32)
            stage[lax.rem(j, 2), :, pl.ds(0, wide_g)] = made.astype(bf16)

            @pl.when(j > 0)
            def _():
                finish(j - 1)

            staged(g, lax.rem(j, 2), part_of(home[g], t)).start()

        loop(steps, one)
        finish(steps - 1)

    def feed_forward(gate, up):
        def feed(part):
            a = part * half
            fetch(
                (full_gate.at[:, pl.ds(a, half)], weights.at[:, pl.ds(0, half)]),
                (full_up.at[:, pl.ds(a, half)], weights.at[:, pl.ds(half, half)]),
            )

            def columns(n):
                def body(m):
                    at = rows(m, size)
                    left = mixed[at, :]
                    gate_part = dot_nn(left, weights[:, rows(n, tile)])
                    up_part = dot_nn(
                        left, weights[:, pl.ds(pl.multiple_of(half + n * tile, tile), tile)]
                    )
                    to = pl.ds(pl.multiple_of(a + n * tile, tile), tile)
                    gate[at, to] = gate_part
                    up[at, to] = up_part
                    hidden[at, to] = (gate_part * jax.nn.sigmoid(gate_part) * up_part).astype(bf16)

                loop(4, body)

            loop(half // tile, columns)

        own_copies[2].wait()
        own_copies[3].wait()
        ag.arrived(3)
        ag.arrived(4)
        feed(0)
        ag.hand_on(6)
        ag.arrived(5)
        ag.arrived(6)
        feed(1)
        send_away(4, tokens, lambda: hidden[...])
        ag.hand_on(7)
        ag.hand_on(8)
        ag.arrived(7)
        ag.arrived(8)
        own_copies[4].wait()
        fetch((full_down, weights))

        def columns(n):
            def body(m):
                at = rows(m, size)
                to = rows(n, tile)
                grad = dot_nn(tokens[at, :], weights[:, to])
                gate_part = gate[at, to]
                up_part = up[at, to]
                sigma = jax.nn.sigmoid(gate_part)
                feed_grad[at, to] = (
                    grad * up_part * sigma * (1.0 + gate_part * (1.0 - sigma))
                ).astype(bf16)
                feed_grad[at, pl.ds(pl.multiple_of(ff + n * tile, tile), tile)] = (
                    grad * gate_part * sigma
                ).astype(bf16)

            loop(4, body)

        loop(ff // tile, columns)

    pl.run_scoped(feed_forward, pltpu.VMEM((span, ff), f32), pltpu.VMEM((span, ff), f32))

    def mixed_grad(both):
        fetch(
            (full_gate, both.at[:, pl.ds(0, ff)]),
            (full_up, both.at[:, pl.ds(ff, ff)]),
        )

        def mixed_tile(start, count, n):
            return dot_nt(feed_grad[pl.ds(start, count), :], both[rows(n, step), :])

        side.drain()
        scattered.append(scatter(mixed_tile))

    scattered = []
    pl.run_scoped(mixed_grad, pltpu.VMEM((width, 2 * ff), bf16))
    other = scattered[0]
    send_away(2, mixed, lambda: feed_grad[:, pl.ds(0, ff)])
    other.wait_recv()
    sums[...] = jnp.zeros_like(sums)
    head_sums[...] = jnp.zeros_like(head_sums)

    def second_back(i):
        at = rows(i, quarter)
        value = resid[at, :]
        scale = row_scale(value)
        unit = value * scale
        grad = total[at, :] + cross_in[at, :].astype(f32)
        sums[1:2, :] += jnp.sum(grad * unit, axis=0, keepdims=True)
        back = norm_back(grad, unit, scale, gains[1:2, :])
        result = dyb_ref[at, :].astype(f32) + back
        o_grad[at, :] = result
        cross_out[at, :] = result.astype(bf16)

    side.drain()
    loop(4, second_back)
    take_dresb = Gather(side, cross_out, all_dresb, size)
    dresb_copy = keep(cross_out, all_dresb.at[pl.ds(0, size)])
    send_away(3, mixed, lambda: feed_grad[:, pl.ds(ff, ff)])
    take_dresb.forward()
    send_home(4, tokens, lambda: hidden[...])
    take_dresb.done()
    dresb_copy.wait()

    def down_tile(start, count, n):
        return dot_nt(hidden[pl.ds(start, count), :], weights[rows(n, step), :])

    side.drain()
    other = scatter(down_tile)
    other.wait_recv()
    o_out[...] = (resid[...] + total[...] + cross_in[...].astype(f32)).astype(bf16)
    pl.semaphore_signal(free_core, inc=1, device_id=place.side(0, 1), device_id_type=MESH)
    pl.semaphore_signal(free_other, inc=1, device_id=place.side(1, 0), device_id_type=MESH)

    def attention_back(qkv, k_act, v_act, ctx_grad, qkv_grad, k_grad, v_grad):
        fetch(
            (all_dresb, tokens),
            (all_qkv, qkv),
            (full_out, weights.at[:, pl.ds(0, out_width)]),
        )
        send_away(1, tokens, lambda: ctx[...])

        def context_grad(m):
            ctx_grad[rows(m, size), :] = dot_nn(
                tokens[rows(m, size), :], weights[:, pl.ds(0, out_width)]
            ).astype(bf16)

        loop(4, context_grad)

        def head_back(raw, grad, gain, a):
            to = pl.ds(a * size, size)
            scale = row_scale(raw)
            unit = raw * scale
            turned = rope_back(grad, cos_ref[to, :], sin_ref[to, :])
            gain_part = jnp.sum(turned * unit, axis=0, keepdims=True)
            return norm_back(turned, unit, scale, gain).astype(bf16), gain_part

        def pair(p):
            keys_of(p, qkv, k_act, v_act)
            k_grad[...] = jnp.zeros_like(k_grad)
            v_grad[...] = jnp.zeros_like(v_grad)

            def head(g):
                column = pl.ds(pl.multiple_of((p * groups + g) * HD, HD), HD)
                for a in range(4):
                    at = rows(place.slot(a), size)
                    to = pl.ds(a * size, size)
                    last = (a + 1) * size
                    raw = qkv[at, column]
                    unit = raw * row_scale(raw) * head_gain[2:3, :]
                    query = rope(unit, cos_ref[to, :], sin_ref[to, :]).astype(bf16)
                    probs = softmax_block(query, k_act[0:last, :], a, size, last, length)
                    grad = ctx_grad[at, column]
                    probs_grad = dot_nt(grad, v_act[0:last, :])
                    v_grad[0:last, :] += dot_tn(probs.astype(bf16), grad)
                    delta = jnp.sum(probs * probs_grad, axis=-1, keepdims=True)
                    scores_grad = (probs * (probs_grad - delta)).astype(bf16)
                    query_grad = dot_nn(scores_grad, k_act[0:last, :]) * HD ** (-0.5)
                    k_grad[0:last, :] += dot_tn(scores_grad, query) * HD ** (-0.5)
                    made, gain_part = head_back(raw, query_grad, head_gain[2:3, :], a)
                    qkv_grad[at, column] = made
                    head_sums[0:1, :] += gain_part

            loop(groups, head)
            for a in range(4):
                at = rows(place.slot(a), size)
                to = pl.ds(a * size, size)
                column = pl.ds(pl.multiple_of((heads + p) * HD, HD), HD)
                made, gain_part = head_back(
                    qkv[at, column], k_grad[to, :], head_gain[3:4, :], a
                )
                qkv_grad[at, column] = made
                head_sums[1:2, :] += gain_part
                column = pl.ds(pl.multiple_of((heads + pairs + p) * HD, HD), HD)
                qkv_grad[at, column] = v_grad[to, :].astype(bf16)

        loop(pairs, pair)
        send_home(1, tokens, lambda: ctx[...])
        fetch((all_normed, tokens), (full_qkv, weights.at[:, pl.ds(0, qkv_width)]))
        send_away(0, tokens, lambda: qkv_grad[...])

        def normed_tile(start, count, n):
            return dot_nt(
                qkv_grad[pl.ds(start, count), :], weights[rows(n, step), pl.ds(0, qkv_width)]
            )

        side.drain()
        pl.semaphore_wait(free_core, 1)
        pl.semaphore_wait(free_other, 1)
        other = scatter(normed_tile)
        send_home(2, mixed, lambda: feed_grad[:, pl.ds(0, ff)])
        other.wait_recv()

        def first_back(i):
            at = rows(i, quarter)
            value = x_ref[at, :].astype(f32)
            scale = row_scale(value)
            unit = value * scale
            grad = total[at, :] + cross_in[at, :].astype(f32)
            sums[0:1, :] += jnp.sum(grad * unit, axis=0, keepdims=True)
            o_grad[at, :] += norm_back(grad, unit, scale, gains[0:1, :])

        loop(4, first_back)

        for flip, (dy, dc) in enumerate(((0, 1), (1, 0))):
            norm_made = side.copy(sums, sums_in.at[flip], dy, dc)
            head_made = side.copy(head_sums, head_sums_in.at[flip], dy, dc)
            norm_made.wait_recv()
            head_made.wait_recv()
            side.drain()
            sums[...] += sums_in[flip]
            head_sums[...] += head_sums_in[flip]
        for made in gain_copies:
            made.wait_send()
        for b in range(wide):
            slots[b, :, 0:block] = sums[:, b * block : (b + 1) * block]
        last = []
        for dx in (0, 1):
            for k in range(depth):
                if k or dx:
                    to = dx * depth + k
                    at = dx * depth + (depth - k) % depth
                    made = remote(
                        slots.at[to], last_norm.at[at], gs.at[at], gr.at[at], place.far(k, dx)
                    )
                    made.start()
                    last.append(made)
                    made = remote(
                        head_sums,
                        last_head.at[at],
                        gs.at[wide + at],
                        gr.at[wide + at],
                        place.far(k, dx),
                    )
                    made.start()
                    last.append(made)
        send_home(3, mixed, lambda: feed_grad[:, pl.ds(ff, ff)])
        send_home(0, tokens, lambda: qkv_grad[...])
        for made in last:
            made.wait_recv()
        norm_total = slots[0]
        head_total = head_sums[...]
        for b in range(1, wide):
            norm_total = norm_total + last_norm[b]
            head_total = head_total + last_head[b]
        o_norm[...] = norm_total
        o_head[...] = head_total
        for made in last:
            made.wait_send()

    pl.run_scoped(
        attention_back,
        pltpu.VMEM((span, qkv_width), f32),
        pltpu.VMEM((span, HD), bf16),
        pltpu.VMEM((span, HD), bf16),
        pltpu.VMEM((span, out_width), bf16),
        pltpu.VMEM((span, qkv_width), bf16),
        pltpu.VMEM((span, HD), f32),
        pltpu.VMEM((span, HD), f32),
    )
    for g in range(5):
        for t in range(steps):
            cross(g, t).wait_send()
        for k in range(1, depth):
            hand_over(g, k).wait()
    side.drain()
    ag.drain()


def layer_call(lengths, x, gain, cosine, sine, dyb, own, heads, pairs):
    wide = lax.axis_size("wide")
    depth = wide // 2
    size, width = x.shape
    span = 4 * size
    block = width // wide
    ff = own[2].shape[1]
    widths = [w.shape[1] for w in own]
    lanes = gain.shape[1]
    shape = jax.ShapeDtypeStruct
    anywhere = pl.BlockSpec(memory_space=pl.ANY)
    vmem = pl.BlockSpec(memory_space=pltpu.VMEM)
    count = len(chunks_of(widths))
    outs = [
        shape((size, width), bf16),
        shape((size, width), f32),
        shape((8, lanes), f32),
        shape((8, HD), f32),
    ]
    outs += [shape((width // 2, w), bf16) for w in widths]
    outs += [shape(((depth - 1) * block, w), bf16) for w in widths]
    outs += [shape((width, w), bf16) for w in widths]
    outs += [shape((width // 2, w), bf16) for w in widths] * 2
    outs += [
        shape((span, width), bf16),
        shape((span, width), bf16),
        shape((span, widths[0]), f32),
        shape((span, width), bf16),
    ]
    dma = pltpu.SemaphoreType.DMA
    return pl.pallas_call(
        functools.partial(layer_kernel, wide, heads, pairs),
        out_shape=outs,
        in_specs=[pl.BlockSpec(memory_space=pltpu.SMEM)] + [vmem] * 5 + [anywhere] * 5,
        out_specs=[vmem] * 4 + [anywhere] * (len(outs) - 4),
        scratch_shapes=[
            pltpu.VMEM((wide, 8, lanes), f32),
            pltpu.VMEM((8, width), f32),
            pltpu.VMEM((8, HD), f32),
            pltpu.VMEM((span, widths[1]), bf16),
            pltpu.VMEM((size, width), f32),
            pltpu.VMEM((size, width), f32),
            pltpu.VMEM((span, width), bf16),
            pltpu.VMEM((span, ff), bf16),
            pltpu.VMEM((width, ff), bf16),
            pltpu.VMEM((span, width), bf16),
            pltpu.VMEM((span, 2 * ff), bf16),
            pltpu.VMEM((2, max(block, HD), max(widths)), bf16),
            pltpu.VMEM((max(block, HD), max(widths)), bf16),
            pltpu.VMEM((2 * size, width), bf16),
            pltpu.VMEM((2 * size, width), bf16),
            pltpu.VMEM((size, width), bf16),
            pltpu.VMEM((size, width), bf16),
            pltpu.VMEM((8, width), f32),
            pltpu.VMEM((2, 8, width), f32),
            pltpu.VMEM((8, HD), f32),
            pltpu.VMEM((2, 8, HD), f32),
            pltpu.VMEM((wide, 8, lanes), f32),
            pltpu.VMEM((wide, 8, HD), f32),
            dma((count, 2 * depth)),
            dma((count, depth)),
            dma((count, depth)),
            dma((count, depth)),
            dma((40,)),
            dma((40,)),
            dma((2 * wide,)),
            dma((2 * wide,)),
            dma((40,)),
            dma((5, depth)),
            dma((5, depth)),
            dma((5, depth)),
            dma((5, depth)),
            dma((2,)),
            dma,
            pltpu.SemaphoreType.REGULAR,
            pltpu.SemaphoreType.REGULAR,
        ],
        compiler_params=pltpu.CompilerParams(
            collective_id=0, has_side_effects=True, vmem_limit_bytes=63 * MIB
        ),
    )(lengths, x, gain, cosine, sine, dyb, *own)


def owners(wide):
    depth = wide // 2
    w = lax.axis_index("wide")
    z, x = w // 2, w % 2
    return [
        ((z + k) % depth) * 2 + (x if dx == 0 else 1 - x) for dx in (0, 1) for k in range(depth)
    ]


def places(wide):
    depth = wide // 2
    w = lax.axis_index("wide")
    z, x = w // 2, w % 2
    return [
        jnp.where(x == o % 2, 0, depth) + (o // 2 - z) % depth for o in range(wide)
    ]


def reorder(values, order):
    block = values.shape[-1] // len(order)
    return jnp.concatenate(
        [lax.dynamic_slice_in_dim(values, at * block, block, axis=-1) for at in order], axis=-1
    )


def per_device(
    layer_input,
    out_grad,
    lengths,
    query_weight,
    query_mean,
    query_square,
    keyval_weight,
    keyval_mean,
    keyval_square,
    output_weight,
    output_mean,
    output_square,
    gateup_weight,
    gateup_mean,
    gateup_square,
    down_weight,
    down_mean,
    down_square,
    norm_gains,
    norm_mean,
    norm_square,
    head_gains,
    head_mean,
    head_square,
):
    wide = lax.axis_size("wide")
    depth = wide // 2
    w = lax.axis_index("wide")
    n = lax.axis_index("narrow")
    _, size, width = layer_input.shape
    block = width // wide
    span = 4 * size
    heads = query_weight.shape[1] // HD
    pairs = keyval_weight.shape[2] // HD
    groups = heads // pairs
    owner, place = owners(wide), places(wide)
    x = reorder(layer_input[0], owner)
    positions = n * size + jnp.arange(size)
    valid = positions < lengths[0]
    dyb = reorder(jnp.where(valid[:, None], out_grad[0], 0).astype(bf16), owner)
    own = [
        jnp.concatenate([query_weight, keyval_weight[0], keyval_weight[1]], axis=1).astype(bf16),
        output_weight.astype(bf16).T,
        gateup_weight[0].astype(bf16),
        gateup_weight[1].astype(bf16),
        down_weight.astype(bf16).T,
    ]
    lanes = max(HD, block)
    part = HD // wide
    gain = jnp.zeros((8, lanes), f32)
    gain = gain.at[0:2, 0:block].set(norm_gains.astype(bf16).astype(f32))
    gain = lax.dynamic_update_slice(gain, head_gains.astype(bf16).astype(f32), (2, w * part))
    cosine, sine = rope_tables(span)
    outs = layer_call(lengths, x, gain, cosine, sine, dyb, own, heads, pairs)
    layer_out = reorder(outs[0], place)[None]
    input_grad = reorder(outs[1], place)[None]
    norm_total = outs[2][0:2, 0:block]
    head_total = lax.dynamic_slice(outs[3], (0, w * part), (2, part))

    def total(g):
        result = outs[4 + g][0:block].astype(f32)
        for k in range(depth - 1):
            result = result + outs[9 + g][k * block : (k + 1) * block].astype(f32)
        return result

    qkv_total, output_total, gate_total, up_total, down_total = [total(g) for g in range(5)]
    split = heads * HD
    key_split = split + pairs * HD
    query = adamw(query_weight, query_mean, query_square, qkv_total[:, :split], 0.04)
    keyval = adamw(
        keyval_weight,
        keyval_mean,
        keyval_square,
        jnp.stack([qkv_total[:, split:key_split], qkv_total[:, key_split:]]),
        0.04,
    )
    output = adamw(output_weight, output_mean, output_square, output_total.T, 0.3)
    gateup = adamw(
        gateup_weight, gateup_mean, gateup_square, jnp.stack([gate_total, up_total]), 0.04
    )
    down = adamw(down_weight, down_mean, down_square, down_total.T, 0.025)
    norm = adamw(norm_gains, norm_mean, norm_square, norm_total, 0.4)
    head = adamw(head_gains, head_mean, head_square, head_total, 0.4)
    return (layer_out, input_grad, *query, *keyval, *output, *gateup, *down, *norm, *head)


def solution(mesh):
    tokens = P("wide", "narrow", None)
    down = [P("wide", "narrow")] * 3
    pair = [P(None, "wide", "narrow")] * 3
    across = [P("narrow", "wide")] * 3
    gain = [P(None, "wide")] * 3
    weights = down + pair + across + pair + across + gain + gain
    return jax.shard_map(
        per_device,
        mesh=mesh,
        in_specs=(tokens, tokens, P("wide"), *weights),
        out_specs=(tokens, tokens, *weights),
        check_vma=False,
    )
```

```python
import functools

import jax
import jax.numpy as jnp
import numpy as np
from jax import lax
from jax.experimental import pallas as pl
from jax.experimental.pallas import tpu as pltpu
from jax.sharding import PartitionSpec as P

HD = 128
STEP = 5
MESH = pl.DeviceIdType.MESH
MIB = 2**20

norm_eps = 1e-06
rope_base = 1000000.0
beta_first = 0.5
beta_second = 0.5
adam_eps = 1e-08
weight_decay = 0.1
masked_fill = -1e30
f32 = jnp.float32
bf16 = jnp.bfloat16


def row_scale(values):
    return lax.rsqrt(jnp.mean(values * values, axis=-1, keepdims=True) + norm_eps)


def norm_back(grad, unit, scale, gain):
    scaled = grad * gain
    return scale * (scaled - unit * jnp.mean(scaled * unit, axis=-1, keepdims=True))


def adamw(weight, first, second, grad, rate):
    first_new = beta_first * first + (1.0 - beta_first) * grad
    second_new = beta_second * second + (1.0 - beta_second) * grad * grad
    first_hat = first_new / (1.0 - beta_first**STEP)
    second_hat = second_new / (1.0 - beta_second**STEP)
    weight_new = weight - rate * (
        first_hat / (jnp.sqrt(second_hat) + adam_eps) + weight_decay * weight
    )
    return (weight_new, first_new, second_new)


def rope_tables(length):
    half = HD // 2
    freqs = rope_base ** (-(np.arange(half, dtype=np.float32) * np.float32(2.0)) / np.float32(HD))
    angles = np.arange(length, dtype=np.float32)[:, None] * freqs.astype(np.float32)[None, :]
    cosine = np.cos(angles.astype(np.float64)).astype(np.float32)
    sine = np.sin(angles.astype(np.float64)).astype(np.float32)
    return (
        jnp.asarray(np.concatenate([cosine, cosine], axis=-1)),
        jnp.asarray(np.concatenate([-sine, sine], axis=-1)),
    )


def dot_nn(left, right):
    return lax.dot_general(left, right, (((1,), (0,)), ((), ())), preferred_element_type=f32)


def dot_nt(left, right):
    return lax.dot_general(left, right, (((1,), (1,)), ((), ())), preferred_element_type=f32)


def dot_tn(left, right):
    return lax.dot_general(left, right, (((0,), (0,)), ((), ())), preferred_element_type=f32)


def loop(count, step):
    def body(index, carry):
        step(index)
        return carry

    lax.fori_loop(0, count, body, 0)


def rows(index, size):
    return pl.ds(pl.multiple_of(index * size, size), size)


class Place:
    def __init__(self, wide, narrow):
        self.depth = wide // 2
        w = lax.axis_index("wide")
        n = lax.axis_index("narrow")
        self.w, self.n = w, n
        self.z = w // 2
        self.x = w - 2 * self.z
        self.y = n // 2
        self.c = n - 2 * self.y
        self.known = {(k, dx): self.reach(k, dx) for k in range(self.depth) for dx in (0, 1)}
        self.sides = {}
        for dy in (0, 1):
            for dc in (0, 1):
                y = self.y if dy == 0 else 1 - self.y
                c = self.c if dc == 0 else 1 - self.c
                self.sides[dy, dc] = (w, y * 2 + c)

    def reach(self, k, dx):
        x = self.x if dx == 0 else 1 - self.x
        return (lax.rem(self.z + k, self.depth) * 2 + x, self.n)

    def far(self, k, dx):
        return self.known[k, dx] if isinstance(k, int) else self.reach(k, dx)

    def side(self, dy, dc):
        return self.sides[dy, dc]

    def slot(self, block):
        ay, ac = block // 2, block % 2
        dy = lax.rem(self.y + ay, 2)
        dc = lax.rem(self.c + ac, 2)
        return dc * 2 + dy


def remote(src, dst, send, recv, device):
    return pltpu.make_async_remote_copy(
        src_ref=src,
        dst_ref=dst,
        send_sem=send,
        recv_sem=recv,
        device_id=device,
        device_id_type=MESH,
    )


class Side:
    def __init__(self, place, send, recv):
        self.place = place
        self.send = [send.at[i] for i in range(send.shape[0])]
        self.recv = [recv.at[i] for i in range(recv.shape[0])]
        self.used = 0
        self.sent = []

    def copy(self, src, dst, dy, dc):
        i = self.used
        self.used += 1
        made = remote(src, dst, self.send[i], self.recv[i], self.place.side(dy, dc))
        made.start()
        self.sent.append(made)
        return made

    def drain(self):
        for made in self.sent:
            made.wait_send()
        self.sent = []


class Gather:
    def __init__(self, side, own, buf, size):
        self.side, self.buf, self.size = side, buf, size
        self.across = side.copy(own, buf.at[pl.ds(size, size)], 1, 0)
        self.core = side.copy(own, buf.at[pl.ds(2 * size, size)], 0, 1)

    def forward(self):
        size = self.size
        self.across.wait_recv()
        self.last = self.side.copy(
            self.buf.at[pl.ds(size, size)], self.buf.at[pl.ds(3 * size, size)], 0, 1
        )

    def done(self):
        self.core.wait_recv()
        self.last.wait_recv()


class Wide:
    def __init__(self, place, block, chunks, full, zs, zr, xs, xr):
        self.place, self.block, self.chunks, self.full = place, block, chunks, full
        self.zs, self.zr, self.xs, self.xr = zs, zr, xs, xr
        self.near = place.depth == 4
        self.odd = place.z - 2 * (place.z // 2)

    def shared(self, i):
        return self.near and i in (3, 5, 7)

    def beside(self, i):
        g, a, b = self.chunks[i]
        at = (self.place.depth + 3 - 2 * self.odd) * self.block
        return remote(
            self.slot(i, self.place.depth),
            self.full[g].at[pl.ds(pl.multiple_of(at, self.block), self.block), pl.ds(a, b - a)],
            self.xs.at[i, 1 + 2 * self.odd],
            self.xr.at[i, 3 - 2 * self.odd],
            self.place.far(1 + 2 * self.odd, 0),
        )

    def slot(self, i, index):
        g, a, b = self.chunks[i]
        return self.full[g].at[pl.ds(index * self.block, self.block), pl.ds(a, b - a)]

    def along(self, i, k):
        depth = self.place.depth
        return remote(
            self.slot(i, 0),
            self.slot(i, k),
            self.zs.at[i, k],
            self.zr.at[i, k],
            self.place.far(depth - k, 0),
        )

    def beyond(self, i, k):
        depth = self.place.depth
        return remote(
            self.slot(i, 2),
            self.slot(i, k),
            self.zs.at[i, depth + k],
            self.zr.at[i, k],
            self.place.far(1 if k == 1 else depth - 1, 0),
        )

    def across(self, i, k):
        depth = self.place.depth
        return remote(
            self.slot(i, k),
            self.slot(i, depth + k),
            self.xs.at[i, k],
            self.xr.at[i, k],
            self.place.far(0, 1),
        )

    def each(self, i, k, act):
        place = self.place
        if self.near and k in (1, 3):
            at_end = (place.z == 0) if k == 1 else (place.z == 3)

            @pl.when(jnp.logical_not(at_end))
            def _():
                act(self.along(i, k))
        else:
            act(self.along(i, k))

    def order(self):
        depth = self.place.depth
        return (2, 1, 3) if self.near else tuple(range(1, depth))

    def issue(self, i):
        if i >= len(self.chunks):
            return
        self.across(i, 0).start()
        for k in self.order():
            self.each(i, k, lambda made: made.start())

    def hand_on(self, i):
        z = self.place.z
        for k in self.order():
            self.along(i, k).wait_recv()
            if self.near and k == 2:

                @pl.when(z == 2)
                def _():
                    self.beyond(i, 1).start()

                @pl.when(z == 1)
                def _():
                    self.beyond(i, 3).start()

            if self.shared(i) and k in (1, 3):

                @pl.when(self.odd == (1 if k == 1 else 0))
                def _():
                    self.across(i, k).start()
            else:
                self.across(i, k).start()
        if self.shared(i):
            self.across(i, 0).wait_recv()
            self.beside(i).start()

    def arrived(self, i):
        for k in range(self.place.depth):
            if k or not self.shared(i):
                self.across(i, k).wait_recv()

    def drain(self):
        z = self.place.z
        for i in range(len(self.chunks)):
            for k in range(self.place.depth):
                if k:
                    self.each(i, k, lambda made: made.wait_send())
                if self.near and k in (1, 3):

                    @pl.when(z == (2 if k == 1 else 1))
                    def _():
                        self.beyond(i, k).wait_send()

                self.across(i, k).wait_send()


def greet(place):
    depth = place.depth
    peers = [place.far(k, dx) for dx in (0, 1) for k in range(depth) if k or dx]
    peers += [place.side(1, 0), place.side(0, 1)]
    barrier = pltpu.get_barrier_semaphore()
    for peer in peers:
        pl.semaphore_signal(barrier, inc=1, device_id=peer, device_id_type=MESH)
    pl.semaphore_wait(barrier, len(peers))


def turn(values):
    return pltpu.roll(values, HD // 2, 1)


def rope(values, cosine, sine):
    return values * cosine + turn(values) * sine


def rope_back(grads, cosine, sine):
    return grads * cosine - turn(grads) * sine


def softmax_block(query, keys, block, size, count, length):
    scores = dot_nt(query, keys) * HD ** (-0.5)
    shape = scores.shape
    at = block * size + lax.broadcasted_iota(jnp.int32, shape, 0)
    to = lax.broadcasted_iota(jnp.int32, shape, 1)
    scores = jnp.where((to <= at) & (to < length), scores, masked_fill)
    lifted = jnp.exp(scores - jnp.max(scores, axis=-1, keepdims=True))
    return lifted / jnp.sum(lifted, axis=-1, keepdims=True)


def chunks_of(widths):
    qkv, out, gate, up, down = widths
    return [
        (0, 0, qkv // 2),
        (0, qkv // 2, qkv),
        (1, 0, out),
        (2, 0, gate // 2),
        (3, 0, up // 2),
        (2, gate // 2, gate),
        (3, up // 2, up),
        (4, 0, down // 2),
        (4, down // 2, down),
    ]


def owners(wide):
    depth = wide // 2
    w = lax.axis_index("wide")
    z, x = w // 2, w % 2
    return [
        ((z + k) % depth) * 2 + (x if dx == 0 else 1 - x) for dx in (0, 1) for k in range(depth)
    ]


def places(wide):
    depth = wide // 2
    w = lax.axis_index("wide")
    z, x = w // 2, w % 2
    return [
        jnp.where(x == o % 2, 0, depth) + (o // 2 - z) % depth for o in range(wide)
    ]


def reorder(values, order):
    block = values.shape[-1] // len(order)
    return jnp.concatenate(
        [lax.dynamic_slice_in_dim(values, at * block, block, axis=-1) for at in order], axis=-1
    )


def layer_kernel(
    wide,
    heads,
    pairs,
    length_ref,
    norm_ref,
    head_ref,
    cos_ref,
    sin_ref,
    x_in,
    dy_in,
    w_query,
    w_keyval,
    w_output,
    w_gateup,
    w_down,
    o_norm,
    o_head,
    o_out,
    o_grad,
    o_query,
    o_keyval,
    o_output,
    o_gateup,
    o_down,
    home_qkv,
    home_out,
    home_gate,
    home_up,
    home_down,
    come_qkv,
    come_out,
    come_gate,
    come_up,
    come_down,
    full_qkv,
    full_out,
    full_gate,
    full_up,
    full_down,
    away_qkv,
    away_out,
    away_gate,
    away_up,
    away_down,
    got_qkv,
    got_out,
    got_gate,
    got_up,
    got_down,
    relay_qkv,
    relay_out,
    relay_gate,
    relay_up,
    relay_down,
    all_dyb,
    all_normed,
    all_qkv,
    all_dresb,
    x_ref,
    dyb_ref,
    grad_own,
    gain_ref,
    slots,
    gains,
    head_gain,
    ctx,
    resid,
    total,
    mixed,
    hidden,
    weights,
    tokens,
    feed_grad,
    stage,
    arrived_tile,
    half_out,
    half_in,
    cross_out,
    cross_in,
    sums,
    sums_in,
    head_sums,
    head_sums_in,
    last_norm,
    last_head,
    zs,
    zr,
    xs,
    xr,
    ns,
    nr,
    gs,
    gr,
    ls,
    rxs,
    rxr,
    rzs,
    rzr,
    stage_sem,
    tile_sem,
    free_core,
    free_other,
):
    place = Place(wide, 4)
    depth = place.depth
    size, width = x_ref.shape
    block = width // wide
    inside = block % HD == 0
    ff = hidden.shape[1]
    groups = heads // pairs
    span = 4 * size
    full = [full_qkv, full_out, full_gate, full_up, full_down]
    away = [away_qkv, away_out, away_gate, away_up, away_down]
    got = [got_qkv, got_out, got_gate, got_up, got_down]
    home = [home_qkv, home_out, home_gate, home_up, home_down]
    come = [come_qkv, come_out, come_gate, come_up, come_down]
    relay = [relay_qkv, relay_out, relay_gate, relay_up, relay_down]
    widths = [ref.shape[1] for ref in full]
    qkv_width, out_width = widths[0], widths[1]
    chunks = chunks_of(widths)
    ag = Wide(place, block, chunks, full, zs, zr, xs, xr)
    side = Side(place, ns, nr)
    copies = []
    quarter = size // 4

    def keep(src, dst):
        made = pltpu.make_async_copy(src, dst, ls.at[len(copies)])
        made.start()
        copies.append(made)
        return made

    def fetch(*pairs_of):
        made = [keep(src, dst) for src, dst in pairs_of]
        for one in made:
            one.wait()

    def in_order(ref, buf, out=False):
        if not inside:
            return [keep(buf, ref) if out else keep(ref, buf)]
        made = []
        for b in range(wide):
            w, _ = place.far(b % depth, b // depth)
            there = ref.at[:, pl.ds(pl.multiple_of(w * block, block), block)]
            here = buf.at[:, pl.ds(b * block, block)]
            made.append(keep(here, there) if out else keep(there, here))
        return made

    def land(g, buf):
        if not inside:
            return [keep([w_query, w_keyval, w_output, w_gateup, w_down][g], full[g].at[0:block])]
        if g == 0:
            at, made = 0, []
            for ref in (w_query, w_keyval.at[0], w_keyval.at[1]):
                made.append(keep(ref, buf.at[:, pl.ds(at, ref.shape[1])]))
                at += ref.shape[1]
            return made
        if g in (2, 3):
            return [keep(w_gateup.at[g - 2], buf.at[:, pl.ds(0, widths[g])])]
        ref = w_output if g == 1 else w_down
        return [
            keep(ref.at[pl.ds(i * block, block)], buf.at[:, pl.ds(i * block, block)])
            for i in range(widths[g] // block)
        ]

    def settle(g, buf, made):
        for one in made:
            one.wait()
        if not inside:
            return
        slot = g % 2
        if g in (1, 4):
            for i in range(widths[g] // block):
                at = pl.ds(i * block, block)
                stage[slot, :, at] = buf[:, at].T.astype(bf16)
        else:

            def cast(i):
                at = rows(i, block // 4)
                stage[slot, at, pl.ds(0, widths[g])] = buf[at, 0 : widths[g]].astype(bf16)

            loop(4, cast)
        fetch((stage.at[slot, :, pl.ds(0, widths[g])], full[g].at[pl.ds(0, block)]))

    landing = land(0, total)
    x_copies = in_order(x_in, x_ref)
    landing_out = land(1, resid)
    dy_copies = in_order(dy_in, dyb_ref)

    part = head_ref.shape[1]
    gain_ref[...] = jnp.zeros_like(gain_ref)
    gain_ref[0:2, 0:part] = head_ref[...]
    spread = pltpu.roll(gain_ref[:, 0:HD], place.w * part, 1)
    gain_ref[:, 0:HD] = pltpu.roll(spread, 2, 0)
    gain_ref[0:2, 0:block] = norm_ref[...]
    gain_ref[...] = gain_ref[...].astype(bf16).astype(f32)
    greet(place)

    gain_copies = []
    for dx in (0, 1):
        for k in range(depth):
            if k or dx:
                at = dx * depth + (depth - k) % depth
                made = remote(gain_ref, slots.at[at], gs.at[at], gr.at[at], place.far(k, dx))
                made.start()
                gain_copies.append(made)
    settle(0, total, landing)
    landing = land(2, total)
    ag.issue(0)
    ag.issue(1)
    settle(1, resid, landing_out)
    landing_up = land(3, resid)
    ag.issue(2)
    slots[0] = gain_ref[...]
    for made in gain_copies:
        made.wait_recv()
    gains[...] = jnp.concatenate([slots[b][:, :block] for b in range(wide)], axis=1)
    heads_row = slots[0][:, :HD]
    for b in range(1, wide):
        heads_row = heads_row + slots[b][:, :HD]
    head_gain[...] = heads_row
    for made in x_copies:
        made.wait()

    def first_norm(i):
        at = rows(i, quarter)
        x = x_ref[at, :].astype(f32)
        cross_out[at, :] = (x * row_scale(x) * gains[0:1, :]).astype(bf16)

    loop(4, first_norm)
    take_normed = Gather(side, cross_out, all_normed, size)
    normed_copy = keep(cross_out, all_normed.at[pl.ds(0, size)])
    length = length_ref[0]
    for made in dy_copies:
        made.wait()

    def mask(i):
        at = rows(i, quarter)
        value = dyb_ref[at, :].astype(f32)
        where = place.n * size + i * quarter + lax.broadcasted_iota(jnp.int32, value.shape, 0)
        dyb_ref[at, :] = jnp.where(where < length, value, 0.0).astype(bf16)

    loop(4, mask)
    take_dyb = Gather(side, dyb_ref, all_dyb, size)
    dyb_copy = keep(dyb_ref, all_dyb.at[pl.ds(0, size)])
    settle(2, total, landing)
    landing = land(4, total)
    ag.hand_on(0)
    settle(3, resid, landing_up)
    ag.issue(3)
    take_normed.forward()
    ag.hand_on(1)
    ag.issue(4)
    settle(4, total, landing)
    ag.hand_on(2)
    ag.issue(5)
    take_dyb.forward()
    take_normed.done()
    normed_copy.wait()
    ag.arrived(0)
    ag.arrived(1)

    def keys_of(p, qkv, k_act, v_act):
        for a in range(4):
            at = rows(place.slot(a), size)
            to = pl.ds(a * size, size)
            raw = qkv[at, pl.ds(pl.multiple_of((heads + p) * HD, HD), HD)]
            unit = raw * row_scale(raw) * head_gain[3:4, :]
            k_act[to, :] = rope(unit, cos_ref[to, :], sin_ref[to, :]).astype(bf16)
            v_act[to, :] = qkv[
                at, pl.ds(pl.multiple_of((heads + pairs + p) * HD, HD), HD)
            ].astype(bf16)

    def attention(normed, qkv, k_act, v_act):
        fetch((all_normed, normed), (full_qkv, weights.at[:, pl.ds(0, qkv_width)]))

        def project(m):
            for n in range(qkv_width // 512):
                qkv[rows(m, size), pl.ds(n * 512, 512)] = dot_nn(
                    normed[rows(m, size), :], weights[:, pl.ds(n * 512, 512)]
                )

        loop(4, project)
        qkv_copy = keep(qkv, all_qkv)

        def pair(p):
            keys_of(p, qkv, k_act, v_act)

            def head(g):
                column = pl.ds(pl.multiple_of((p * groups + g) * HD, HD), HD)
                for a in range(4):
                    at = rows(place.slot(a), size)
                    to = pl.ds(a * size, size)
                    raw = qkv[at, column]
                    unit = raw * row_scale(raw) * head_gain[2:3, :]
                    query = rope(unit, cos_ref[to, :], sin_ref[to, :]).astype(bf16)
                    last = (a + 1) * size
                    probs = softmax_block(query, k_act[0:last, :], a, size, last, length)
                    ctx[at, column] = dot_nn(probs.astype(bf16), v_act[0:last, :]).astype(bf16)

            loop(groups, head)

        loop(pairs, pair)
        qkv_copy.wait()

    pl.run_scoped(
        attention,
        pltpu.VMEM((span, width), bf16),
        pltpu.VMEM((span, qkv_width), f32),
        pltpu.VMEM((span, HD), bf16),
        pltpu.VMEM((span, HD), bf16),
    )
    ag.hand_on(3)
    ag.issue(6)
    ag.arrived(2)
    fetch((full_out, weights.at[:, pl.ds(0, out_width)]))
    step = 512

    def scatter(tile):
        def to_core(n):
            half_out[:, rows(n, step)] = tile(2 * size, 2 * size, n).astype(bf16)

        loop(width // step, to_core)
        core = side.copy(half_out, half_in, 0, 1)

        def to_self(n):
            total[:, rows(n, step)] = tile(0, size, n)

        loop(width // step, to_self)
        core.wait_recv()

        def to_other(n):
            at = rows(n, step)
            part = tile(size, size, n) + half_in[pl.ds(size, size), at].astype(f32)
            cross_out[:, at] = part.astype(bf16)

        loop(width // step, to_other)
        other = side.copy(cross_out, cross_in, 1, 0)
        total[...] += half_in[pl.ds(0, size), :].astype(f32)
        return other

    def out_tile(start, count, n):
        return dot_nt(ctx[pl.ds(start, count), :], weights[rows(n, step), pl.ds(0, out_width)])

    side.drain()
    other = scatter(out_tile)
    other.wait_recv()

    def second_norm(i):
        at = rows(i, quarter)
        value = x_ref[at, :].astype(f32) + total[at, :] + cross_in[at, :].astype(f32)
        resid[at, :] = value
        mixed[at, :] = (value * row_scale(value) * gains[1:2, :]).astype(bf16)

    loop(4, second_norm)
    take_mixed = Gather(side, mixed.at[pl.ds(0, size)], mixed, size)
    ag.hand_on(4)
    ag.issue(7)
    take_mixed.forward()
    ag.hand_on(5)
    ag.issue(8)
    take_mixed.done()
    half = ff // 2
    tile = 256

    piece = max(block, HD)
    steps = depth * block // piece
    held = piece // block

    def staged(g, slot, to):
        return pltpu.make_async_copy(
            stage.at[slot, :, pl.ds(0, full[g].shape[1])], to, stage_sem.at[slot]
        )

    def part_of(ref, t):
        return ref.at[rows(t, piece)]

    def cross(g, t):
        return remote(
            part_of(away[g], t), part_of(got[g], t), rxs.at[g, t], rxr.at[g, t], place.far(0, 1)
        )

    def hand_over(g, k):
        return remote(
            home[g].at[rows(k, block)],
            come[g].at[rows(k - 1, block)],
            rzs.at[g, k],
            rzr.at[g, k],
            place.far(k, 0),
        )

    order = (1, 3, 2, 0) if ag.near else tuple(range(1, steps)) + (0,)
    waiting = []
    turns = [0]

    def flush():
        while waiting:
            waiting.pop(0)()

    def send_away(g, left, right):
        wide_g = widths[g]
        for t in order:
            flush()
            slot = turns[0] % 2
            turns[0] += 1
            at = (steps + t) * piece
            stage[slot, :, 0:wide_g] = dot_tn(left[:, at : at + piece], right()).astype(bf16)
            staged(g, slot, part_of(away[g], t)).start()

            def finish(t=t, slot=slot):
                staged(g, slot, part_of(away[g], t)).wait()
                cross(g, t).start()

            waiting.append(finish)

    def add_to_stage(g, slot, src, made):
        wide_g = full[g].shape[1]
        made.wait_recv()
        more = pltpu.make_async_copy(src, arrived_tile.at[:, pl.ds(0, wide_g)], tile_sem)
        more.start()
        more.wait()
        stage[slot, :, 0:wide_g] = (
            stage[slot, :, 0:wide_g].astype(f32) + arrived_tile[:, 0:wide_g].astype(f32)
        ).astype(bf16)

    def relay_over(g, k):
        return remote(
            part_of(home[g], k),
            relay[g],
            rzs.at[g, k],
            rzr.at[g, 0],
            place.far(depth - 1 if k == 1 else 1, 0),
        )

    def send_home(g, left, right, which=None):
        wide_g = full[g].shape[1]
        for t in order if which is None else which:
            flush()
            slot = turns[0] % 2
            turns[0] += 1
            cross(g, t).wait_recv()
            get = pltpu.make_async_copy(
                part_of(got[g], t), arrived_tile.at[:, pl.ds(0, wide_g)], tile_sem
            )
            get.start()
            made = dot_tn(left[:, t * piece : (t + 1) * piece], right())
            get.wait()
            made = made + arrived_tile[:, 0:wide_g].astype(f32)
            stage[slot, :, 0:wide_g] = made.astype(bf16)
            if ag.near and t == 2:

                @pl.when((place.z == 1) | (place.z == 2))
                def _():
                    add_to_stage(g, slot, relay[g], relay_over(g, 1))

            staged(g, slot, part_of(home[g], t)).start()

            def finish(t=t, slot=slot):
                staged(g, slot, part_of(home[g], t)).wait()
                for r in range(held):
                    k = t * held + r
                    if ag.near and k in (1, 3):
                        at_end = place.z == (3 if k == 1 else 0)

                        @pl.when(at_end)
                        def _():
                            relay_over(g, k).start()

                        @pl.when(jnp.logical_not(at_end))
                        def _():
                            hand_over(g, k).start()
                    elif k:
                        hand_over(g, k).start()

            waiting.append(finish)

    def feed_forward(gate, up):
        def feed(part):
            a = part * half
            fetch(
                (full_gate.at[:, pl.ds(a, half)], weights.at[:, pl.ds(0, half)]),
                (full_up.at[:, pl.ds(a, half)], weights.at[:, pl.ds(half, half)]),
            )

            def columns(n):
                def body(m):
                    at = rows(m, size)
                    left = mixed[at, :]
                    gate_part = dot_nn(left, weights[:, rows(n, tile)])
                    up_part = dot_nn(
                        left, weights[:, pl.ds(pl.multiple_of(half + n * tile, tile), tile)]
                    )
                    to = pl.ds(pl.multiple_of(a + n * tile, tile), tile)
                    gate[at, to] = gate_part
                    up[at, to] = up_part
                    hidden[at, to] = (gate_part * jax.nn.sigmoid(gate_part) * up_part).astype(bf16)

                loop(4, body)

            loop(half // tile, columns)

        ag.arrived(3)
        ag.arrived(4)
        feed(0)
        take_dyb.done()
        dyb_copy.wait()
        tokens_copy = keep(all_dyb, tokens)
        ag.hand_on(6)
        ag.hand_on(7)
        ag.arrived(5)
        ag.arrived(6)
        feed(1)
        ag.hand_on(8)
        tokens_copy.wait()
        send_away(4, tokens, lambda: hidden[...])
        flush()
        ag.arrived(7)
        ag.arrived(8)
        fetch((full_down, weights))

        def columns(n):
            def body(m):
                at = rows(m, size)
                to = rows(n, tile)
                grad = dot_nn(tokens[at, :], weights[:, to])
                gate_part = gate[at, to]
                up_part = up[at, to]
                sigma = jax.nn.sigmoid(gate_part)
                feed_grad[at, to] = (
                    grad * up_part * sigma * (1.0 + gate_part * (1.0 - sigma))
                ).astype(bf16)
                feed_grad[at, pl.ds(pl.multiple_of(ff + n * tile, tile), tile)] = (
                    grad * gate_part * sigma
                ).astype(bf16)

            loop(4, body)

        loop(ff // tile, columns)

    pl.run_scoped(feed_forward, pltpu.VMEM((span, ff), f32), pltpu.VMEM((span, ff), f32))

    def mixed_grad(both):
        fetch(
            (full_gate, both.at[:, pl.ds(0, ff)]),
            (full_up, both.at[:, pl.ds(ff, ff)]),
        )

        def mixed_tile(start, count, n):
            return dot_nt(feed_grad[pl.ds(start, count), :], both[rows(n, step), :])

        side.drain()
        scattered.append(scatter(mixed_tile))

    scattered = []
    pl.run_scoped(mixed_grad, pltpu.VMEM((width, 2 * ff), bf16))
    other = scattered[0]
    send_away(2, mixed, lambda: feed_grad[:, pl.ds(0, ff)])
    flush()
    down_home = functools.partial(send_home, 4, tokens, lambda: hidden[...])
    down_home(order[:1])
    other.wait_recv()
    sums[...] = jnp.zeros_like(sums)
    head_sums[...] = jnp.zeros_like(head_sums)

    def second_back(i):
        at = rows(i, quarter)
        value = resid[at, :]
        scale = row_scale(value)
        unit = value * scale
        grad = total[at, :] + cross_in[at, :].astype(f32)
        sums[1:2, :] += jnp.sum(grad * unit, axis=0, keepdims=True)
        back = norm_back(grad, unit, scale, gains[1:2, :])
        result = dyb_ref[at, :].astype(f32) + back
        grad_own[at, :] = result
        cross_out[at, :] = result.astype(bf16)

    side.drain()
    loop(4, second_back)
    take_dresb = Gather(side, cross_out, all_dresb, size)
    dresb_copy = keep(cross_out, all_dresb.at[pl.ds(0, size)])
    send_away(3, mixed, lambda: feed_grad[:, pl.ds(ff, ff)])
    flush()
    down_home(order[1:2])
    take_dresb.forward()
    down_home(order[2:])
    flush()
    take_dresb.done()
    dresb_copy.wait()

    def attention_back(qkv_grad, qkv, k_act, v_act, ctx_grad, k_grad, v_grad):
        fetch(
            (all_dresb, tokens),
            (all_qkv, qkv),
            (full_out, weights.at[:, pl.ds(0, out_width)]),
        )

        def context_grad(m):
            ctx_grad[rows(m, size), :] = dot_nn(
                tokens[rows(m, size), :], weights[:, pl.ds(0, out_width)]
            ).astype(bf16)

        loop(4, context_grad)

        def head_back(raw, grad, gain, a):
            to = pl.ds(a * size, size)
            scale = row_scale(raw)
            unit = raw * scale
            turned = rope_back(grad, cos_ref[to, :], sin_ref[to, :])
            gain_part = jnp.sum(turned * unit, axis=0, keepdims=True)
            return norm_back(turned, unit, scale, gain).astype(bf16), gain_part

        def pair(p):
            keys_of(p, qkv, k_act, v_act)
            k_grad[...] = jnp.zeros_like(k_grad)
            v_grad[...] = jnp.zeros_like(v_grad)

            def head(g):
                column = pl.ds(pl.multiple_of((p * groups + g) * HD, HD), HD)
                for a in range(4):
                    at = rows(place.slot(a), size)
                    to = pl.ds(a * size, size)
                    last = (a + 1) * size
                    raw = qkv[at, column]
                    unit = raw * row_scale(raw) * head_gain[2:3, :]
                    query = rope(unit, cos_ref[to, :], sin_ref[to, :]).astype(bf16)
                    probs = softmax_block(query, k_act[0:last, :], a, size, last, length)
                    grad = ctx_grad[at, column]
                    probs_grad = dot_nt(grad, v_act[0:last, :])
                    v_grad[0:last, :] += dot_tn(probs.astype(bf16), grad)
                    delta = jnp.sum(probs * probs_grad, axis=-1, keepdims=True)
                    scores_grad = (probs * (probs_grad - delta)).astype(bf16)
                    query_grad = dot_nn(scores_grad, k_act[0:last, :]) * HD ** (-0.5)
                    k_grad[0:last, :] += dot_tn(scores_grad, query) * HD ** (-0.5)
                    made, gain_part = head_back(raw, query_grad, head_gain[2:3, :], a)
                    qkv_grad[at, column] = made
                    head_sums[0:1, :] += gain_part

            loop(groups, head)
            for a in range(4):
                at = rows(place.slot(a), size)
                to = pl.ds(a * size, size)
                column = pl.ds(pl.multiple_of((heads + p) * HD, HD), HD)
                made, gain_part = head_back(
                    qkv[at, column], k_grad[to, :], head_gain[3:4, :], a
                )
                qkv_grad[at, column] = made
                head_sums[1:2, :] += gain_part
                column = pl.ds(pl.multiple_of((heads + pairs + p) * HD, HD), HD)
                qkv_grad[at, column] = v_grad[to, :].astype(bf16)

        loop(pairs, pair)

    def finish_back(qkv_grad, normed, come_v, home_v, sum_v, sum_t):
        normed_copy = keep(all_normed, normed)
        qkv_copy = keep(full_qkv, weights.at[:, pl.ds(0, qkv_width)])
        send_away(1, tokens, lambda: ctx[...])
        normed_copy.wait()
        send_away(0, normed, lambda: qkv_grad[...])
        flush()
        gate_home = functools.partial(send_home, 2, mixed, lambda: feed_grad[:, pl.ds(0, ff)])
        up_home = functools.partial(send_home, 3, mixed, lambda: feed_grad[:, pl.ds(ff, ff)])
        out_home = functools.partial(send_home, 1, tokens, lambda: ctx[...])
        qkv_home = functools.partial(send_home, 0, normed, lambda: qkv_grad[...])
        gate_home(order[:-1])
        flush()
        qkv_copy.wait()
        written = []

        def finals(g):
            flush()
            wide_g = widths[g]
            mine = keep(home[g].at[pl.ds(0, block)], home_v.at[:, pl.ds(0, wide_g)])
            for k in range(1, depth):
                at = pl.ds((k - 1) * block, block)

                def bring(g=g, k=k, at=at):
                    hand_over(g, k).wait_recv()
                    made = pltpu.make_async_copy(
                        come[g].at[at], come_v.at[at, pl.ds(0, wide_g)], tile_sem
                    )
                    made.start()
                    made.wait()

                if ag.near and k in (1, 3):
                    here = place.z != (0 if k == 1 else 3)
                    pl.when(here)(bring)

                    @pl.when(jnp.logical_not(here))
                    def _(at=at):
                        come_v[at, 0:wide_g] = jnp.zeros((block, wide_g), bf16)
                else:
                    bring()
            mine.wait()
            while written:
                written.pop().wait()

            def add(i):
                at = rows(i, block // 4)
                value = home_v[at, 0:wide_g].astype(f32)
                for k in range(1, depth):
                    more = pl.ds(
                        pl.multiple_of((k - 1) * block + i * (block // 4), block // 4), block // 4
                    )
                    value = value + come_v[more, 0:wide_g].astype(f32)
                sum_v[at, 0:wide_g] = value

            loop(4, add)
            if g in (1, 4):
                for i in range(wide_g // HD):
                    sum_t[pl.ds(i * HD, HD), :] = sum_v[:, i * HD : (i + 1) * HD].T
                ref = o_output if g == 1 else o_down
                written.append(keep(sum_t.at[pl.ds(0, wide_g)], ref))
            elif g == 0:
                ends = (o_query, o_keyval.at[0], o_keyval.at[1])
                columns = (heads * HD, pairs * HD, pairs * HD)
                at = 0
                for ref, count in zip(ends, columns, strict=True):
                    written.append(keep(sum_v.at[:, pl.ds(at, count)], ref))
                    at += count
            else:
                written.append(keep(sum_v.at[:, pl.ds(0, wide_g)], o_gateup.at[g - 2]))

        def normed_tile(start, count, n):
            return dot_nt(
                qkv_grad[pl.ds(start, count), :], weights[rows(n, step), pl.ds(0, qkv_width)]
            )

        side.drain()
        other = scatter(normed_tile)
        finals(4)
        gate_home(order[-1:])
        up_home(order[:1])
        flush()
        other.wait_recv()

        def first_back(i):
            at = rows(i, quarter)
            value = x_ref[at, :].astype(f32)
            scale = row_scale(value)
            unit = value * scale
            grad = total[at, :] + cross_in[at, :].astype(f32)
            sums[0:1, :] += jnp.sum(grad * unit, axis=0, keepdims=True)
            grad_own[at, :] += norm_back(grad, unit, scale, gains[0:1, :])

        loop(4, first_back)
        pl.semaphore_signal(free_core, inc=1, device_id=place.side(0, 1), device_id_type=MESH)
        pl.semaphore_signal(free_other, inc=1, device_id=place.side(1, 0), device_id_type=MESH)

        for flip, (dy, dc) in enumerate(((0, 1), (1, 0))):
            norm_made = side.copy(sums, sums_in.at[flip], dy, dc)
            head_made = side.copy(head_sums, head_sums_in.at[flip], dy, dc)
            norm_made.wait_recv()
            head_made.wait_recv()
            side.drain()
            sums[...] += sums_in[flip]
            head_sums[...] += head_sums_in[flip]
        for made in gain_copies:
            made.wait_send()
        for b in range(wide):
            slots[b, :, 0:block] = sums[:, b * block : (b + 1) * block]
        last = []
        for dx in (0, 1):
            for k in range(depth):
                if k or dx:
                    to = dx * depth + k
                    at = dx * depth + (depth - k) % depth
                    made = remote(
                        slots.at[to], last_norm.at[at], gs.at[at], gr.at[at], place.far(k, dx)
                    )
                    made.start()
                    last.append(made)
                    made = remote(
                        head_sums,
                        last_head.at[at],
                        gs.at[wide + at],
                        gr.at[wide + at],
                        place.far(k, dx),
                    )
                    made.start()
                    last.append(made)
        up_home(order[1:-1])
        fetch((full_down, weights))

        def down_tile(start, count, n):
            return dot_nt(hidden[pl.ds(start, count), :], weights[rows(n, step), :])

        pl.semaphore_wait(free_core, 1)
        pl.semaphore_wait(free_other, 1)
        other = scatter(down_tile)
        grads = in_order(o_grad, grad_own, out=True)
        finals(2)
        up_home(order[-1:])
        flush()
        other.wait_recv()
        side.drain()
        cross_out[...] = (resid[...] + total[...] + cross_in[...].astype(f32)).astype(bf16)
        results = in_order(o_out, cross_out, out=True)
        out_home(None)
        qkv_home(order[:-1])
        finals(3)
        finals(1)
        qkv_home(order[-1:])
        finals(0)
        for made in grads + results + written:
            made.wait()
        for made in last:
            made.wait_recv()
        norm_total = slots[0]
        head_total = head_sums[...]
        for b in range(1, wide):
            norm_total = norm_total + last_norm[b]
            head_total = head_total + last_head[b]
        o_norm[...] = norm_total
        o_head[...] = head_total
        for made in last:
            made.wait_send()

    def back(qkv_grad):
        pl.run_scoped(
            functools.partial(attention_back, qkv_grad),
            pltpu.VMEM((span, qkv_width), f32),
            pltpu.VMEM((span, HD), bf16),
            pltpu.VMEM((span, HD), bf16),
            pltpu.VMEM((span, out_width), bf16),
            pltpu.VMEM((span, HD), f32),
            pltpu.VMEM((span, HD), f32),
        )
        pl.run_scoped(
            functools.partial(finish_back, qkv_grad),
            pltpu.VMEM((span, width), bf16),
            pltpu.VMEM(((depth - 1) * block, max(widths)), bf16),
            pltpu.VMEM((block, max(widths)), bf16),
            pltpu.VMEM((block, max(widths)), f32),
            pltpu.VMEM((max(widths), block), f32),
        )

    pl.run_scoped(back, pltpu.VMEM((span, qkv_width), bf16))
    for g in range(5):
        for t in range(steps):
            cross(g, t).wait_send()
        for k in range(1, depth):
            hand_over(g, k).wait_send()
    side.drain()
    ag.drain()


def layer_call(lengths, norm_gains, head_gains, x, dy, weights, heads, pairs):
    wide = lax.axis_size("wide")
    depth = wide // 2
    size, width = x.shape
    span = 4 * size
    block = width // wide
    inside = block % HD == 0
    ff = weights[3].shape[-1]
    widths = [(heads + 2 * pairs) * HD, heads * HD, ff, ff, ff]
    lanes = max(HD, block)
    shape = jax.ShapeDtypeStruct
    anywhere = pl.BlockSpec(memory_space=pl.ANY)
    vmem = pl.BlockSpec(memory_space=pltpu.VMEM)
    smem = pl.BlockSpec(memory_space=pltpu.SMEM)
    count = len(chunks_of(widths))
    cosine, sine = rope_tables(span)
    outs = [
        shape((8, lanes), f32),
        shape((8, HD), f32),
        shape((size, width), bf16),
        shape((size, width), f32),
        shape((block, heads * HD), f32),
        shape((2, block, pairs * HD), f32),
        shape((heads * HD, block), f32),
        shape((2, block, ff), f32),
        shape((ff, block), f32),
    ]
    outs += [shape((width // 2, w), bf16) for w in widths]
    outs += [shape(((depth - 1) * block, w), bf16) for w in widths]
    outs += [shape((width, w), bf16) for w in widths]
    outs += [shape((width // 2, w), bf16) for w in widths] * 2
    outs += [shape((block, w), bf16) for w in widths]
    outs += [
        shape((span, width), bf16),
        shape((span, width), bf16),
        shape((span, widths[0]), f32),
        shape((span, width), bf16),
    ]
    dma = pltpu.SemaphoreType.DMA
    if not inside:
        query, keyval, output, gateup, down = [w.astype(bf16) for w in weights]
        weights = [
            jnp.concatenate([query, keyval[0], keyval[1]], axis=1),
            output.T,
            gateup[0],
            gateup[1],
            down.T,
        ]
        owner, place = owners(wide), places(wide)
        x, dy = reorder(x, owner), reorder(dy, owner)
    results = pl.pallas_call(
        functools.partial(layer_kernel, wide, heads, pairs),
        out_shape=outs,
        in_specs=[smem] + [vmem] * 4 + [anywhere] * 7,
        out_specs=[vmem] * 2 + [anywhere] * (len(outs) - 2),
        scratch_shapes=[
            pltpu.VMEM((size, width), bf16),
            pltpu.VMEM((size, width), bf16),
            pltpu.VMEM((size, width), f32),
            pltpu.VMEM((8, lanes), f32),
            pltpu.VMEM((wide, 8, lanes), f32),
            pltpu.VMEM((8, width), f32),
            pltpu.VMEM((8, HD), f32),
            pltpu.VMEM((span, widths[1]), bf16),
            pltpu.VMEM((size, width), f32),
            pltpu.VMEM((size, width), f32),
            pltpu.VMEM((span, width), bf16),
            pltpu.VMEM((span, ff), bf16),
            pltpu.VMEM((width, ff), bf16),
            pltpu.VMEM((span, width), bf16),
            pltpu.VMEM((span, 2 * ff), bf16),
            pltpu.VMEM((2, max(block, HD), max(widths)), bf16),
            pltpu.VMEM((max(block, HD), max(widths)), bf16),
            pltpu.VMEM((2 * size, width), bf16),
            pltpu.VMEM((2 * size, width), bf16),
            pltpu.VMEM((size, width), bf16),
            pltpu.VMEM((size, width), bf16),
            pltpu.VMEM((8, width), f32),
            pltpu.VMEM((2, 8, width), f32),
            pltpu.VMEM((8, HD), f32),
            pltpu.VMEM((2, 8, HD), f32),
            pltpu.VMEM((wide, 8, lanes), f32),
            pltpu.VMEM((wide, 8, HD), f32),
            dma((count, 2 * depth)),
            dma((count, depth)),
            dma((count, depth)),
            dma((count, depth)),
            dma((40,)),
            dma((40,)),
            dma((2 * wide,)),
            dma((2 * wide,)),
            dma((160,)),
            dma((5, depth)),
            dma((5, depth)),
            dma((5, depth)),
            dma((5, depth)),
            dma((2,)),
            dma,
            pltpu.SemaphoreType.REGULAR,
            pltpu.SemaphoreType.REGULAR,
        ],
        compiler_params=pltpu.CompilerParams(
            collective_id=0, has_side_effects=True, vmem_limit_bytes=63 * MIB
        ),
    )(lengths, norm_gains, head_gains, cosine, sine, x, dy, *weights)
    results = list(results[:9])
    if not inside:
        results[2] = reorder(results[2], place)
        results[3] = reorder(results[3], place)
    return results


def per_device(
    layer_input,
    out_grad,
    lengths,
    query_weight,
    query_mean,
    query_square,
    keyval_weight,
    keyval_mean,
    keyval_square,
    output_weight,
    output_mean,
    output_square,
    gateup_weight,
    gateup_mean,
    gateup_square,
    down_weight,
    down_mean,
    down_square,
    norm_gains,
    norm_mean,
    norm_square,
    head_gains,
    head_mean,
    head_square,
):
    wide = lax.axis_size("wide")
    w = lax.axis_index("wide")
    block = layer_input.shape[2] // wide
    heads = query_weight.shape[1] // HD
    pairs = keyval_weight.shape[2] // HD
    weights = [query_weight, keyval_weight, output_weight, gateup_weight, down_weight]
    results = layer_call(
        lengths, norm_gains, head_gains, layer_input[0], out_grad[0], weights, heads, pairs
    )
    norm_total = results[0][0:2, 0:block]
    part = HD // wide
    head_total = lax.dynamic_slice(results[1], (0, w * part), (2, part))
    layer_out, input_grad = results[2][None], results[3][None]
    query_total, keyval_total, output_total, gateup_total, down_total = results[4:]
    query = adamw(query_weight, query_mean, query_square, query_total, 0.04)
    keyval = adamw(keyval_weight, keyval_mean, keyval_square, keyval_total, 0.04)
    output = adamw(output_weight, output_mean, output_square, output_total, 0.3)
    gateup = adamw(gateup_weight, gateup_mean, gateup_square, gateup_total, 0.04)
    down = adamw(down_weight, down_mean, down_square, down_total, 0.025)
    norm = adamw(norm_gains, norm_mean, norm_square, norm_total, 0.4)
    head = adamw(head_gains, head_mean, head_square, head_total, 0.4)
    return (layer_out, input_grad, *query, *keyval, *output, *gateup, *down, *norm, *head)


def solution(mesh):
    tokens = P("wide", "narrow", None)
    down = [P("wide", "narrow")] * 3
    pair = [P(None, "wide", "narrow")] * 3
    across = [P("narrow", "wide")] * 3
    gain = [P(None, "wide")] * 3
    weights = down + pair + across + pair + across + gain + gain
    return jax.shard_map(
        per_device,
        mesh=mesh,
        in_specs=(tokens, tokens, P("wide"), *weights),
        out_specs=(tokens, tokens, *weights),
        check_vma=False,
    )
```

```python
import functools

import jax
import jax.numpy as jnp
import numpy as np
from jax import lax
from jax.experimental import pallas as pl
from jax.experimental.pallas import tpu as pltpu
from jax.sharding import PartitionSpec as P

HD = 128
STEP = 5
MESH = pl.DeviceIdType.MESH
MIB = 2**20

norm_eps = 1e-06
rope_base = 1000000.0
beta_first = 0.5
beta_second = 0.5
adam_eps = 1e-08
weight_decay = 0.1
masked_fill = -1e30
f32 = jnp.float32
bf16 = jnp.bfloat16


def row_scale(values):
    return lax.rsqrt(jnp.mean(values * values, axis=-1, keepdims=True) + norm_eps)


def norm_back(grad, unit, scale, gain):
    scaled = grad * gain
    return scale * (scaled - unit * jnp.mean(scaled * unit, axis=-1, keepdims=True))


def adamw(weight, first, second, grad, rate):
    first_new = beta_first * first + (1.0 - beta_first) * grad
    second_new = beta_second * second + (1.0 - beta_second) * grad * grad
    first_hat = first_new / (1.0 - beta_first**STEP)
    second_hat = second_new / (1.0 - beta_second**STEP)
    weight_new = weight - rate * (
        first_hat / (jnp.sqrt(second_hat) + adam_eps) + weight_decay * weight
    )
    return (weight_new, first_new, second_new)


def rope_tables(length):
    half = HD // 2
    freqs = rope_base ** (-(np.arange(half, dtype=np.float32) * np.float32(2.0)) / np.float32(HD))
    angles = np.arange(length, dtype=np.float32)[:, None] * freqs.astype(np.float32)[None, :]
    cosine = np.cos(angles.astype(np.float64)).astype(np.float32)
    sine = np.sin(angles.astype(np.float64)).astype(np.float32)
    return (
        jnp.asarray(np.concatenate([cosine, cosine], axis=-1)),
        jnp.asarray(np.concatenate([-sine, sine], axis=-1)),
    )


def dot_nn(left, right):
    return lax.dot_general(left, right, (((1,), (0,)), ((), ())), preferred_element_type=f32)


def dot_nt(left, right):
    return lax.dot_general(left, right, (((1,), (1,)), ((), ())), preferred_element_type=f32)


def dot_tn(left, right):
    return lax.dot_general(left, right, (((0,), (0,)), ((), ())), preferred_element_type=f32)


def loop(count, step):
    def body(index, carry):
        step(index)
        return carry

    lax.fori_loop(0, count, body, 0)


def rows(index, size):
    return pl.ds(pl.multiple_of(index * size, size), size)


class Place:
    def __init__(self, wide, narrow):
        self.depth = wide // 2
        w = lax.axis_index("wide")
        n = lax.axis_index("narrow")
        self.w, self.n = w, n
        self.z = w // 2
        self.x = w - 2 * self.z
        self.y = n // 2
        self.c = n - 2 * self.y
        self.known = {(k, dx): self.reach(k, dx) for k in range(self.depth) for dx in (0, 1)}
        self.sides = {}
        for dy in (0, 1):
            for dc in (0, 1):
                y = self.y if dy == 0 else 1 - self.y
                c = self.c if dc == 0 else 1 - self.c
                self.sides[dy, dc] = (w, y * 2 + c)

    def reach(self, k, dx):
        x = self.x if dx == 0 else 1 - self.x
        return (lax.rem(self.z + k, self.depth) * 2 + x, self.n)

    def far(self, k, dx):
        return self.known[k, dx] if isinstance(k, int) else self.reach(k, dx)

    def side(self, dy, dc):
        return self.sides[dy, dc]

    def slot(self, block):
        ay, ac = block // 2, block % 2
        dy = lax.rem(self.y + ay, 2)
        dc = lax.rem(self.c + ac, 2)
        return dc * 2 + dy


def remote(src, dst, send, recv, device):
    return pltpu.make_async_remote_copy(
        src_ref=src,
        dst_ref=dst,
        send_sem=send,
        recv_sem=recv,
        device_id=device,
        device_id_type=MESH,
    )


class Side:
    def __init__(self, place, send, recv):
        self.place = place
        self.send = [send.at[i] for i in range(send.shape[0])]
        self.recv = [recv.at[i] for i in range(recv.shape[0])]
        self.used = 0
        self.sent = []

    def copy(self, src, dst, dy, dc):
        i = self.used
        self.used += 1
        made = remote(src, dst, self.send[i], self.recv[i], self.place.side(dy, dc))
        made.start()
        self.sent.append(made)
        return made

    def drain(self):
        for made in self.sent:
            made.wait_send()
        self.sent = []


class Gather:
    def __init__(self, side, own, buf, size):
        self.side, self.buf, self.size = side, buf, size
        self.across = side.copy(own, buf.at[pl.ds(size, size)], 1, 0)
        self.core = side.copy(own, buf.at[pl.ds(2 * size, size)], 0, 1)

    def forward(self):
        size = self.size
        self.across.wait_recv()
        self.last = self.side.copy(
            self.buf.at[pl.ds(size, size)], self.buf.at[pl.ds(3 * size, size)], 0, 1
        )

    def done(self):
        self.core.wait_recv()
        self.last.wait_recv()


class Wide:
    def __init__(self, place, block, chunks, full, zs, zr, xs, xr):
        self.place, self.block, self.chunks, self.full = place, block, chunks, full
        self.zs, self.zr, self.xs, self.xr = zs, zr, xs, xr
        self.near = place.depth == 4
        self.odd = place.z - 2 * (place.z // 2)

    def shared(self, i):
        return self.near and i == 3

    def early(self, i):
        return self.near and i == 8

    def pass_on(self, i, k):
        depth = self.place.depth
        return remote(
            self.slot(i, depth),
            self.slot(i, depth + k),
            self.xs.at[i, k],
            self.xr.at[i, k],
            self.place.far(depth - k, 0),
        )

    def beside(self, i):
        g, a, b = self.chunks[i]
        at = (self.place.depth + 3 - 2 * self.odd) * self.block
        return remote(
            self.slot(i, self.place.depth),
            self.full[g].at[pl.ds(pl.multiple_of(at, self.block), self.block), pl.ds(a, b - a)],
            self.xs.at[i, 1 + 2 * self.odd],
            self.xr.at[i, 3 - 2 * self.odd],
            self.place.far(1 + 2 * self.odd, 0),
        )

    def slot(self, i, index):
        g, a, b = self.chunks[i]
        return self.full[g].at[pl.ds(index * self.block, self.block), pl.ds(a, b - a)]

    def along(self, i, k):
        depth = self.place.depth
        return remote(
            self.slot(i, 0),
            self.slot(i, k),
            self.zs.at[i, k],
            self.zr.at[i, k],
            self.place.far(depth - k, 0),
        )

    def beyond(self, i, k):
        depth = self.place.depth
        return remote(
            self.slot(i, 2),
            self.slot(i, k),
            self.zs.at[i, depth + k],
            self.zr.at[i, k],
            self.place.far(1 if k == 1 else depth - 1, 0),
        )

    def across(self, i, k):
        depth = self.place.depth
        return remote(
            self.slot(i, k),
            self.slot(i, depth + k),
            self.xs.at[i, k],
            self.xr.at[i, k],
            self.place.far(0, 1),
        )

    def each(self, i, k, act):
        place = self.place
        if self.near and k in (1, 3):
            at_end = (place.z == 0) if k == 1 else (place.z == 3)

            @pl.when(jnp.logical_not(at_end))
            def _():
                act(self.along(i, k))
        else:
            act(self.along(i, k))

    def order(self):
        depth = self.place.depth
        return (2, 1, 3) if self.near else tuple(range(1, depth))

    def issue(self, i):
        if i >= len(self.chunks):
            return
        self.across(i, 0).start()
        for k in self.order():
            self.each(i, k, lambda made: made.start())

    def hand_on(self, i):
        z = self.place.z
        if self.early(i):
            self.across(i, 0).wait_recv()
            for k in self.order():
                self.pass_on(i, k).start()
        for k in self.order():
            self.along(i, k).wait_recv()
            if self.near and k == 2:

                @pl.when(z == 2)
                def _():
                    self.beyond(i, 1).start()

                @pl.when(z == 1)
                def _():
                    self.beyond(i, 3).start()

            if self.early(i):
                continue
            if self.shared(i) and k in (1, 3):

                @pl.when(self.odd == (1 if k == 1 else 0))
                def _():
                    self.across(i, k).start()
            else:
                self.across(i, k).start()
        if self.shared(i):
            self.across(i, 0).wait_recv()
            self.beside(i).start()

    def arrived(self, i):
        for k in range(self.place.depth):
            if k or not (self.shared(i) or self.early(i)):
                self.across(i, k).wait_recv()

    def drain(self):
        z = self.place.z
        for i in range(len(self.chunks)):
            for k in range(self.place.depth):
                if k:
                    self.each(i, k, lambda made: made.wait_send())
                if self.near and k in (1, 3):

                    @pl.when(z == (2 if k == 1 else 1))
                    def _():
                        self.beyond(i, k).wait_send()

                self.across(i, k).wait_send()


def greet(place):
    depth = place.depth
    peers = [place.far(k, dx) for dx in (0, 1) for k in range(depth) if k or dx]
    peers += [place.side(1, 0), place.side(0, 1)]
    barrier = pltpu.get_barrier_semaphore()
    for peer in peers:
        pl.semaphore_signal(barrier, inc=1, device_id=peer, device_id_type=MESH)
    pl.semaphore_wait(barrier, len(peers))


def turn(values):
    return pltpu.roll(values, HD // 2, 1)


def rope(values, cosine, sine):
    return values * cosine + turn(values) * sine


def rope_back(grads, cosine, sine):
    return grads * cosine - turn(grads) * sine


def softmax_block(query, keys, block, size, count, length):
    scores = dot_nt(query, keys) * HD ** (-0.5)
    shape = scores.shape
    at = block * size + lax.broadcasted_iota(jnp.int32, shape, 0)
    to = lax.broadcasted_iota(jnp.int32, shape, 1)
    scores = jnp.where((to <= at) & (to < length), scores, masked_fill)
    lifted = jnp.exp(scores - jnp.max(scores, axis=-1, keepdims=True))
    return lifted / jnp.sum(lifted, axis=-1, keepdims=True)


def chunks_of(widths):
    qkv, out, gate, up, down = widths
    return [
        (0, 0, qkv // 2),
        (0, qkv // 2, qkv),
        (1, 0, out),
        (2, 0, gate // 2),
        (3, 0, up // 2),
        (2, gate // 2, gate),
        (3, up // 2, up),
        (4, 0, down // 2),
        (4, down // 2, down),
    ]


def owners(wide):
    depth = wide // 2
    w = lax.axis_index("wide")
    z, x = w // 2, w % 2
    return [
        ((z + k) % depth) * 2 + (x if dx == 0 else 1 - x) for dx in (0, 1) for k in range(depth)
    ]


def places(wide):
    depth = wide // 2
    w = lax.axis_index("wide")
    z, x = w // 2, w % 2
    return [
        jnp.where(x == o % 2, 0, depth) + (o // 2 - z) % depth for o in range(wide)
    ]


def reorder(values, order):
    block = values.shape[-1] // len(order)
    return jnp.concatenate(
        [lax.dynamic_slice_in_dim(values, at * block, block, axis=-1) for at in order], axis=-1
    )


def layer_kernel(
    wide,
    heads,
    pairs,
    length_ref,
    norm_ref,
    head_ref,
    cos_ref,
    sin_ref,
    x_in,
    dy_in,
    w_query,
    w_keyval,
    w_output,
    w_gateup,
    w_down,
    o_norm,
    o_head,
    o_out,
    o_grad,
    o_query,
    o_keyval,
    o_output,
    o_gateup,
    o_down,
    home_qkv,
    home_out,
    home_gate,
    home_up,
    home_down,
    come_qkv,
    come_out,
    come_gate,
    come_up,
    come_down,
    full_qkv,
    full_out,
    full_gate,
    full_up,
    full_down,
    away_qkv,
    away_out,
    away_gate,
    away_up,
    away_down,
    got_qkv,
    got_out,
    got_gate,
    got_up,
    got_down,
    relay_qkv,
    relay_out,
    relay_gate,
    relay_up,
    relay_down,
    aside_up,
    aside_down,
    all_dyb,
    all_normed,
    all_qkv,
    all_dresb,
    dyb_ref,
    grad_own,
    gain_ref,
    slots,
    gains,
    head_gain,
    ctx,
    resid,
    total,
    mixed,
    hidden,
    weights,
    tokens,
    feed_grad,
    stage,
    arrived_tile,
    half_out,
    half_in,
    cross_out,
    cross_in,
    sums,
    sums_in,
    head_sums,
    head_sums_in,
    last_norm,
    last_head,
    zs,
    zr,
    xs,
    xr,
    ns,
    nr,
    gs,
    gr,
    ls,
    rxs,
    rxr,
    rzs,
    rzr,
    stage_sem,
    tile_sem,
    free_core,
    free_other,
):
    place = Place(wide, 4)
    depth = place.depth
    size, width = x_in.shape
    block = width // wide
    inside = block % HD == 0
    ff = hidden.shape[1]
    groups = heads // pairs
    span = 4 * size
    full = [full_qkv, full_out, full_gate, full_up, full_down]
    away = [away_qkv, away_out, away_gate, away_up, away_down]
    got = [got_qkv, got_out, got_gate, got_up, got_down]
    home = [home_qkv, home_out, home_gate, home_up, home_down]
    come = [come_qkv, come_out, come_gate, come_up, come_down]
    relay = [relay_qkv, relay_out, relay_gate, relay_up, relay_down]
    aside = [aside_up, aside_down]
    widths = [ref.shape[1] for ref in full]
    qkv_width, out_width = widths[0], widths[1]
    chunks = chunks_of(widths)
    ag = Wide(place, block, chunks, full, zs, zr, xs, xr)
    side = Side(place, ns, nr)
    copies = []
    quarter = size // 4

    def keep(src, dst):
        made = pltpu.make_async_copy(src, dst, ls.at[len(copies)])
        made.start()
        copies.append(made)
        return made

    def fetch(*pairs_of):
        made = [keep(src, dst) for src, dst in pairs_of]
        for one in made:
            one.wait()

    def in_order(ref, buf, out=False):
        if not inside:
            return [keep(buf, ref) if out else keep(ref, buf)]
        made = []
        for b in range(wide):
            w, _ = place.far(b % depth, b // depth)
            there = ref.at[:, pl.ds(pl.multiple_of(w * block, block), block)]
            here = buf.at[:, pl.ds(b * block, block)]
            made.append(keep(here, there) if out else keep(there, here))
        return made

    def land(g, buf):
        if not inside:
            return [keep([w_query, w_keyval, w_output, w_gateup, w_down][g], full[g].at[0:block])]
        if g == 0:
            at, made = 0, []
            for ref in (w_query, w_keyval.at[0], w_keyval.at[1]):
                made.append(keep(ref, buf.at[:, pl.ds(at, ref.shape[1])]))
                at += ref.shape[1]
            return made
        if g in (2, 3):
            return [keep(w_gateup.at[g - 2], buf.at[:, pl.ds(0, widths[g])])]
        ref = w_output if g == 1 else w_down
        return [
            keep(ref.at[pl.ds(i * block, block)], buf.at[:, pl.ds(i * block, block)])
            for i in range(widths[g] // block)
        ]

    def settle(g, buf, made):
        for one in made:
            one.wait()
        if not inside:
            return
        slot = g % 2
        if g in (1, 4):
            for i in range(widths[g] // block):
                at = pl.ds(i * block, block)
                stage[slot, :, at] = buf[:, at].T.astype(bf16)
        else:

            def cast(i):
                at = rows(i, block // 4)
                stage[slot, at, pl.ds(0, widths[g])] = buf[at, 0 : widths[g]].astype(bf16)

            loop(4, cast)
        fetch((stage.at[slot, :, pl.ds(0, widths[g])], full[g].at[pl.ds(0, block)]))

    waiting = []

    def flush():
        while waiting:
            waiting.pop(0)()

    landing = land(0, total)
    x_copies = in_order(x_in, tokens.at[pl.ds(0, size)])
    landing_out = land(1, resid)
    dy_copies = in_order(dy_in, dyb_ref)

    part = head_ref.shape[1]
    gain_ref[...] = jnp.zeros_like(gain_ref)
    gain_ref[0:2, 0:part] = head_ref[...]
    spread = pltpu.roll(gain_ref[:, 0:HD], place.w * part, 1)
    gain_ref[:, 0:HD] = pltpu.roll(spread, 2, 0)
    gain_ref[0:2, 0:block] = norm_ref[...]
    gain_ref[...] = gain_ref[...].astype(bf16).astype(f32)
    greet(place)

    gain_copies = []
    for dx in (0, 1):
        for k in range(depth):
            if k or dx:
                at = dx * depth + (depth - k) % depth
                made = remote(gain_ref, slots.at[at], gs.at[at], gr.at[at], place.far(k, dx))
                made.start()
                gain_copies.append(made)
    settle(0, total, landing)
    ag.issue(0)
    ag.issue(1)
    landing = land(2, total)
    settle(1, resid, landing_out)
    ag.issue(2)
    landing_up = land(3, resid)
    window = 4

    def hand(i):
        flush()
        ag.hand_on(i)
        ag.issue(i + window)

    settle(2, total, landing)
    ag.issue(3)
    landing = land(4, total)
    settle(3, resid, landing_up)
    slots[0] = gain_ref[...]
    for made in gain_copies:
        made.wait_recv()
    gains[...] = jnp.concatenate([slots[b][:, :block] for b in range(wide)], axis=1)
    heads_row = slots[0][:, :HD]
    for b in range(1, wide):
        heads_row = heads_row + slots[b][:, :HD]
    head_gain[...] = heads_row
    for made in x_copies:
        made.wait()

    def first_norm(i):
        at = rows(i, quarter)
        x = tokens[at, :].astype(f32)
        cross_out[at, :] = (x * row_scale(x) * gains[0:1, :]).astype(bf16)

    loop(4, first_norm)
    take_normed = Gather(side, cross_out, all_normed, size)
    normed_copy = keep(cross_out, all_normed.at[pl.ds(0, size)])
    settle(4, total, landing)
    hand(0)
    length = length_ref[0]
    for made in dy_copies:
        made.wait()

    def mask(i):
        at = rows(i, quarter)
        value = dyb_ref[at, :].astype(f32)
        where = place.n * size + i * quarter + lax.broadcasted_iota(jnp.int32, value.shape, 0)
        dyb_ref[at, :] = jnp.where(where < length, value, 0.0).astype(bf16)

    loop(4, mask)
    take_dyb = Gather(side, dyb_ref, all_dyb, size)
    dyb_copy = keep(dyb_ref, all_dyb.at[pl.ds(0, size)])
    hand(1)
    take_normed.forward()
    take_dyb.forward()
    hand(2)
    take_dyb.done()
    dyb_copy.wait()
    take_normed.done()
    normed_copy.wait()
    ag.arrived(0)
    ag.arrived(1)

    def keys_of(p, qkv, k_act, v_act):
        for a in range(4):
            at = rows(place.slot(a), size)
            to = pl.ds(a * size, size)
            raw = qkv[at, pl.ds(pl.multiple_of((heads + p) * HD, HD), HD)]
            unit = raw * row_scale(raw) * head_gain[3:4, :]
            k_act[to, :] = rope(unit, cos_ref[to, :], sin_ref[to, :]).astype(bf16)
            v_act[to, :] = qkv[
                at, pl.ds(pl.multiple_of((heads + pairs + p) * HD, HD), HD)
            ].astype(bf16)

    def attention(normed, qkv, k_act, v_act):
        fetch((all_normed, normed), (full_qkv, weights.at[:, pl.ds(0, qkv_width)]))

        def project(m):
            for n in range(qkv_width // 512):
                qkv[rows(m, size), pl.ds(n * 512, 512)] = dot_nn(
                    normed[rows(m, size), :], weights[:, pl.ds(n * 512, 512)]
                )

        loop(4, project)
        qkv_copy = keep(qkv, all_qkv)

        def pair(p):
            keys_of(p, qkv, k_act, v_act)

            def head(g):
                column = pl.ds(pl.multiple_of((p * groups + g) * HD, HD), HD)
                for a in range(4):
                    at = rows(place.slot(a), size)
                    to = pl.ds(a * size, size)
                    raw = qkv[at, column]
                    unit = raw * row_scale(raw) * head_gain[2:3, :]
                    query = rope(unit, cos_ref[to, :], sin_ref[to, :]).astype(bf16)
                    last = (a + 1) * size
                    probs = softmax_block(query, k_act[0:last, :], a, size, last, length)
                    ctx[at, column] = dot_nn(probs.astype(bf16), v_act[0:last, :]).astype(bf16)

            loop(groups, head)

        hand(3)
        for p in range(pairs):
            pair(p)
        qkv_copy.wait()

    pl.run_scoped(
        attention,
        pltpu.VMEM((span, width), bf16),
        pltpu.VMEM((span, qkv_width), f32),
        pltpu.VMEM((span, HD), bf16),
        pltpu.VMEM((span, HD), bf16),
    )
    ag.arrived(2)
    fetch((full_out, weights.at[:, pl.ds(0, out_width)]))
    step = 512

    class Scatter:
        def __init__(self, tile):
            self.tile = tile

        def half(self):
            flush()

            def one(n):
                half_out[:, rows(n, step)] = self.tile(2 * size, 2 * size, n).astype(bf16)

            loop(width // step, one)
            self.core = side.copy(half_out, half_in, 0, 1)

        def own(self):
            flush()

            def one(n):
                total[:, rows(n, step)] = self.tile(0, size, n)

            loop(width // step, one)

        def rest(self):
            flush()
            self.core.wait_recv()
            side.drain()

            def one(n):
                at = rows(n, step)
                part = self.tile(size, size, n) + half_in[pl.ds(size, size), at].astype(f32)
                cross_out[:, at] = part.astype(bf16)

            loop(width // step, one)
            self.other = side.copy(cross_out, cross_in, 1, 0)

            def add(i):
                at = rows(i, quarter)
                total[at, :] += half_in[at, :].astype(f32)

            loop(4, add)

        def done(self):
            flush()
            self.other.wait_recv()

    def out_tile(start, count, n):
        return dot_nt(ctx[pl.ds(start, count), :], weights[rows(n, step), pl.ds(0, out_width)])

    summed_out = Scatter(out_tile)
    summed_out.half()
    summed_out.own()
    hand(4)
    hand(5)
    summed_out.rest()
    summed_out.done()

    def second_norm(i):
        at = rows(i, quarter)
        value = tokens[at, :].astype(f32) + total[at, :] + cross_in[at, :].astype(f32)
        resid[at, :] = value
        mixed[at, :] = (value * row_scale(value) * gains[1:2, :]).astype(bf16)

    loop(4, second_norm)
    take_mixed = Gather(side, mixed.at[pl.ds(0, size)], mixed, size)
    hand(6)
    take_mixed.forward()
    take_mixed.done()
    hand(7)
    half = ff // 2
    tile = 256

    piece = max(block, HD)
    steps = depth * block // piece
    held = piece // block

    def staged(g, slot, to):
        return pltpu.make_async_copy(
            stage.at[slot, :, pl.ds(0, full[g].shape[1])], to, stage_sem.at[slot]
        )

    def part_of(ref, t):
        return ref.at[rows(t, piece)]

    def cross(g, t):
        return remote(
            part_of(away[g], t), part_of(got[g], t), rxs.at[g, t], rxr.at[g, t], place.far(0, 1)
        )

    def hand_over(g, k):
        return remote(
            home[g].at[rows(k, block)],
            come[g].at[rows(k - 1, block)],
            rzs.at[g, k],
            rzr.at[g, k],
            place.far(k, 0),
        )

    beside, beyond = 1 + 2 * ag.odd, 3 - 2 * ag.odd

    def lean_over(g):
        return remote(
            part_of(away[g], beside),
            aside[g - 3],
            rxs.at[g, beside],
            rxr.at[g, depth],
            place.far(beside, 0),
        )

    def relay_over(g):
        return remote(
            part_of(home[g], beyond),
            relay[g],
            rzs.at[g, beyond],
            rzr.at[g, 0],
            place.far(depth - beyond, 0),
        )

    def add_to_stage(g, slot, src, made):
        wide_g = widths[g]
        made.wait_recv()
        more = pltpu.make_async_copy(src, arrived_tile.at[:, pl.ds(0, wide_g)], tile_sem)
        more.start()
        more.wait()
        stage[slot, :, 0:wide_g] = (
            stage[slot, :, 0:wide_g].astype(f32) + arrived_tile[:, 0:wide_g].astype(f32)
        ).astype(bf16)

    operands = {}
    turns = [0]
    gone = {g: 0 for g in range(5)}
    come_home = {g: 0 for g in range(5)}

    def known(t, value):
        return isinstance(t, int) and t == value

    def product(g, t):
        left, right = operands[g]
        return dot_tn(left[:, rows(t, piece)], right())

    def send(g, t, lean=False):
        wide_g = widths[g]
        made = product(g, steps + t)
        flush()
        slot = turns[0] % 2
        turns[0] += 1
        stage[slot, :, 0:wide_g] = made.astype(bf16)
        if lean and known(t, 0):
            add_to_stage(g, slot, aside[g - 3], lean_over(g))
        staged(g, slot, part_of(away[g], t)).start()

        def finish():
            staged(g, slot, part_of(away[g], t)).wait()
            if lean and t is beside:
                lean_over(g).start()
            else:
                cross(g, t).start()

        waiting.append(finish)

    def take(g, t, bare=False):
        wide_g = widths[g]
        flush()
        slot = turns[0] % 2
        turns[0] += 1
        if bare:
            stage[slot, :, 0:wide_g] = product(g, t).astype(bf16)
        else:
            cross(g, t).wait_recv()
            get = pltpu.make_async_copy(
                part_of(got[g], t), arrived_tile.at[:, pl.ds(0, wide_g)], tile_sem
            )
            get.start()
            made = product(g, t)
            get.wait()
            made = made + arrived_tile[:, 0:wide_g].astype(f32)
            stage[slot, :, 0:wide_g] = made.astype(bf16)
        if ag.near and known(t, 2):

            @pl.when((place.z == 1) | (place.z == 2))
            def _():
                add_to_stage(g, slot, relay[g], relay_over(g))

        staged(g, slot, part_of(home[g], t)).start()

        def finish():
            staged(g, slot, part_of(home[g], t)).wait()
            if ag.near:
                if t is beyond:
                    at_end = (place.z == 0) | (place.z == 3)

                    @pl.when(at_end)
                    def _():
                        relay_over(g).start()

                    @pl.when(jnp.logical_not(at_end))
                    def _():
                        hand_over(g, t).start()
                elif not known(t, 0):
                    hand_over(g, t).start()
                return
            for r in range(held):
                if t * held + r:
                    hand_over(g, t * held + r).start()

        waiting.append(finish)

    def away_step(g):
        i = gone[g]
        gone[g] += 1
        if not ag.near:
            for t in range(steps) if i == 0 else ():
                send(g, t)
            return
        lean = g in (3, 4)
        send(g, ((beside, beyond, 2, 0) if lean else (beyond, beside, 2, 0))[i], lean)

    def home_step(g, which):
        come_home[g] += 1
        if not ag.near:
            for t in tuple(range(1, steps)) + (0,) if come_home[g] == 4 else ():
                take(g, t)
            return
        lean = g in (3, 4)
        order = (beside, beyond, 2, 0) if lean else (beyond, beside, 2, 0)
        take(g, order[which], lean and which == 0)

    tokens_copy = keep(all_dyb, tokens)

    def feed_forward(gate, up):
        def feed(part):
            a = part * half
            fetch(
                (full_gate.at[:, pl.ds(a, half)], weights.at[:, pl.ds(0, half)]),
                (full_up.at[:, pl.ds(a, half)], weights.at[:, pl.ds(half, half)]),
            )

            def columns(n):
                def body(m):
                    at = rows(m, size)
                    left = mixed[at, :]
                    gate_part = dot_nn(left, weights[:, rows(n, tile)])
                    up_part = dot_nn(
                        left, weights[:, pl.ds(pl.multiple_of(half + n * tile, tile), tile)]
                    )
                    to = pl.ds(pl.multiple_of(a + n * tile, tile), tile)
                    gate[at, to] = gate_part
                    up[at, to] = up_part
                    hidden[at, to] = (gate_part * jax.nn.sigmoid(gate_part) * up_part).astype(bf16)

                loop(4, body)

            loop(half // tile, columns)

        ag.arrived(3)
        ag.arrived(4)
        feed(0)
        hand(8)
        ag.arrived(5)
        ag.arrived(6)
        feed(1)
        tokens_copy.wait()
        operands[4] = tokens, lambda: hidden[...]
        away_step(4)
        home_step(4, 0)
        away_step(4)
        away_step(4)
        flush()
        ag.arrived(7)
        ag.arrived(8)
        fetch((full_down, weights))

        def columns(n):
            def body(m):
                at = rows(m, size)
                to = rows(n, tile)
                grad = dot_nn(tokens[at, :], weights[:, to])
                gate_part = gate[at, to]
                up_part = up[at, to]
                sigma = jax.nn.sigmoid(gate_part)
                feed_grad[at, to] = (
                    grad * up_part * sigma * (1.0 + gate_part * (1.0 - sigma))
                ).astype(bf16)
                feed_grad[at, pl.ds(pl.multiple_of(ff + n * tile, tile), tile)] = (
                    grad * gate_part * sigma
                ).astype(bf16)

            loop(4, body)

        loop(ff // tile, columns)

    pl.run_scoped(feed_forward, pltpu.VMEM((span, ff), f32), pltpu.VMEM((span, ff), f32))

    operands[2] = mixed, lambda: feed_grad[:, pl.ds(0, ff)]
    operands[3] = mixed, lambda: feed_grad[:, pl.ds(ff, ff)]
    away_step(3)
    away_step(2)
    away_step(3)
    flush()

    def mixed_grad(both):
        fetch(
            (full_gate, both.at[:, pl.ds(0, ff)]),
            (full_up, both.at[:, pl.ds(ff, ff)]),
        )

        def mixed_tile(start, count, n):
            return dot_nt(feed_grad[pl.ds(start, count), :], both[rows(n, step), :])

        summed.append(Scatter(mixed_tile))
        summed[0].half()
        summed[0].own()
        summed[0].rest()

    summed = []
    pl.run_scoped(mixed_grad, pltpu.VMEM((width, 2 * ff), bf16))
    home_step(4, 1)
    home_step(2, 0)
    home_step(4, 2)
    away_step(2)
    away_step(4)
    away_step(2)
    home_step(3, 1)
    away_step(2)
    summed[0].done()
    sums[...] = jnp.zeros_like(sums)
    head_sums[...] = jnp.zeros_like(head_sums)

    def second_back(i):
        at = rows(i, quarter)
        value = resid[at, :]
        scale = row_scale(value)
        unit = value * scale
        grad = total[at, :] + cross_in[at, :].astype(f32)
        sums[1:2, :] += jnp.sum(grad * unit, axis=0, keepdims=True)
        back = norm_back(grad, unit, scale, gains[1:2, :])
        result = dyb_ref[at, :].astype(f32) + back
        grad_own[at, :] = result
        cross_out[at, :] = result.astype(bf16)

    side.drain()
    loop(4, second_back)
    take_dresb = Gather(side, cross_out, all_dresb, size)
    dresb_copy = keep(cross_out, all_dresb.at[pl.ds(0, size)])
    take_dresb.core.wait_recv()
    away_step(3)

    def down_tile(start, count, n):
        return dot_nt(hidden[pl.ds(start, count), :], weights[rows(n, step), :])

    summed_down = Scatter(down_tile)
    summed_down.half()
    home_step(2, 1)
    summed_down.own()
    home_step(4, 3)
    home_step(3, 0)
    flush()
    take_dresb.forward()
    dresb_copy.wait()
    summed_down.rest()
    pl.semaphore_signal(free_core, inc=1, device_id=place.side(0, 1), device_id_type=MESH)
    take_dresb.last.wait_recv()

    def attention_back(qkv_grad, qkv, k_act, v_act, ctx_grad, k_grad, v_grad):
        fetch(
            (all_dresb, tokens),
            (all_qkv, qkv),
            (full_out, weights.at[:, pl.ds(0, out_width)]),
        )

        operands[1] = tokens, lambda: ctx[...]

        def context_grad(m):
            ctx_grad[rows(m, size), :] = dot_nn(
                tokens[rows(m, size), :], weights[:, pl.ds(0, out_width)]
            ).astype(bf16)

        loop(4, context_grad)

        def head_back(raw, grad, gain, a):
            to = pl.ds(a * size, size)
            scale = row_scale(raw)
            unit = raw * scale
            turned = rope_back(grad, cos_ref[to, :], sin_ref[to, :])
            gain_part = jnp.sum(turned * unit, axis=0, keepdims=True)
            return norm_back(turned, unit, scale, gain).astype(bf16), gain_part

        def pair(p):
            keys_of(p, qkv, k_act, v_act)
            k_grad[...] = jnp.zeros_like(k_grad)
            v_grad[...] = jnp.zeros_like(v_grad)

            def head(g):
                column = pl.ds(pl.multiple_of((p * groups + g) * HD, HD), HD)
                for a in range(4):
                    at = rows(place.slot(a), size)
                    to = pl.ds(a * size, size)
                    last = (a + 1) * size
                    raw = qkv[at, column]
                    unit = raw * row_scale(raw) * head_gain[2:3, :]
                    query = rope(unit, cos_ref[to, :], sin_ref[to, :]).astype(bf16)
                    probs = softmax_block(query, k_act[0:last, :], a, size, last, length)
                    grad = ctx_grad[at, column]
                    probs_grad = dot_nt(grad, v_act[0:last, :])
                    v_grad[0:last, :] += dot_tn(probs.astype(bf16), grad)
                    delta = jnp.sum(probs * probs_grad, axis=-1, keepdims=True)
                    scores_grad = (probs * (probs_grad - delta)).astype(bf16)
                    query_grad = dot_nn(scores_grad, k_act[0:last, :]) * HD ** (-0.5)
                    k_grad[0:last, :] += dot_tn(scores_grad, query) * HD ** (-0.5)
                    made, gain_part = head_back(raw, query_grad, head_gain[2:3, :], a)
                    qkv_grad[at, column] = made
                    head_sums[0:1, :] += gain_part

            loop(groups, head)
            for a in range(4):
                at = rows(place.slot(a), size)
                to = pl.ds(a * size, size)
                column = pl.ds(pl.multiple_of((heads + p) * HD, HD), HD)
                made, gain_part = head_back(
                    qkv[at, column], k_grad[to, :], head_gain[3:4, :], a
                )
                qkv_grad[at, column] = made
                head_sums[1:2, :] += gain_part
                column = pl.ds(pl.multiple_of((heads + pairs + p) * HD, HD), HD)
                qkv_grad[at, column] = v_grad[to, :].astype(bf16)

        pair(0)
        home_step(2, 2)
        away_step(1)
        flush()
        summed_down.done()
        side.drain()

        def last_sum(i):
            at = rows(i, quarter)
            value = resid[at, :] + total[at, :] + cross_in[at, :].astype(f32)
            cross_out[at, :] = value.astype(bf16)

        loop(4, last_sum)
        results.extend(in_order(o_out, cross_out, out=True))
        pl.semaphore_signal(free_other, inc=1, device_id=place.side(1, 0), device_id_type=MESH)
        for p in range(1, pairs):
            pair(p)
        for made in results:
            made.wait()

    results = []

    def finish_back(qkv_grad, normed, come_v, home_v, sum_v, sum_t):
        normed_copy = keep(all_normed, normed)
        qkv_copy = keep(full_qkv, weights.at[:, pl.ds(0, qkv_width)])
        operands[0] = normed, lambda: qkv_grad[...]
        normed_copy.wait()
        away_step(0)
        away_step(0)
        away_step(1)
        flush()
        qkv_copy.wait()
        written = []

        def finals(g):
            flush()
            wide_g = widths[g]
            mine = keep(home[g].at[pl.ds(0, block)], home_v.at[:, pl.ds(0, wide_g)])
            for k in range(1, depth):
                at = pl.ds((k - 1) * block, block)

                def bring(g=g, k=k, at=at):
                    hand_over(g, k).wait_recv()
                    made = pltpu.make_async_copy(
                        come[g].at[at], come_v.at[at, pl.ds(0, wide_g)], tile_sem
                    )
                    made.start()
                    made.wait()

                if ag.near and k in (1, 3):
                    here = place.z != (0 if k == 1 else 3)
                    pl.when(here)(bring)

                    @pl.when(jnp.logical_not(here))
                    def _(at=at):
                        come_v[at, 0:wide_g] = jnp.zeros((block, wide_g), bf16)
                else:
                    bring()
            mine.wait()
            while written:
                written.pop().wait()

            def add(i):
                at = rows(i, block // 4)
                value = home_v[at, 0:wide_g].astype(f32)
                for k in range(1, depth):
                    more = pl.ds(
                        pl.multiple_of((k - 1) * block + i * (block // 4), block // 4), block // 4
                    )
                    value = value + come_v[more, 0:wide_g].astype(f32)
                sum_v[at, 0:wide_g] = value

            loop(4, add)
            if g in (1, 4):
                for i in range(wide_g // HD):
                    sum_t[pl.ds(i * HD, HD), :] = sum_v[:, i * HD : (i + 1) * HD].T
                ref = o_output if g == 1 else o_down
                written.append(keep(sum_t.at[pl.ds(0, wide_g)], ref))
            elif g == 0:
                ends = (o_query, o_keyval.at[0], o_keyval.at[1])
                columns = (heads * HD, pairs * HD, pairs * HD)
                at = 0
                for ref, count in zip(ends, columns, strict=True):
                    written.append(keep(sum_v.at[:, pl.ds(at, count)], ref))
                    at += count
            else:
                written.append(keep(sum_v.at[:, pl.ds(0, wide_g)], o_gateup.at[g - 2]))

        def normed_tile(start, count, n):
            return dot_nt(
                qkv_grad[pl.ds(start, count), :], weights[rows(n, step), pl.ds(0, qkv_width)]
            )

        summed_normed = Scatter(normed_tile)
        pl.semaphore_wait(free_core, 1)
        summed_normed.half()
        home_step(1, 0)
        summed_normed.own()
        home_step(3, 2)
        pl.semaphore_wait(free_other, 1)
        summed_normed.rest()
        x_again = in_order(x_in, half_out.at[pl.ds(0, size)])
        home_step(2, 3)
        away_step(0)
        away_step(1)
        finals(4)
        away_step(1)
        home_step(0, 1)
        finals(2)
        home_step(1, 1)
        away_step(3)
        home_step(0, 0)
        summed_normed.done()
        for made in x_again:
            made.wait()

        def first_back(i):
            at = rows(i, quarter)
            value = half_out[at, :].astype(f32)
            scale = row_scale(value)
            unit = value * scale
            grad = total[at, :] + cross_in[at, :].astype(f32)
            sums[0:1, :] += jnp.sum(grad * unit, axis=0, keepdims=True)
            grad_own[at, :] += norm_back(grad, unit, scale, gains[0:1, :])

        loop(4, first_back)
        grads = in_order(o_grad, grad_own, out=True)

        def trade(flip, dy, dc):
            return (
                side.copy(sums, sums_in.at[flip], dy, dc),
                side.copy(head_sums, head_sums_in.at[flip], dy, dc),
            )

        def add_trade(flip, made):
            flush()
            for one in made:
                one.wait_recv()
            side.drain()
            sums[...] += sums_in[flip]
            head_sums[...] += head_sums_in[flip]

        made = trade(0, 0, 1)
        home_step(1, 2)
        add_trade(0, made)
        made = trade(1, 1, 0)
        home_step(1, 3)
        away_step(0)
        home_step(0, 2)
        add_trade(1, made)
        for made in gain_copies:
            made.wait_send()
        for b in range(wide):
            slots[b, :, 0:block] = sums[:, b * block : (b + 1) * block]
        last = []
        for dx in (0, 1):
            for k in range(depth):
                if k or dx:
                    to = dx * depth + k
                    at = dx * depth + (depth - k) % depth
                    made = remote(
                        slots.at[to], last_norm.at[at], gs.at[at], gr.at[at], place.far(k, dx)
                    )
                    made.start()
                    last.append(made)
                    made = remote(
                        head_sums,
                        last_head.at[at],
                        gs.at[wide + at],
                        gr.at[wide + at],
                        place.far(k, dx),
                    )
                    made.start()
                    last.append(made)
        home_step(3, 3)
        finals(3)
        finals(1)
        home_step(0, 3)
        finals(0)
        for made in grads + written:
            made.wait()
        for made in last:
            made.wait_recv()
        norm_total = slots[0]
        head_total = head_sums[...]
        for b in range(1, wide):
            norm_total = norm_total + last_norm[b]
            head_total = head_total + last_head[b]
        o_norm[...] = norm_total
        o_head[...] = head_total
        for made in last:
            made.wait_send()

    def back(qkv_grad):
        pl.run_scoped(
            functools.partial(attention_back, qkv_grad),
            pltpu.VMEM((span, qkv_width), f32),
            pltpu.VMEM((span, HD), bf16),
            pltpu.VMEM((span, HD), bf16),
            pltpu.VMEM((span, out_width), bf16),
            pltpu.VMEM((span, HD), f32),
            pltpu.VMEM((span, HD), f32),
        )
        pl.run_scoped(
            functools.partial(finish_back, qkv_grad),
            pltpu.VMEM((span, width), bf16),
            pltpu.VMEM(((depth - 1) * block, max(widths)), bf16),
            pltpu.VMEM((block, max(widths)), bf16),
            pltpu.VMEM((block, max(widths)), f32),
            pltpu.VMEM((max(widths), block), f32),
        )

    pl.run_scoped(back, pltpu.VMEM((span, qkv_width), bf16))
    for g in range(5):
        for t in range(steps):
            cross(g, t).wait_send()
        for k in range(1, depth):
            hand_over(g, k).wait_send()
    side.drain()
    ag.drain()


def layer_call(lengths, norm_gains, head_gains, x, dy, weights, heads, pairs):
    wide = lax.axis_size("wide")
    depth = wide // 2
    size, width = x.shape
    span = 4 * size
    block = width // wide
    inside = block % HD == 0
    ff = weights[3].shape[-1]
    widths = [(heads + 2 * pairs) * HD, heads * HD, ff, ff, ff]
    lanes = max(HD, block)
    shape = jax.ShapeDtypeStruct
    anywhere = pl.BlockSpec(memory_space=pl.ANY)
    vmem = pl.BlockSpec(memory_space=pltpu.VMEM)
    smem = pl.BlockSpec(memory_space=pltpu.SMEM)
    count = len(chunks_of(widths))
    cosine, sine = rope_tables(span)
    outs = [
        shape((8, lanes), f32),
        shape((8, HD), f32),
        shape((size, width), bf16),
        shape((size, width), f32),
        shape((block, heads * HD), f32),
        shape((2, block, pairs * HD), f32),
        shape((heads * HD, block), f32),
        shape((2, block, ff), f32),
        shape((ff, block), f32),
    ]
    outs += [shape((width // 2, w), bf16) for w in widths]
    outs += [shape(((depth - 1) * block, w), bf16) for w in widths]
    outs += [shape((width, w), bf16) for w in widths]
    outs += [shape((width // 2, w), bf16) for w in widths] * 2
    outs += [shape((block, w), bf16) for w in widths]
    outs += [shape((block, w), bf16) for w in widths[3:]]
    outs += [
        shape((span, width), bf16),
        shape((span, width), bf16),
        shape((span, widths[0]), f32),
        shape((span, width), bf16),
    ]
    dma = pltpu.SemaphoreType.DMA
    if not inside:
        query, keyval, output, gateup, down = [w.astype(bf16) for w in weights]
        weights = [
            jnp.concatenate([query, keyval[0], keyval[1]], axis=1),
            output.T,
            gateup[0],
            gateup[1],
            down.T,
        ]
        owner, place = owners(wide), places(wide)
        x, dy = reorder(x, owner), reorder(dy, owner)
    results = pl.pallas_call(
        functools.partial(layer_kernel, wide, heads, pairs),
        out_shape=outs,
        in_specs=[smem] + [vmem] * 4 + [anywhere] * 7,
        out_specs=[vmem] * 2 + [anywhere] * (len(outs) - 2),
        scratch_shapes=[
            pltpu.VMEM((size, width), bf16),
            pltpu.VMEM((size, width), f32),
            pltpu.VMEM((8, lanes), f32),
            pltpu.VMEM((wide, 8, lanes), f32),
            pltpu.VMEM((8, width), f32),
            pltpu.VMEM((8, HD), f32),
            pltpu.VMEM((span, widths[1]), bf16),
            pltpu.VMEM((size, width), f32),
            pltpu.VMEM((size, width), f32),
            pltpu.VMEM((span, width), bf16),
            pltpu.VMEM((span, ff), bf16),
            pltpu.VMEM((width, ff), bf16),
            pltpu.VMEM((span, width), bf16),
            pltpu.VMEM((span, 2 * ff), bf16),
            pltpu.VMEM((2, max(block, HD), max(widths)), bf16),
            pltpu.VMEM((max(block, HD), max(widths)), bf16),
            pltpu.VMEM((2 * size, width), bf16),
            pltpu.VMEM((2 * size, width), bf16),
            pltpu.VMEM((size, width), bf16),
            pltpu.VMEM((size, width), bf16),
            pltpu.VMEM((8, width), f32),
            pltpu.VMEM((2, 8, width), f32),
            pltpu.VMEM((8, HD), f32),
            pltpu.VMEM((2, 8, HD), f32),
            pltpu.VMEM((wide, 8, lanes), f32),
            pltpu.VMEM((wide, 8, HD), f32),
            dma((count, 2 * depth)),
            dma((count, depth)),
            dma((count, depth)),
            dma((count, depth)),
            dma((40,)),
            dma((40,)),
            dma((2 * wide,)),
            dma((2 * wide,)),
            dma((160,)),
            dma((5, depth)),
            dma((5, depth + 1)),
            dma((5, depth)),
            dma((5, depth)),
            dma((2,)),
            dma,
            pltpu.SemaphoreType.REGULAR,
            pltpu.SemaphoreType.REGULAR,
        ],
        compiler_params=pltpu.CompilerParams(
            collective_id=0, has_side_effects=True, vmem_limit_bytes=63 * MIB
        ),
    )(lengths, norm_gains, head_gains, cosine, sine, x, dy, *weights)
    results = list(results[:9])
    if not inside:
        results[2] = reorder(results[2], place)
        results[3] = reorder(results[3], place)
    return results


def per_device(
    layer_input,
    out_grad,
    lengths,
    query_weight,
    query_mean,
    query_square,
    keyval_weight,
    keyval_mean,
    keyval_square,
    output_weight,
    output_mean,
    output_square,
    gateup_weight,
    gateup_mean,
    gateup_square,
    down_weight,
    down_mean,
    down_square,
    norm_gains,
    norm_mean,
    norm_square,
    head_gains,
    head_mean,
    head_square,
):
    wide = lax.axis_size("wide")
    w = lax.axis_index("wide")
    block = layer_input.shape[2] // wide
    heads = query_weight.shape[1] // HD
    pairs = keyval_weight.shape[2] // HD
    weights = [query_weight, keyval_weight, output_weight, gateup_weight, down_weight]
    results = layer_call(
        lengths, norm_gains, head_gains, layer_input[0], out_grad[0], weights, heads, pairs
    )
    norm_total = results[0][0:2, 0:block]
    part = HD // wide
    head_total = lax.dynamic_slice(results[1], (0, w * part), (2, part))
    layer_out, input_grad = results[2][None], results[3][None]
    query_total, keyval_total, output_total, gateup_total, down_total = results[4:]
    query = adamw(query_weight, query_mean, query_square, query_total, 0.04)
    keyval = adamw(keyval_weight, keyval_mean, keyval_square, keyval_total, 0.04)
    output = adamw(output_weight, output_mean, output_square, output_total, 0.3)
    gateup = adamw(gateup_weight, gateup_mean, gateup_square, gateup_total, 0.04)
    down = adamw(down_weight, down_mean, down_square, down_total, 0.025)
    norm = adamw(norm_gains, norm_mean, norm_square, norm_total, 0.4)
    head = adamw(head_gains, head_mean, head_square, head_total, 0.4)
    return (layer_out, input_grad, *query, *keyval, *output, *gateup, *down, *norm, *head)


def solution(mesh):
    tokens = P("wide", "narrow", None)
    down = [P("wide", "narrow")] * 3
    pair = [P(None, "wide", "narrow")] * 3
    across = [P("narrow", "wide")] * 3
    gain = [P(None, "wide")] * 3
    weights = down + pair + across + pair + across + gain + gain
    return jax.shard_map(
        per_device,
        mesh=mesh,
        in_specs=(tokens, tokens, P("wide"), *weights),
        out_specs=(tokens, tokens, *weights),
        check_vma=False,
    )
```

```python
import functools

import jax
import jax.numpy as jnp
import numpy as np
from jax import lax
from jax.experimental import pallas as pl
from jax.experimental.pallas import tpu as pltpu
from jax.sharding import PartitionSpec as P

HD = 128
STEP = 5
MESH = pl.DeviceIdType.MESH
MIB = 2**20

norm_eps = 1e-06
rope_base = 1000000.0
beta_first = 0.5
beta_second = 0.5
adam_eps = 1e-08
weight_decay = 0.1
masked_fill = -1e30
f32 = jnp.float32
bf16 = jnp.bfloat16


def row_scale(values):
    return lax.rsqrt(jnp.mean(values * values, axis=-1, keepdims=True) + norm_eps)


def norm_back(grad, unit, scale, gain):
    scaled = grad * gain
    return scale * (scaled - unit * jnp.mean(scaled * unit, axis=-1, keepdims=True))


def adamw(weight, first, second, grad, rate):
    first_new = beta_first * first + (1.0 - beta_first) * grad
    second_new = beta_second * second + (1.0 - beta_second) * grad * grad
    first_hat = first_new / (1.0 - beta_first**STEP)
    second_hat = second_new / (1.0 - beta_second**STEP)
    weight_new = weight - rate * (
        first_hat / (jnp.sqrt(second_hat) + adam_eps) + weight_decay * weight
    )
    return (weight_new, first_new, second_new)


def rope_tables(length):
    half = HD // 2
    freqs = rope_base ** (-(np.arange(half, dtype=np.float32) * np.float32(2.0)) / np.float32(HD))
    angles = np.arange(length, dtype=np.float32)[:, None] * freqs.astype(np.float32)[None, :]
    cosine = np.cos(angles.astype(np.float64)).astype(np.float32)
    sine = np.sin(angles.astype(np.float64)).astype(np.float32)
    return (
        jnp.asarray(np.concatenate([cosine, cosine], axis=-1)),
        jnp.asarray(np.concatenate([-sine, sine], axis=-1)),
    )


def dot_nn(left, right):
    return lax.dot_general(left, right, (((1,), (0,)), ((), ())), preferred_element_type=f32)


def dot_nt(left, right):
    return lax.dot_general(left, right, (((1,), (1,)), ((), ())), preferred_element_type=f32)


def dot_tn(left, right):
    return lax.dot_general(left, right, (((0,), (0,)), ((), ())), preferred_element_type=f32)


def loop(count, step):
    def body(index, carry):
        step(index)
        return carry

    lax.fori_loop(0, count, body, 0)


def rows(index, size):
    return pl.ds(pl.multiple_of(index * size, size), size)


class Place:
    def __init__(self, wide, narrow):
        self.depth = wide // 2
        w = lax.axis_index("wide")
        n = lax.axis_index("narrow")
        self.w, self.n = w, n
        self.z = w // 2
        self.x = w - 2 * self.z
        self.y = n // 2
        self.c = n - 2 * self.y
        self.known = {(k, dx): self.reach(k, dx) for k in range(self.depth) for dx in (0, 1)}
        self.sides = {}
        for dy in (0, 1):
            for dc in (0, 1):
                y = self.y if dy == 0 else 1 - self.y
                c = self.c if dc == 0 else 1 - self.c
                self.sides[dy, dc] = (w, y * 2 + c)

    def reach(self, k, dx):
        x = self.x if dx == 0 else 1 - self.x
        return (lax.rem(self.z + k, self.depth) * 2 + x, self.n)

    def far(self, k, dx):
        return self.known[k, dx] if isinstance(k, int) else self.reach(k, dx)

    def side(self, dy, dc):
        return self.sides[dy, dc]

    def slot(self, block):
        ay, ac = block // 2, block % 2
        dy = lax.rem(self.y + ay, 2)
        dc = lax.rem(self.c + ac, 2)
        return dc * 2 + dy


def remote(src, dst, send, recv, device):
    return pltpu.make_async_remote_copy(
        src_ref=src,
        dst_ref=dst,
        send_sem=send,
        recv_sem=recv,
        device_id=device,
        device_id_type=MESH,
    )


class Side:
    def __init__(self, place, send, recv):
        self.place = place
        self.send = [send.at[i] for i in range(send.shape[0])]
        self.recv = [recv.at[i] for i in range(recv.shape[0])]
        self.used = 0
        self.sent = []

    def copy(self, src, dst, dy, dc):
        i = self.used
        self.used += 1
        made = remote(src, dst, self.send[i], self.recv[i], self.place.side(dy, dc))
        made.start()
        self.sent.append(made)
        return made

    def drain(self):
        for made in self.sent:
            made.wait_send()
        self.sent = []


class Gather:
    def __init__(self, side, own, buf, size):
        self.side, self.buf, self.size = side, buf, size
        self.across = side.copy(own, buf.at[pl.ds(size, size)], 1, 0)
        self.core = side.copy(own, buf.at[pl.ds(2 * size, size)], 0, 1)

    def forward(self):
        size = self.size
        self.across.wait_recv()
        self.last = self.side.copy(
            self.buf.at[pl.ds(size, size)], self.buf.at[pl.ds(3 * size, size)], 0, 1
        )

    def done(self):
        self.core.wait_recv()
        self.last.wait_recv()


class Wide:
    def __init__(self, place, block, chunks, full, zs, zr, xs, xr):
        self.place, self.block, self.chunks, self.full = place, block, chunks, full
        self.zs, self.zr, self.xs, self.xr = zs, zr, xs, xr
        self.near = place.depth == 4
        self.odd = place.z - 2 * (place.z // 2)

    def shared(self, i):
        return self.near and i == 3

    def early(self, i):
        return self.near and i == 8

    def pass_on(self, i, k):
        depth = self.place.depth
        return remote(
            self.slot(i, depth),
            self.slot(i, depth + k),
            self.xs.at[i, k],
            self.xr.at[i, k],
            self.place.far(depth - k, 0),
        )

    def beside(self, i):
        g, a, b = self.chunks[i]
        at = (self.place.depth + 3 - 2 * self.odd) * self.block
        return remote(
            self.slot(i, self.place.depth),
            self.full[g].at[pl.ds(pl.multiple_of(at, self.block), self.block), pl.ds(a, b - a)],
            self.xs.at[i, 1 + 2 * self.odd],
            self.xr.at[i, 3 - 2 * self.odd],
            self.place.far(1 + 2 * self.odd, 0),
        )

    def slot(self, i, index):
        g, a, b = self.chunks[i]
        return self.full[g].at[pl.ds(index * self.block, self.block), pl.ds(a, b - a)]

    def along(self, i, k):
        depth = self.place.depth
        return remote(
            self.slot(i, 0),
            self.slot(i, k),
            self.zs.at[i, k],
            self.zr.at[i, k],
            self.place.far(depth - k, 0),
        )

    def beyond(self, i, k):
        depth = self.place.depth
        return remote(
            self.slot(i, 2),
            self.slot(i, k),
            self.zs.at[i, depth + k],
            self.zr.at[i, k],
            self.place.far(1 if k == 1 else depth - 1, 0),
        )

    def across(self, i, k):
        depth = self.place.depth
        return remote(
            self.slot(i, k),
            self.slot(i, depth + k),
            self.xs.at[i, k],
            self.xr.at[i, k],
            self.place.far(0, 1),
        )

    def each(self, i, k, act):
        place = self.place
        if self.near and k in (1, 3):
            at_end = (place.z == 0) if k == 1 else (place.z == 3)

            @pl.when(jnp.logical_not(at_end))
            def _():
                act(self.along(i, k))
        else:
            act(self.along(i, k))

    def order(self):
        depth = self.place.depth
        return (2, 1, 3) if self.near else tuple(range(1, depth))

    def issue(self, i):
        if i >= len(self.chunks):
            return
        self.across(i, 0).start()
        for k in self.order():
            self.each(i, k, lambda made: made.start())

    def hand_on(self, i):
        z = self.place.z
        if self.early(i):
            self.across(i, 0).wait_recv()
            for k in self.order():
                self.pass_on(i, k).start()
        for k in self.order():
            self.along(i, k).wait_recv()
            if self.near and k == 2:

                @pl.when(z == 2)
                def _():
                    self.beyond(i, 1).start()

                @pl.when(z == 1)
                def _():
                    self.beyond(i, 3).start()

            if self.early(i):
                continue
            if self.shared(i) and k in (1, 3):

                @pl.when(self.odd == (1 if k == 1 else 0))
                def _():
                    self.across(i, k).start()
            else:
                self.across(i, k).start()
        if self.shared(i):
            self.across(i, 0).wait_recv()
            self.beside(i).start()

    def arrived(self, i):
        for k in range(self.place.depth):
            if k or not (self.shared(i) or self.early(i)):
                self.across(i, k).wait_recv()

    def drain(self):
        z = self.place.z
        for i in range(len(self.chunks)):
            for k in range(self.place.depth):
                if k:
                    self.each(i, k, lambda made: made.wait_send())
                if self.near and k in (1, 3):

                    @pl.when(z == (2 if k == 1 else 1))
                    def _():
                        self.beyond(i, k).wait_send()

                self.across(i, k).wait_send()


def greet(place):
    depth = place.depth
    peers = [place.far(k, dx) for dx in (0, 1) for k in range(depth) if k or dx]
    peers += [place.side(1, 0), place.side(0, 1)]
    barrier = pltpu.get_barrier_semaphore()
    for peer in peers:
        pl.semaphore_signal(barrier, inc=1, device_id=peer, device_id_type=MESH)
    pl.semaphore_wait(barrier, len(peers))


def turn(values):
    return pltpu.roll(values, HD // 2, 1)


def rope(values, cosine, sine):
    return values * cosine + turn(values) * sine


def rope_back(grads, cosine, sine):
    return grads * cosine - turn(grads) * sine


def softmax_block(query, keys, block, size, count, length):
    scores = dot_nt(query, keys) * HD ** (-0.5)
    shape = scores.shape
    at = block * size + lax.broadcasted_iota(jnp.int32, shape, 0)
    to = lax.broadcasted_iota(jnp.int32, shape, 1)
    scores = jnp.where((to <= at) & (to < length), scores, masked_fill)
    lifted = jnp.exp(scores - jnp.max(scores, axis=-1, keepdims=True))
    return lifted / jnp.sum(lifted, axis=-1, keepdims=True)


def chunks_of(widths):
    qkv, out, gate, up, down = widths
    return [
        (0, 0, qkv // 2),
        (0, qkv // 2, qkv),
        (1, 0, out),
        (2, 0, gate // 2),
        (3, 0, up // 2),
        (2, gate // 2, gate),
        (3, up // 2, up),
        (4, 0, down // 2),
        (4, down // 2, down),
    ]


def owners(wide):
    depth = wide // 2
    w = lax.axis_index("wide")
    z, x = w // 2, w % 2
    return [
        ((z + k) % depth) * 2 + (x if dx == 0 else 1 - x) for dx in (0, 1) for k in range(depth)
    ]


def places(wide):
    depth = wide // 2
    w = lax.axis_index("wide")
    z, x = w // 2, w % 2
    return [
        jnp.where(x == o % 2, 0, depth) + (o // 2 - z) % depth for o in range(wide)
    ]


def reorder(values, order):
    block = values.shape[-1] // len(order)
    return jnp.concatenate(
        [lax.dynamic_slice_in_dim(values, at * block, block, axis=-1) for at in order], axis=-1
    )


def layer_kernel(
    wide,
    heads,
    pairs,
    length_ref,
    norm_ref,
    head_ref,
    cos_ref,
    sin_ref,
    x_in,
    dy_in,
    w_query,
    w_keyval,
    w_output,
    w_gateup,
    w_down,
    o_norm,
    o_head,
    o_out,
    o_grad,
    o_query,
    o_keyval,
    o_output,
    o_gateup,
    o_down,
    home_qkv,
    home_out,
    home_gate,
    home_up,
    home_down,
    come_qkv,
    come_out,
    come_gate,
    come_up,
    come_down,
    full_qkv,
    full_out,
    full_gate,
    full_up,
    full_down,
    away_qkv,
    away_out,
    away_gate,
    away_up,
    away_down,
    got_qkv,
    got_out,
    got_gate,
    got_up,
    got_down,
    relay_qkv,
    relay_out,
    relay_gate,
    relay_up,
    relay_down,
    aside,
    all_dyb,
    all_normed,
    all_qkv,
    all_dresb,
    dyb_ref,
    grad_own,
    gain_ref,
    slots,
    gains,
    head_gain,
    ctx,
    resid,
    total,
    mixed,
    hidden,
    weights,
    tokens,
    feed_grad,
    stage,
    arrived_tile,
    half_out,
    half_in,
    cross_out,
    cross_in,
    sums,
    sums_in,
    head_sums,
    head_sums_in,
    last_norm,
    last_head,
    zs,
    zr,
    xs,
    xr,
    ns,
    nr,
    gs,
    gr,
    ls,
    rxs,
    rxr,
    rzs,
    rzr,
    stage_sem,
    tile_sem,
    come_sem,
    free_core,
    free_other,
):
    place = Place(wide, 4)
    depth = place.depth
    size, width = x_in.shape
    block = width // wide
    inside = block % HD == 0
    ff = hidden.shape[1]
    groups = heads // pairs
    span = 4 * size
    full = [full_qkv, full_out, full_gate, full_up, full_down]
    away = [away_qkv, away_out, away_gate, away_up, away_down]
    got = [got_qkv, got_out, got_gate, got_up, got_down]
    home = [home_qkv, home_out, home_gate, home_up, home_down]
    come = [come_qkv, come_out, come_gate, come_up, come_down]
    relay = [relay_qkv, relay_out, relay_gate, relay_up, relay_down]
    widths = [ref.shape[1] for ref in full]
    qkv_width, out_width = widths[0], widths[1]
    chunks = chunks_of(widths)
    ag = Wide(place, block, chunks, full, zs, zr, xs, xr)
    side = Side(place, ns, nr)
    copies = []
    quarter = size // 4

    def keep(src, dst):
        made = pltpu.make_async_copy(src, dst, ls.at[len(copies)])
        made.start()
        copies.append(made)
        return made

    def fetch(*pairs_of):
        made = [keep(src, dst) for src, dst in pairs_of]
        for one in made:
            one.wait()

    def in_order(ref, buf, out=False):
        if not inside:
            return [keep(buf, ref) if out else keep(ref, buf)]
        made = []
        for b in range(wide):
            w, _ = place.far(b % depth, b // depth)
            there = ref.at[:, pl.ds(pl.multiple_of(w * block, block), block)]
            here = buf.at[:, pl.ds(b * block, block)]
            made.append(keep(here, there) if out else keep(there, here))
        return made

    def land(g, buf):
        if not inside:
            return [keep([w_query, w_keyval, w_output, w_gateup, w_down][g], full[g].at[0:block])]
        if g == 0:
            at, made = 0, []
            for ref in (w_query, w_keyval.at[0], w_keyval.at[1]):
                made.append(keep(ref, buf.at[:, pl.ds(at, ref.shape[1])]))
                at += ref.shape[1]
            return made
        if g in (2, 3):
            return [keep(w_gateup.at[g - 2], buf.at[:, pl.ds(0, widths[g])])]
        ref = w_output if g == 1 else w_down
        return [
            keep(ref.at[pl.ds(i * block, block)], buf.at[:, pl.ds(i * block, block)])
            for i in range(widths[g] // block)
        ]

    def settle(g, buf, made):
        for one in made:
            one.wait()
        if not inside:
            return
        slot = g % 2
        if g in (1, 4):
            for i in range(widths[g] // block):
                at = pl.ds(i * block, block)
                stage[slot, :, at] = buf[:, at].T.astype(bf16)
        else:

            def cast(i):
                at = rows(i, block // 4)
                stage[slot, at, pl.ds(0, widths[g])] = buf[at, 0 : widths[g]].astype(bf16)

            loop(4, cast)
        fetch((stage.at[slot, :, pl.ds(0, widths[g])], full[g].at[pl.ds(0, block)]))

    waiting = []

    def flush():
        while waiting:
            waiting.pop(0)()

    landing = land(0, total)
    x_copies = in_order(x_in, tokens.at[pl.ds(0, size)])
    landing_out = land(1, resid)
    dy_copies = in_order(dy_in, dyb_ref)

    part = head_ref.shape[1]
    gain_ref[...] = jnp.zeros_like(gain_ref)
    gain_ref[0:2, 0:part] = head_ref[...]
    spread = pltpu.roll(gain_ref[:, 0:HD], place.w * part, 1)
    gain_ref[:, 0:HD] = pltpu.roll(spread, 2, 0)
    gain_ref[0:2, 0:block] = norm_ref[...]
    gain_ref[...] = gain_ref[...].astype(bf16).astype(f32)
    greet(place)

    gain_copies = []
    for dx in (0, 1):
        for k in range(depth):
            if k or dx:
                at = dx * depth + (depth - k) % depth
                made = remote(gain_ref, slots.at[at], gs.at[at], gr.at[at], place.far(k, dx))
                made.start()
                gain_copies.append(made)
    settle(0, total, landing)
    ag.issue(0)
    ag.issue(1)
    landing = land(2, total)
    settle(1, resid, landing_out)
    ag.issue(2)
    landing_up = land(3, resid)
    window = 3

    def hand(i):
        flush()
        ag.hand_on(i)
        ag.issue(i + window)

    settle(2, total, landing)
    landing = land(4, total)
    settle(3, resid, landing_up)
    slots[0] = gain_ref[...]
    for made in gain_copies:
        made.wait_recv()
    gains[...] = jnp.concatenate([slots[b][:, :block] for b in range(wide)], axis=1)
    heads_row = slots[0][:, :HD]
    for b in range(1, wide):
        heads_row = heads_row + slots[b][:, :HD]
    head_gain[...] = heads_row
    for made in x_copies:
        made.wait()

    def first_norm(i):
        at = rows(i, quarter)
        x = tokens[at, :].astype(f32)
        cross_out[at, :] = (x * row_scale(x) * gains[0:1, :]).astype(bf16)

    loop(4, first_norm)
    take_normed = Gather(side, cross_out, all_normed, size)
    normed_copy = keep(cross_out, all_normed.at[pl.ds(0, size)])
    settle(4, total, landing)
    hand(0)
    length = length_ref[0]
    for made in dy_copies:
        made.wait()

    def mask(i):
        at = rows(i, quarter)
        value = dyb_ref[at, :].astype(f32)
        where = place.n * size + i * quarter + lax.broadcasted_iota(jnp.int32, value.shape, 0)
        dyb_ref[at, :] = jnp.where(where < length, value, 0.0).astype(bf16)

    loop(4, mask)
    take_dyb = Gather(side, dyb_ref, all_dyb, size)
    dyb_copy = keep(dyb_ref, all_dyb.at[pl.ds(0, size)])
    hand(1)
    take_normed.forward()
    take_dyb.forward()
    hand(2)
    take_dyb.done()
    dyb_copy.wait()
    take_normed.done()
    normed_copy.wait()
    ag.arrived(0)
    ag.arrived(1)

    def keys_of(p, qkv, k_act, v_act):
        for a in range(4):
            at = rows(place.slot(a), size)
            to = pl.ds(a * size, size)
            raw = qkv[at, pl.ds(pl.multiple_of((heads + p) * HD, HD), HD)]
            unit = raw * row_scale(raw) * head_gain[3:4, :]
            k_act[to, :] = rope(unit, cos_ref[to, :], sin_ref[to, :]).astype(bf16)
            v_act[to, :] = qkv[
                at, pl.ds(pl.multiple_of((heads + pairs + p) * HD, HD), HD)
            ].astype(bf16)

    def attention(normed, qkv, k_act, v_act):
        fetch((all_normed, normed), (full_qkv, weights.at[:, pl.ds(0, qkv_width)]))

        def project(m):
            for n in range(qkv_width // 512):
                qkv[rows(m, size), pl.ds(n * 512, 512)] = dot_nn(
                    normed[rows(m, size), :], weights[:, pl.ds(n * 512, 512)]
                )

        loop(4, project)
        qkv_copy = keep(qkv, all_qkv)

        def pair(p):
            keys_of(p, qkv, k_act, v_act)

            def head(g):
                column = pl.ds(pl.multiple_of((p * groups + g) * HD, HD), HD)
                for a in range(4):
                    at = rows(place.slot(a), size)
                    to = pl.ds(a * size, size)
                    raw = qkv[at, column]
                    unit = raw * row_scale(raw) * head_gain[2:3, :]
                    query = rope(unit, cos_ref[to, :], sin_ref[to, :]).astype(bf16)
                    last = (a + 1) * size
                    probs = softmax_block(query, k_act[0:last, :], a, size, last, length)
                    ctx[at, column] = dot_nn(probs.astype(bf16), v_act[0:last, :]).astype(bf16)

            loop(groups, head)

        hand(3)
        for p in range(pairs):
            pair(p)
        qkv_copy.wait()

    pl.run_scoped(
        attention,
        pltpu.VMEM((span, width), bf16),
        pltpu.VMEM((span, qkv_width), f32),
        pltpu.VMEM((span, HD), bf16),
        pltpu.VMEM((span, HD), bf16),
    )
    ag.arrived(2)
    fetch((full_out, weights.at[:, pl.ds(0, out_width)]))
    step = 512

    class Scatter:
        def __init__(self, tile):
            self.tile = tile

        def half(self):
            flush()

            def one(n):
                half_out[:, rows(n, step)] = self.tile(2 * size, 2 * size, n).astype(bf16)

            loop(width // step, one)
            self.core = side.copy(half_out, half_in, 0, 1)

        def own(self):
            flush()

            def one(n):
                total[:, rows(n, step)] = self.tile(0, size, n)

            loop(width // step, one)

        def rest(self):
            flush()
            self.core.wait_recv()
            side.drain()

            def one(n):
                at = rows(n, step)
                part = self.tile(size, size, n) + half_in[pl.ds(size, size), at].astype(f32)
                cross_out[:, at] = part.astype(bf16)

            loop(width // step, one)
            self.other = side.copy(cross_out, cross_in, 1, 0)

            def add(i):
                at = rows(i, quarter)
                total[at, :] += half_in[at, :].astype(f32)

            loop(4, add)

        def done(self):
            flush()
            self.other.wait_recv()

    def out_tile(start, count, n):
        return dot_nt(ctx[pl.ds(start, count), :], weights[rows(n, step), pl.ds(0, out_width)])

    summed_out = Scatter(out_tile)
    summed_out.half()
    summed_out.own()
    hand(4)
    hand(5)
    summed_out.rest()
    summed_out.done()

    def second_norm(i):
        at = rows(i, quarter)
        value = tokens[at, :].astype(f32) + total[at, :] + cross_in[at, :].astype(f32)
        resid[at, :] = value
        mixed[at, :] = (value * row_scale(value) * gains[1:2, :]).astype(bf16)

    loop(4, second_norm)
    take_mixed = Gather(side, mixed.at[pl.ds(0, size)], mixed, size)
    hand(6)
    take_mixed.forward()
    take_mixed.done()
    hand(7)
    half = ff // 2
    tile = 256

    piece = max(block, HD)
    steps = depth * block // piece
    held = piece // block

    def staged(g, slot, to):
        return pltpu.make_async_copy(
            stage.at[slot, :, pl.ds(0, full[g].shape[1])], to, stage_sem.at[slot]
        )

    def part_of(ref, t):
        return ref.at[rows(t, piece)]

    def cross(g, t):
        return remote(
            part_of(away[g], t), part_of(got[g], t), rxs.at[g, t], rxr.at[g, t], place.far(0, 1)
        )

    def hand_over(g, k):
        return remote(
            home[g].at[rows(k, block)],
            come[g].at[rows(k - 1, block)],
            rzs.at[g, k],
            rzr.at[g, k],
            place.far(k, 0),
        )

    beside, beyond = 1 + 2 * ag.odd, 3 - 2 * ag.odd

    def lean_over(g):
        return remote(
            part_of(away[g], beside),
            aside,
            rxs.at[g, beside],
            rxr.at[g, depth],
            place.far(beside, 0),
        )

    def relay_over(g):
        return remote(
            part_of(home[g], beyond),
            relay[g],
            rzs.at[g, beyond],
            rzr.at[g, 0],
            place.far(depth - beyond, 0),
        )

    def add_to_stage(g, slot, src, made):
        wide_g = widths[g]
        made.wait_recv()
        more = pltpu.make_async_copy(src, arrived_tile.at[:, pl.ds(0, wide_g)], tile_sem)
        more.start()
        more.wait()
        stage[slot, :, 0:wide_g] = (
            stage[slot, :, 0:wide_g].astype(f32) + arrived_tile[:, 0:wide_g].astype(f32)
        ).astype(bf16)

    operands = {}
    turns = [0]
    gone = {g: 0 for g in range(5)}
    come_home = {g: 0 for g in range(5)}

    def known(t, value):
        return isinstance(t, int) and t == value

    def product(g, t):
        left, right = operands[g]
        return dot_tn(left[:, rows(t, piece)], right())

    def send(g, t, lean=False):
        wide_g = widths[g]
        made = product(g, steps + t)
        flush()
        slot = turns[0] % 2
        turns[0] += 1
        stage[slot, :, 0:wide_g] = made.astype(bf16)
        if lean and known(t, 0):
            add_to_stage(g, slot, aside, lean_over(g))
        staged(g, slot, part_of(away[g], t)).start()

        def finish():
            staged(g, slot, part_of(away[g], t)).wait()
            if lean and t is beside:
                lean_over(g).start()
            else:
                cross(g, t).start()

        waiting.append(finish)

    late = []
    in_stage = []

    def take(g, t, bare=False):
        wide_g = widths[g]
        slot = turns[0] % 2
        turns[0] += 1
        if bare:
            made = product(g, t)
            flush()
            stage[slot, :, 0:wide_g] = made.astype(bf16)
        else:
            if not late:
                flush()
            cross(g, t).wait_recv()
            get = pltpu.make_async_copy(
                part_of(got[g], t), arrived_tile.at[:, pl.ds(0, wide_g)], tile_sem
            )
            get.start()
            made = product(g, t)
            flush()
            get.wait()
            made = made + arrived_tile[:, 0:wide_g].astype(f32)
            stage[slot, :, 0:wide_g] = made.astype(bf16)
        if ag.near and known(t, 2):

            @pl.when((place.z == 1) | (place.z == 2))
            def _():
                add_to_stage(g, slot, relay[g], relay_over(g))

        if ag.near and g == 0 and known(t, 0):
            in_stage.append(slot)
            return
        staged(g, slot, part_of(home[g], t)).start()

        def finish():
            staged(g, slot, part_of(home[g], t)).wait()
            if ag.near:
                if t is beyond:
                    at_end = (place.z == 0) | (place.z == 3)

                    @pl.when(at_end)
                    def _():
                        relay_over(g).start()

                    @pl.when(jnp.logical_not(at_end))
                    def _():
                        hand_over(g, t).start()
                elif not known(t, 0):
                    hand_over(g, t).start()
                return
            for r in range(held):
                if t * held + r:
                    hand_over(g, t * held + r).start()

        waiting.append(finish)

    def away_step(g):
        i = gone[g]
        gone[g] += 1
        if not ag.near:
            for t in range(steps) if i == 0 else ():
                send(g, t)
            return
        lean = g == 4
        send(g, ((beside, beyond, 2, 0) if lean else (beyond, beside, 2, 0))[i], lean)

    def home_step(g, which):
        come_home[g] += 1
        if not ag.near:
            for t in tuple(range(1, steps)) + (0,) if come_home[g] == 4 else ():
                take(g, t)
            return
        lean = g == 4
        order = (beside, beyond, 2, 0) if lean else (beyond, beside, 2, 0)
        take(g, order[which], lean and which == 0)

    tokens_copy = keep(all_dyb, tokens)

    def feed_forward(gate, up):
        def feed(part):
            a = part * half
            fetch(
                (full_gate.at[:, pl.ds(a, half)], weights.at[:, pl.ds(0, half)]),
                (full_up.at[:, pl.ds(a, half)], weights.at[:, pl.ds(half, half)]),
            )

            def columns(n):
                def body(m):
                    at = rows(m, size)
                    left = mixed[at, :]
                    gate_part = dot_nn(left, weights[:, rows(n, tile)])
                    up_part = dot_nn(
                        left, weights[:, pl.ds(pl.multiple_of(half + n * tile, tile), tile)]
                    )
                    to = pl.ds(pl.multiple_of(a + n * tile, tile), tile)
                    gate[at, to] = gate_part
                    up[at, to] = up_part
                    hidden[at, to] = (gate_part * jax.nn.sigmoid(gate_part) * up_part).astype(bf16)

                loop(4, body)

            loop(half // tile, columns)

        ag.arrived(3)
        ag.arrived(4)
        feed(0)
        hand(8)
        ag.arrived(5)
        ag.arrived(6)
        feed(1)
        tokens_copy.wait()
        operands[4] = tokens, lambda: hidden[...]
        away_step(4)
        home_step(4, 0)
        away_step(4)
        away_step(4)
        flush()
        ag.arrived(7)
        ag.arrived(8)
        fetch((full_down, weights))

        def columns(n):
            def body(m):
                at = rows(m, size)
                to = rows(n, tile)
                grad = dot_nn(tokens[at, :], weights[:, to])
                gate_part = gate[at, to]
                up_part = up[at, to]
                sigma = jax.nn.sigmoid(gate_part)
                feed_grad[at, to] = (
                    grad * up_part * sigma * (1.0 + gate_part * (1.0 - sigma))
                ).astype(bf16)
                feed_grad[at, pl.ds(pl.multiple_of(ff + n * tile, tile), tile)] = (
                    grad * gate_part * sigma
                ).astype(bf16)

            loop(4, body)

        loop(ff // tile, columns)

    pl.run_scoped(feed_forward, pltpu.VMEM((span, ff), f32), pltpu.VMEM((span, ff), f32))

    operands[2] = mixed, lambda: feed_grad[:, pl.ds(0, ff)]
    operands[3] = mixed, lambda: feed_grad[:, pl.ds(ff, ff)]
    away_step(3)
    away_step(2)
    away_step(3)
    flush()

    def mixed_grad(both):
        fetch(
            (full_gate, both.at[:, pl.ds(0, ff)]),
            (full_up, both.at[:, pl.ds(ff, ff)]),
        )

        def mixed_tile(start, count, n):
            return dot_nt(feed_grad[pl.ds(start, count), :], both[rows(n, step), :])

        summed.append(Scatter(mixed_tile))
        summed[0].half()
        summed[0].own()
        summed[0].rest()

    summed = []
    pl.run_scoped(mixed_grad, pltpu.VMEM((width, 2 * ff), bf16))
    home_step(4, 1)
    home_step(2, 0)
    home_step(4, 2)
    away_step(2)
    away_step(4)
    away_step(2)
    home_step(3, 1)
    away_step(2)
    summed[0].done()
    sums[...] = jnp.zeros_like(sums)
    head_sums[...] = jnp.zeros_like(head_sums)

    def second_back(i):
        at = rows(i, quarter)
        value = resid[at, :]
        scale = row_scale(value)
        unit = value * scale
        grad = total[at, :] + cross_in[at, :].astype(f32)
        sums[1:2, :] += jnp.sum(grad * unit, axis=0, keepdims=True)
        back = norm_back(grad, unit, scale, gains[1:2, :])
        result = dyb_ref[at, :].astype(f32) + back
        grad_own[at, :] = result
        cross_out[at, :] = result.astype(bf16)

    side.drain()
    loop(4, second_back)
    take_dresb = Gather(side, cross_out, all_dresb, size)
    dresb_copy = keep(cross_out, all_dresb.at[pl.ds(0, size)])
    take_dresb.core.wait_recv()
    away_step(3)

    def down_tile(start, count, n):
        return dot_nt(hidden[pl.ds(start, count), :], weights[rows(n, step), :])

    summed_down = Scatter(down_tile)
    summed_down.half()
    home_step(2, 1)
    summed_down.own()
    home_step(4, 3)
    home_step(3, 0)
    flush()
    take_dresb.forward()
    dresb_copy.wait()
    summed_down.rest()
    pl.semaphore_signal(free_core, inc=1, device_id=place.side(0, 1), device_id_type=MESH)
    take_dresb.last.wait_recv()

    late.append(True)

    def attention_back(qkv_grad, qkv, k_act, v_act, ctx_grad, k_grad, v_grad):
        fetch(
            (all_dresb, tokens),
            (all_qkv, qkv),
            (full_out, weights.at[:, pl.ds(0, out_width)]),
        )

        operands[1] = tokens, lambda: ctx[...]

        def context_grad(m):
            ctx_grad[rows(m, size), :] = dot_nn(
                tokens[rows(m, size), :], weights[:, pl.ds(0, out_width)]
            ).astype(bf16)

        loop(4, context_grad)

        def head_back(raw, grad, gain, a):
            to = pl.ds(a * size, size)
            scale = row_scale(raw)
            unit = raw * scale
            turned = rope_back(grad, cos_ref[to, :], sin_ref[to, :])
            gain_part = jnp.sum(turned * unit, axis=0, keepdims=True)
            return norm_back(turned, unit, scale, gain).astype(bf16), gain_part

        def pair(p):
            keys_of(p, qkv, k_act, v_act)
            k_grad[...] = jnp.zeros_like(k_grad)
            v_grad[...] = jnp.zeros_like(v_grad)

            def head(g):
                column = pl.ds(pl.multiple_of((p * groups + g) * HD, HD), HD)
                for a in range(4):
                    at = rows(place.slot(a), size)
                    to = pl.ds(a * size, size)
                    last = (a + 1) * size
                    raw = qkv[at, column]
                    unit = raw * row_scale(raw) * head_gain[2:3, :]
                    query = rope(unit, cos_ref[to, :], sin_ref[to, :]).astype(bf16)
                    probs = softmax_block(query, k_act[0:last, :], a, size, last, length)
                    grad = ctx_grad[at, column]
                    probs_grad = dot_nt(grad, v_act[0:last, :])
                    v_grad[0:last, :] += dot_tn(probs.astype(bf16), grad)
                    delta = jnp.sum(probs * probs_grad, axis=-1, keepdims=True)
                    scores_grad = (probs * (probs_grad - delta)).astype(bf16)
                    query_grad = dot_nn(scores_grad, k_act[0:last, :]) * HD ** (-0.5)
                    k_grad[0:last, :] += dot_tn(scores_grad, query) * HD ** (-0.5)
                    made, gain_part = head_back(raw, query_grad, head_gain[2:3, :], a)
                    qkv_grad[at, column] = made
                    head_sums[0:1, :] += gain_part

            loop(groups, head)
            for a in range(4):
                at = rows(place.slot(a), size)
                to = pl.ds(a * size, size)
                column = pl.ds(pl.multiple_of((heads + p) * HD, HD), HD)
                made, gain_part = head_back(
                    qkv[at, column], k_grad[to, :], head_gain[3:4, :], a
                )
                qkv_grad[at, column] = made
                head_sums[1:2, :] += gain_part
                column = pl.ds(pl.multiple_of((heads + pairs + p) * HD, HD), HD)
                qkv_grad[at, column] = v_grad[to, :].astype(bf16)

        pair(0)
        home_step(2, 2)
        away_step(1)
        flush()
        summed_down.done()
        side.drain()

        def last_sum(i):
            at = rows(i, quarter)
            value = resid[at, :] + total[at, :] + cross_in[at, :].astype(f32)
            cross_out[at, :] = value.astype(bf16)

        loop(4, last_sum)
        results.extend(in_order(o_out, cross_out, out=True))
        pl.semaphore_signal(free_other, inc=1, device_id=place.side(1, 0), device_id_type=MESH)
        for p in range(1, pairs):
            pair(p)
        for made in results:
            made.wait()

    results = []

    def finish_back(qkv_grad, normed, come_v, home_v, sum_v, sum_t):
        normed_copy = keep(all_normed, normed)
        qkv_copy = keep(full_qkv, weights.at[:, pl.ds(0, qkv_width)])
        operands[0] = normed, lambda: qkv_grad[...]
        normed_copy.wait()
        away_step(0)
        away_step(0)
        away_step(1)
        flush()
        qkv_copy.wait()
        written = []

        def finals(g):
            flush()
            wide_g = widths[g]
            kept = in_stage if g == 0 else []
            if not kept:
                mine = keep(home[g].at[pl.ds(0, block)], home_v.at[:, pl.ds(0, wide_g)])

            def slot_of(k):
                return pl.ds((k - 1) * block, block)

            def bring(k):
                return pltpu.make_async_copy(
                    come[g].at[slot_of(k)], come_v.at[slot_of(k), pl.ds(0, wide_g)], come_sem.at[k]
                )

            def begin(k):
                hand_over(g, k).wait_recv()
                bring(k).start()

            def none(k):
                come_v[slot_of(k), 0:wide_g] = jnp.zeros((block, wide_g), bf16)

            for act, other in ((begin, none), (lambda k: bring(k).wait(), None)):
                for k in (1, 3, 2) if ag.near else range(1, depth):
                    if ag.near and k in (1, 3):
                        here = place.z != (0 if k == 1 else 3)
                        pl.when(here)(functools.partial(act, k))
                        if other is not None:
                            pl.when(jnp.logical_not(here))(functools.partial(other, k))
                    else:
                        act(k)
            if not kept:
                mine.wait()
            while written:
                written.pop().wait()

            def add(i):
                at = rows(i, block // 4)
                if kept:
                    value = stage[kept[0], at, 0:wide_g].astype(f32)
                else:
                    value = home_v[at, 0:wide_g].astype(f32)
                for k in range(1, depth):
                    more = pl.ds(
                        pl.multiple_of((k - 1) * block + i * (block // 4), block // 4), block // 4
                    )
                    value = value + come_v[more, 0:wide_g].astype(f32)
                sum_v[at, 0:wide_g] = value

            loop(4, add)
            if g in (1, 4):
                for i in range(wide_g // HD):
                    sum_t[pl.ds(i * HD, HD), :] = sum_v[:, i * HD : (i + 1) * HD].T
                ref = o_output if g == 1 else o_down
                written.append(keep(sum_t.at[pl.ds(0, wide_g)], ref))
            elif g == 0:
                ends = (o_query, o_keyval.at[0], o_keyval.at[1])
                columns = (heads * HD, pairs * HD, pairs * HD)
                at = 0
                for ref, count in zip(ends, columns, strict=True):
                    written.append(keep(sum_v.at[:, pl.ds(at, count)], ref))
                    at += count
            else:
                written.append(keep(sum_v.at[:, pl.ds(0, wide_g)], o_gateup.at[g - 2]))

        def normed_tile(start, count, n):
            return dot_nt(
                qkv_grad[pl.ds(start, count), :], weights[rows(n, step), pl.ds(0, qkv_width)]
            )

        summed_normed = Scatter(normed_tile)
        pl.semaphore_wait(free_core, 1)
        summed_normed.half()
        home_step(1, 0)
        summed_normed.own()
        home_step(3, 2)
        pl.semaphore_wait(free_other, 1)
        summed_normed.rest()
        x_again = in_order(x_in, half_out.at[pl.ds(0, size)])
        home_step(2, 3)
        away_step(0)
        away_step(1)
        finals(4)
        away_step(1)
        home_step(0, 1)
        finals(2)
        home_step(1, 1)
        away_step(3)
        home_step(0, 0)
        summed_normed.done()
        for made in x_again:
            made.wait()

        def first_back(i):
            at = rows(i, quarter)
            value = half_out[at, :].astype(f32)
            scale = row_scale(value)
            unit = value * scale
            grad = total[at, :] + cross_in[at, :].astype(f32)
            sums[0:1, :] += jnp.sum(grad * unit, axis=0, keepdims=True)
            grad_own[at, :] += norm_back(grad, unit, scale, gains[0:1, :])

        loop(4, first_back)
        grads = in_order(o_grad, grad_own, out=True)

        def trade(flip, dy, dc):
            return (
                side.copy(sums, sums_in.at[flip], dy, dc),
                side.copy(head_sums, head_sums_in.at[flip], dy, dc),
            )

        def add_trade(flip, made):
            flush()
            for one in made:
                one.wait_recv()
            side.drain()
            sums[...] += sums_in[flip]
            head_sums[...] += head_sums_in[flip]

        made = trade(0, 0, 1)
        home_step(1, 2)
        add_trade(0, made)
        made = trade(1, 1, 0)
        home_step(1, 3)
        away_step(0)
        home_step(0, 2)
        add_trade(1, made)
        for made in gain_copies:
            made.wait_send()
        for b in range(wide):
            slots[b, :, 0:block] = sums[:, b * block : (b + 1) * block]
        last = []
        for dx in (0, 1):
            for k in range(depth):
                if k or dx:
                    to = dx * depth + k
                    at = dx * depth + (depth - k) % depth
                    made = remote(
                        slots.at[to], last_norm.at[at], gs.at[at], gr.at[at], place.far(k, dx)
                    )
                    made.start()
                    last.append(made)
                    made = remote(
                        head_sums,
                        last_head.at[at],
                        gs.at[wide + at],
                        gr.at[wide + at],
                        place.far(k, dx),
                    )
                    made.start()
                    last.append(made)
        home_step(3, 3)
        finals(3)
        finals(1)
        home_step(0, 3)
        finals(0)
        for made in grads + written:
            made.wait()
        for made in last:
            made.wait_recv()
        norm_total = slots[0]
        head_total = head_sums[...]
        for b in range(1, wide):
            norm_total = norm_total + last_norm[b]
            head_total = head_total + last_head[b]
        o_norm[...] = norm_total
        o_head[...] = head_total
        for made in last:
            made.wait_send()

    def back(qkv_grad):
        pl.run_scoped(
            functools.partial(attention_back, qkv_grad),
            pltpu.VMEM((span, qkv_width), f32),
            pltpu.VMEM((span, HD), bf16),
            pltpu.VMEM((span, HD), bf16),
            pltpu.VMEM((span, out_width), bf16),
            pltpu.VMEM((span, HD), f32),
            pltpu.VMEM((span, HD), f32),
        )
        pl.run_scoped(
            functools.partial(finish_back, qkv_grad),
            pltpu.VMEM((span, width), bf16),
            pltpu.VMEM(((depth - 1) * block, max(widths)), bf16),
            pltpu.VMEM((block, max(widths)), bf16),
            pltpu.VMEM((block, max(widths)), f32),
            pltpu.VMEM((max(widths), block), f32),
        )

    pl.run_scoped(back, pltpu.VMEM((span, qkv_width), bf16))
    for g in range(5):
        for t in range(steps):
            cross(g, t).wait_send()
        for k in range(1, depth):
            hand_over(g, k).wait_send()
    side.drain()
    ag.drain()


def layer_call(lengths, norm_gains, head_gains, x, dy, weights, heads, pairs):
    wide = lax.axis_size("wide")
    depth = wide // 2
    size, width = x.shape
    span = 4 * size
    block = width // wide
    inside = block % HD == 0
    ff = weights[3].shape[-1]
    widths = [(heads + 2 * pairs) * HD, heads * HD, ff, ff, ff]
    lanes = max(HD, block)
    shape = jax.ShapeDtypeStruct
    anywhere = pl.BlockSpec(memory_space=pl.ANY)
    vmem = pl.BlockSpec(memory_space=pltpu.VMEM)
    smem = pl.BlockSpec(memory_space=pltpu.SMEM)
    count = len(chunks_of(widths))
    cosine, sine = rope_tables(span)
    outs = [
        shape((8, lanes), f32),
        shape((8, HD), f32),
        shape((size, width), bf16),
        shape((size, width), f32),
        shape((block, heads * HD), f32),
        shape((2, block, pairs * HD), f32),
        shape((heads * HD, block), f32),
        shape((2, block, ff), f32),
        shape((ff, block), f32),
    ]
    outs += [shape((width // 2, w), bf16) for w in widths]
    outs += [shape(((depth - 1) * block, w), bf16) for w in widths]
    outs += [shape((width, w), bf16) for w in widths]
    outs += [shape((width // 2, w), bf16) for w in widths] * 2
    outs += [shape((block, w), bf16) for w in widths]
    outs += [shape((block, ff), bf16)]
    outs += [
        shape((span, width), bf16),
        shape((span, width), bf16),
        shape((span, widths[0]), f32),
        shape((span, width), bf16),
    ]
    dma = pltpu.SemaphoreType.DMA
    if not inside:
        query, keyval, output, gateup, down = [w.astype(bf16) for w in weights]
        weights = [
            jnp.concatenate([query, keyval[0], keyval[1]], axis=1),
            output.T,
            gateup[0],
            gateup[1],
            down.T,
        ]
        owner, place = owners(wide), places(wide)
        x, dy = reorder(x, owner), reorder(dy, owner)
    results = pl.pallas_call(
        functools.partial(layer_kernel, wide, heads, pairs),
        out_shape=outs,
        in_specs=[smem] + [vmem] * 4 + [anywhere] * 7,
        out_specs=[vmem] * 2 + [anywhere] * (len(outs) - 2),
        scratch_shapes=[
            pltpu.VMEM((size, width), bf16),
            pltpu.VMEM((size, width), f32),
            pltpu.VMEM((8, lanes), f32),
            pltpu.VMEM((wide, 8, lanes), f32),
            pltpu.VMEM((8, width), f32),
            pltpu.VMEM((8, HD), f32),
            pltpu.VMEM((span, widths[1]), bf16),
            pltpu.VMEM((size, width), f32),
            pltpu.VMEM((size, width), f32),
            pltpu.VMEM((span, width), bf16),
            pltpu.VMEM((span, ff), bf16),
            pltpu.VMEM((width, ff), bf16),
            pltpu.VMEM((span, width), bf16),
            pltpu.VMEM((span, 2 * ff), bf16),
            pltpu.VMEM((2, max(block, HD), max(widths)), bf16),
            pltpu.VMEM((max(block, HD), max(widths)), bf16),
            pltpu.VMEM((2 * size, width), bf16),
            pltpu.VMEM((2 * size, width), bf16),
            pltpu.VMEM((size, width), bf16),
            pltpu.VMEM((size, width), bf16),
            pltpu.VMEM((8, width), f32),
            pltpu.VMEM((2, 8, width), f32),
            pltpu.VMEM((8, HD), f32),
            pltpu.VMEM((2, 8, HD), f32),
            pltpu.VMEM((wide, 8, lanes), f32),
            pltpu.VMEM((wide, 8, HD), f32),
            dma((count, 2 * depth)),
            dma((count, depth)),
            dma((count, depth)),
            dma((count, depth)),
            dma((40,)),
            dma((40,)),
            dma((2 * wide,)),
            dma((2 * wide,)),
            dma((160,)),
            dma((5, depth)),
            dma((5, depth + 1)),
            dma((5, depth)),
            dma((5, depth)),
            dma((2,)),
            dma,
            dma((depth,)),
            pltpu.SemaphoreType.REGULAR,
            pltpu.SemaphoreType.REGULAR,
        ],
        compiler_params=pltpu.CompilerParams(
            collective_id=0, has_side_effects=True, vmem_limit_bytes=63 * MIB
        ),
    )(lengths, norm_gains, head_gains, cosine, sine, x, dy, *weights)
    results = list(results[:9])
    if not inside:
        results[2] = reorder(results[2], place)
        results[3] = reorder(results[3], place)
    return results


def per_device(
    layer_input,
    out_grad,
    lengths,
    query_weight,
    query_mean,
    query_square,
    keyval_weight,
    keyval_mean,
    keyval_square,
    output_weight,
    output_mean,
    output_square,
    gateup_weight,
    gateup_mean,
    gateup_square,
    down_weight,
    down_mean,
    down_square,
    norm_gains,
    norm_mean,
    norm_square,
    head_gains,
    head_mean,
    head_square,
):
    wide = lax.axis_size("wide")
    w = lax.axis_index("wide")
    block = layer_input.shape[2] // wide
    heads = query_weight.shape[1] // HD
    pairs = keyval_weight.shape[2] // HD
    weights = [query_weight, keyval_weight, output_weight, gateup_weight, down_weight]
    results = layer_call(
        lengths, norm_gains, head_gains, layer_input[0], out_grad[0], weights, heads, pairs
    )
    norm_total = results[0][0:2, 0:block]
    part = HD // wide
    head_total = lax.dynamic_slice(results[1], (0, w * part), (2, part))
    layer_out, input_grad = results[2][None], results[3][None]
    query_total, keyval_total, output_total, gateup_total, down_total = results[4:]
    query = adamw(query_weight, query_mean, query_square, query_total, 0.04)
    keyval = adamw(keyval_weight, keyval_mean, keyval_square, keyval_total, 0.04)
    output = adamw(output_weight, output_mean, output_square, output_total, 0.3)
    gateup = adamw(gateup_weight, gateup_mean, gateup_square, gateup_total, 0.04)
    down = adamw(down_weight, down_mean, down_square, down_total, 0.025)
    norm = adamw(norm_gains, norm_mean, norm_square, norm_total, 0.4)
    head = adamw(head_gains, head_mean, head_square, head_total, 0.4)
    return (layer_out, input_grad, *query, *keyval, *output, *gateup, *down, *norm, *head)


def solution(mesh):
    tokens = P("wide", "narrow", None)
    down = [P("wide", "narrow")] * 3
    pair = [P(None, "wide", "narrow")] * 3
    across = [P("narrow", "wide")] * 3
    gain = [P(None, "wide")] * 3
    weights = down + pair + across + pair + across + gain + gain
    return jax.shard_map(
        per_device,
        mesh=mesh,
        in_specs=(tokens, tokens, P("wide"), *weights),
        out_specs=(tokens, tokens, *weights),
        check_vma=False,
    )
```

```python
import functools

import jax
import jax.numpy as jnp
import numpy as np
from jax import lax
from jax.experimental import pallas as pl
from jax.experimental.pallas import tpu as pltpu
from jax.sharding import PartitionSpec as P

HD = 128
STEP = 5
MESH = pl.DeviceIdType.MESH
MIB = 2**20

norm_eps = 1e-06
rope_base = 1000000.0
beta_first = 0.5
beta_second = 0.5
adam_eps = 1e-08
weight_decay = 0.1
masked_fill = -1e30
f32 = jnp.float32
bf16 = jnp.bfloat16


def row_scale(values):
    return lax.rsqrt(jnp.mean(values * values, axis=-1, keepdims=True) + norm_eps)


def norm_back(grad, unit, scale, gain):
    scaled = grad * gain
    return scale * (scaled - unit * jnp.mean(scaled * unit, axis=-1, keepdims=True))


def adamw(weight, first, second, grad, rate):
    first_new = beta_first * first + (1.0 - beta_first) * grad
    second_new = beta_second * second + (1.0 - beta_second) * grad * grad
    first_hat = first_new / (1.0 - beta_first**STEP)
    second_hat = second_new / (1.0 - beta_second**STEP)
    weight_new = weight - rate * (
        first_hat / (jnp.sqrt(second_hat) + adam_eps) + weight_decay * weight
    )
    return (weight_new, first_new, second_new)


def rope_tables(length):
    half = HD // 2
    freqs = rope_base ** (-(np.arange(half, dtype=np.float32) * np.float32(2.0)) / np.float32(HD))
    angles = np.arange(length, dtype=np.float32)[:, None] * freqs.astype(np.float32)[None, :]
    cosine = np.cos(angles.astype(np.float64)).astype(np.float32)
    sine = np.sin(angles.astype(np.float64)).astype(np.float32)
    return (
        jnp.asarray(np.concatenate([cosine, cosine], axis=-1)),
        jnp.asarray(np.concatenate([-sine, sine], axis=-1)),
    )


def dot_nn(left, right):
    return lax.dot_general(left, right, (((1,), (0,)), ((), ())), preferred_element_type=f32)


def dot_nt(left, right):
    return lax.dot_general(left, right, (((1,), (1,)), ((), ())), preferred_element_type=f32)


def dot_tn(left, right):
    return lax.dot_general(left, right, (((0,), (0,)), ((), ())), preferred_element_type=f32)


def loop(count, step):
    def body(index, carry):
        step(index)
        return carry

    lax.fori_loop(0, count, body, 0)


def rows(index, size):
    return pl.ds(pl.multiple_of(index * size, size), size)


class Place:
    def __init__(self, wide, narrow):
        self.depth = wide // 2
        w = lax.axis_index("wide")
        n = lax.axis_index("narrow")
        self.w, self.n = w, n
        self.z = w // 2
        self.x = w - 2 * self.z
        self.y = n // 2
        self.c = n - 2 * self.y
        self.known = {(k, dx): self.reach(k, dx) for k in range(self.depth) for dx in (0, 1)}
        self.sides = {}
        for dy in (0, 1):
            for dc in (0, 1):
                y = self.y if dy == 0 else 1 - self.y
                c = self.c if dc == 0 else 1 - self.c
                self.sides[dy, dc] = (w, y * 2 + c)

    def reach(self, k, dx):
        x = self.x if dx == 0 else 1 - self.x
        return (lax.rem(self.z + k, self.depth) * 2 + x, self.n)

    def far(self, k, dx):
        return self.known[k, dx] if isinstance(k, int) else self.reach(k, dx)

    def side(self, dy, dc):
        return self.sides[dy, dc]

    def slot(self, block):
        ay, ac = block // 2, block % 2
        dy = lax.rem(self.y + ay, 2)
        dc = lax.rem(self.c + ac, 2)
        return dc * 2 + dy


def remote(src, dst, send, recv, device):
    return pltpu.make_async_remote_copy(
        src_ref=src,
        dst_ref=dst,
        send_sem=send,
        recv_sem=recv,
        device_id=device,
        device_id_type=MESH,
    )


class Side:
    def __init__(self, place, send, recv):
        self.place = place
        self.send = [send.at[i] for i in range(send.shape[0])]
        self.recv = [recv.at[i] for i in range(recv.shape[0])]
        self.used = 0
        self.sent = []

    def copy(self, src, dst, dy, dc):
        i = self.used
        self.used += 1
        made = remote(src, dst, self.send[i], self.recv[i], self.place.side(dy, dc))
        made.start()
        self.sent.append(made)
        return made

    def drain(self):
        for made in self.sent:
            made.wait_send()
        self.sent = []


class Gather:
    def __init__(self, side, own, buf, size):
        self.side, self.buf, self.size = side, buf, size
        self.across = side.copy(own, buf.at[pl.ds(size, size)], 1, 0)
        self.core = side.copy(own, buf.at[pl.ds(2 * size, size)], 0, 1)

    def forward(self):
        size = self.size
        self.across.wait_recv()
        self.last = self.side.copy(
            self.buf.at[pl.ds(size, size)], self.buf.at[pl.ds(3 * size, size)], 0, 1
        )

    def done(self):
        self.core.wait_recv()
        self.last.wait_recv()


class Wide:
    def __init__(self, place, block, chunks, full, zs, zr, xs, xr):
        self.place, self.block, self.chunks, self.full = place, block, chunks, full
        self.zs, self.zr, self.xs, self.xr = zs, zr, xs, xr
        self.near = place.depth == 4
        self.odd = place.z - 2 * (place.z // 2)

    def shared(self, i):
        return self.near and i == 3

    def early(self, i):
        return self.near and i == 8

    def pass_on(self, i, k):
        depth = self.place.depth
        return remote(
            self.slot(i, depth),
            self.slot(i, depth + k),
            self.xs.at[i, k],
            self.xr.at[i, k],
            self.place.far(depth - k, 0),
        )

    def beside(self, i):
        g, a, b = self.chunks[i]
        at = (self.place.depth + 3 - 2 * self.odd) * self.block
        return remote(
            self.slot(i, self.place.depth),
            self.full[g].at[pl.ds(pl.multiple_of(at, self.block), self.block), pl.ds(a, b - a)],
            self.xs.at[i, 1 + 2 * self.odd],
            self.xr.at[i, 3 - 2 * self.odd],
            self.place.far(1 + 2 * self.odd, 0),
        )

    def slot(self, i, index):
        g, a, b = self.chunks[i]
        return self.full[g].at[pl.ds(index * self.block, self.block), pl.ds(a, b - a)]

    def along(self, i, k):
        depth = self.place.depth
        return remote(
            self.slot(i, 0),
            self.slot(i, k),
            self.zs.at[i, k],
            self.zr.at[i, k],
            self.place.far(depth - k, 0),
        )

    def beyond(self, i, k):
        depth = self.place.depth
        return remote(
            self.slot(i, 2),
            self.slot(i, k),
            self.zs.at[i, depth + k],
            self.zr.at[i, k],
            self.place.far(1 if k == 1 else depth - 1, 0),
        )

    def across(self, i, k):
        depth = self.place.depth
        return remote(
            self.slot(i, k),
            self.slot(i, depth + k),
            self.xs.at[i, k],
            self.xr.at[i, k],
            self.place.far(0, 1),
        )

    def each(self, i, k, act):
        place = self.place
        if self.near and k in (1, 3):
            at_end = (place.z == 0) if k == 1 else (place.z == 3)

            @pl.when(jnp.logical_not(at_end))
            def _():
                act(self.along(i, k))
        else:
            act(self.along(i, k))

    def order(self):
        depth = self.place.depth
        return (2, 1, 3) if self.near else tuple(range(1, depth))

    def issue(self, i):
        if i >= len(self.chunks):
            return
        self.across(i, 0).start()
        for k in self.order():
            self.each(i, k, lambda made: made.start())

    def hand_on(self, i):
        z = self.place.z
        if self.early(i):
            self.across(i, 0).wait_recv()
            for k in self.order():
                self.pass_on(i, k).start()
        for k in self.order():
            self.along(i, k).wait_recv()
            if self.near and k == 2:

                @pl.when(z == 2)
                def _():
                    self.beyond(i, 1).start()

                @pl.when(z == 1)
                def _():
                    self.beyond(i, 3).start()

            if self.early(i):
                continue
            if self.shared(i) and k in (1, 3):

                @pl.when(self.odd == (1 if k == 1 else 0))
                def _():
                    self.across(i, k).start()
            else:
                self.across(i, k).start()
        if self.shared(i):
            self.across(i, 0).wait_recv()
            self.beside(i).start()

    def arrived(self, i):
        for k in range(self.place.depth):
            if k or not (self.shared(i) or self.early(i)):
                self.across(i, k).wait_recv()

    def drain(self):
        z = self.place.z
        for i in range(len(self.chunks)):
            for k in range(self.place.depth):
                if k:
                    self.each(i, k, lambda made: made.wait_send())
                if self.near and k in (1, 3):

                    @pl.when(z == (2 if k == 1 else 1))
                    def _():
                        self.beyond(i, k).wait_send()

                self.across(i, k).wait_send()


def peers_of(place):
    depth = place.depth
    peers = [place.far(k, dx) for dx in (0, 1) for k in range(depth) if k or dx]
    return peers + [place.side(1, 0), place.side(0, 1)]


def greet(place):
    barrier = pltpu.get_barrier_semaphore()
    for peer in peers_of(place):
        pl.semaphore_signal(barrier, inc=1, device_id=peer, device_id_type=MESH)


def await_greetings(place):
    pl.semaphore_wait(pltpu.get_barrier_semaphore(), len(peers_of(place)))


def turn(values):
    return pltpu.roll(values, HD // 2, 1)


def rope(values, cosine, sine):
    return values * cosine + turn(values) * sine


def rope_back(grads, cosine, sine):
    return grads * cosine - turn(grads) * sine


def softmax_block(query, keys, block, size, count, length):
    scores = dot_nt(query, keys) * HD ** (-0.5)
    shape = scores.shape
    at = block * size + lax.broadcasted_iota(jnp.int32, shape, 0)
    to = lax.broadcasted_iota(jnp.int32, shape, 1)
    scores = jnp.where((to <= at) & (to < length), scores, masked_fill)
    lifted = jnp.exp(scores - jnp.max(scores, axis=-1, keepdims=True))
    return lifted / jnp.sum(lifted, axis=-1, keepdims=True)


def chunks_of(widths):
    qkv, out, gate, up, down = widths
    return [
        (0, 0, qkv // 2),
        (0, qkv // 2, qkv),
        (1, 0, out),
        (2, 0, gate // 2),
        (3, 0, up // 2),
        (2, gate // 2, gate),
        (3, up // 2, up),
        (4, 0, down // 2),
        (4, down // 2, down),
    ]


def owners(wide):
    depth = wide // 2
    w = lax.axis_index("wide")
    z, x = w // 2, w % 2
    return [
        ((z + k) % depth) * 2 + (x if dx == 0 else 1 - x) for dx in (0, 1) for k in range(depth)
    ]


def places(wide):
    depth = wide // 2
    w = lax.axis_index("wide")
    z, x = w // 2, w % 2
    return [
        jnp.where(x == o % 2, 0, depth) + (o // 2 - z) % depth for o in range(wide)
    ]


def reorder(values, order):
    block = values.shape[-1] // len(order)
    return jnp.concatenate(
        [lax.dynamic_slice_in_dim(values, at * block, block, axis=-1) for at in order], axis=-1
    )


def layer_kernel(
    wide,
    heads,
    pairs,
    length_ref,
    norm_ref,
    head_ref,
    cos_ref,
    sin_ref,
    x_in,
    dy_in,
    w_query,
    w_keyval,
    w_output,
    w_gateup,
    w_down,
    o_norm,
    o_head,
    o_out,
    o_grad,
    o_query,
    o_keyval,
    o_output,
    o_gateup,
    o_down,
    home_qkv,
    home_out,
    home_gate,
    home_up,
    home_down,
    come_qkv,
    come_out,
    come_gate,
    come_up,
    come_down,
    full_qkv,
    full_out,
    full_gate,
    full_up,
    full_down,
    away_qkv,
    away_out,
    away_gate,
    away_up,
    away_down,
    got_qkv,
    got_out,
    got_gate,
    got_up,
    got_down,
    relay_qkv,
    relay_out,
    relay_gate,
    relay_up,
    relay_down,
    aside,
    all_dyb,
    all_normed,
    all_qkv,
    all_dresb,
    dyb_ref,
    grad_own,
    gain_ref,
    slots,
    gains,
    head_gain,
    ctx,
    resid,
    total,
    mixed,
    hidden,
    weights,
    tokens,
    feed_grad,
    stage,
    arrived_tile,
    half_out,
    half_in,
    cross_out,
    cross_in,
    sums,
    sums_in,
    head_sums,
    head_sums_in,
    last_norm,
    last_head,
    zs,
    zr,
    xs,
    xr,
    ns,
    nr,
    gs,
    gr,
    ls,
    rxs,
    rxr,
    rzs,
    rzr,
    stage_sem,
    tile_sem,
    come_sem,
    free_core,
    free_other,
):
    place = Place(wide, 4)
    depth = place.depth
    size, width = x_in.shape
    block = width // wide
    inside = block % HD == 0
    ff = hidden.shape[1]
    groups = heads // pairs
    span = 4 * size
    full = [full_qkv, full_out, full_gate, full_up, full_down]
    away = [away_qkv, away_out, away_gate, away_up, away_down]
    got = [got_qkv, got_out, got_gate, got_up, got_down]
    home = [home_qkv, home_out, home_gate, home_up, home_down]
    come = [come_qkv, come_out, come_gate, come_up, come_down]
    relay = [relay_qkv, relay_out, relay_gate, relay_up, relay_down]
    widths = [ref.shape[1] for ref in full]
    qkv_width, out_width = widths[0], widths[1]
    chunks = chunks_of(widths)
    ag = Wide(place, block, chunks, full, zs, zr, xs, xr)
    side = Side(place, ns, nr)
    copies = []
    quarter = size // 4

    def keep(src, dst):
        made = pltpu.make_async_copy(src, dst, ls.at[len(copies)])
        made.start()
        copies.append(made)
        return made

    def fetch(*pairs_of):
        made = [keep(src, dst) for src, dst in pairs_of]
        for one in made:
            one.wait()

    def in_order(ref, buf, out=False):
        if not inside:
            return [keep(buf, ref) if out else keep(ref, buf)]
        made = []
        for b in range(wide):
            w, _ = place.far(b % depth, b // depth)
            there = ref.at[:, pl.ds(pl.multiple_of(w * block, block), block)]
            here = buf.at[:, pl.ds(b * block, block)]
            made.append(keep(here, there) if out else keep(there, here))
        return made

    def land(g, buf):
        if not inside:
            return [keep([w_query, w_keyval, w_output, w_gateup, w_down][g], full[g].at[0:block])]
        if g == 0:
            at, made = 0, []
            for ref in (w_query, w_keyval.at[0], w_keyval.at[1]):
                made.append(keep(ref, buf.at[:, pl.ds(at, ref.shape[1])]))
                at += ref.shape[1]
            return made
        if g in (2, 3):
            return [keep(w_gateup.at[g - 2], buf.at[:, pl.ds(0, widths[g])])]
        ref = w_output if g == 1 else w_down
        return [
            keep(ref.at[pl.ds(i * block, block)], buf.at[:, pl.ds(i * block, block)])
            for i in range(widths[g] // block)
        ]

    def settle(g, buf, made):
        for one in made:
            one.wait()
        if not inside:
            return
        slot = g % 2
        if g in (1, 4):
            for i in range(widths[g] // block):
                at = pl.ds(i * block, block)
                stage[slot, :, at] = buf[:, at].T.astype(bf16)
        else:

            def cast(i):
                at = rows(i, block // 4)
                stage[slot, at, pl.ds(0, widths[g])] = buf[at, 0 : widths[g]].astype(bf16)

            loop(4, cast)
        fetch((stage.at[slot, :, pl.ds(0, widths[g])], full[g].at[pl.ds(0, block)]))

    waiting = []

    def flush():
        while waiting:
            waiting.pop(0)()

    landing = land(0, total)
    greet(place)
    landing_out = land(1, resid)
    x_copies = in_order(x_in, tokens.at[pl.ds(0, size)])
    dy_copies = in_order(dy_in, dyb_ref)
    part = head_ref.shape[1]
    gain_ref[...] = jnp.zeros_like(gain_ref)
    gain_ref[0:2, 0:part] = head_ref[...]
    spread = pltpu.roll(gain_ref[:, 0:HD], place.w * part, 1)
    gain_ref[:, 0:HD] = pltpu.roll(spread, 2, 0)
    gain_ref[0:2, 0:block] = norm_ref[...]
    gain_ref[...] = gain_ref[...].astype(bf16).astype(f32)

    await_greetings(place)

    gain_copies = []
    for dx in (0, 1):
        for k in range(depth):
            if k or dx:
                at = dx * depth + (depth - k) % depth
                made = remote(gain_ref, slots.at[at], gs.at[at], gr.at[at], place.far(k, dx))
                made.start()
                gain_copies.append(made)
    settle(0, total, landing)
    ag.issue(0)
    ag.issue(1)
    landing = land(2, total)
    settle(1, resid, landing_out)
    ag.issue(2)
    landing_up = land(3, resid)
    window = 3

    def hand(i):
        flush()
        ag.hand_on(i)
        ag.issue(i + window)

    settle(2, total, landing)
    landing = land(4, total)
    settle(3, resid, landing_up)
    slots[0] = gain_ref[...]
    for made in gain_copies:
        made.wait_recv()
    gains[...] = jnp.concatenate([slots[b][:, :block] for b in range(wide)], axis=1)
    heads_row = slots[0][:, :HD]
    for b in range(1, wide):
        heads_row = heads_row + slots[b][:, :HD]
    head_gain[...] = heads_row
    for made in x_copies:
        made.wait()

    def first_norm(i):
        at = rows(i, quarter)
        x = tokens[at, :].astype(f32)
        cross_out[at, :] = (x * row_scale(x) * gains[0:1, :]).astype(bf16)

    loop(4, first_norm)
    take_normed = Gather(side, cross_out, all_normed, size)
    normed_copy = keep(cross_out, all_normed.at[pl.ds(0, size)])
    settle(4, total, landing)
    hand(0)
    length = length_ref[0]
    for made in dy_copies:
        made.wait()

    def mask(i):
        at = rows(i, quarter)
        value = dyb_ref[at, :].astype(f32)
        where = place.n * size + i * quarter + lax.broadcasted_iota(jnp.int32, value.shape, 0)
        dyb_ref[at, :] = jnp.where(where < length, value, 0.0).astype(bf16)

    loop(4, mask)
    take_dyb = Gather(side, dyb_ref, all_dyb, size)
    dyb_copy = keep(dyb_ref, all_dyb.at[pl.ds(0, size)])
    hand(1)
    take_normed.forward()
    take_dyb.forward()
    hand(2)
    take_dyb.done()
    dyb_copy.wait()
    take_normed.done()
    normed_copy.wait()
    ag.arrived(0)
    ag.arrived(1)

    def keys_of(p, qkv, k_act, v_act):
        for a in range(4):
            at = rows(place.slot(a), size)
            to = pl.ds(a * size, size)
            raw = qkv[at, pl.ds(pl.multiple_of((heads + p) * HD, HD), HD)]
            unit = raw * row_scale(raw) * head_gain[3:4, :]
            k_act[to, :] = rope(unit, cos_ref[to, :], sin_ref[to, :]).astype(bf16)
            v_act[to, :] = qkv[
                at, pl.ds(pl.multiple_of((heads + pairs + p) * HD, HD), HD)
            ].astype(bf16)

    def attention(normed, qkv, k_act, v_act):
        fetch((all_normed, normed), (full_qkv, weights.at[:, pl.ds(0, qkv_width)]))

        def project(m):
            for n in range(qkv_width // 512):
                qkv[rows(m, size), pl.ds(n * 512, 512)] = dot_nn(
                    normed[rows(m, size), :], weights[:, pl.ds(n * 512, 512)]
                )

        loop(4, project)
        qkv_copy = keep(qkv, all_qkv)

        def pair(p):
            keys_of(p, qkv, k_act, v_act)

            def head(g):
                column = pl.ds(pl.multiple_of((p * groups + g) * HD, HD), HD)
                for a in range(4):
                    at = rows(place.slot(a), size)
                    to = pl.ds(a * size, size)
                    raw = qkv[at, column]
                    unit = raw * row_scale(raw) * head_gain[2:3, :]
                    query = rope(unit, cos_ref[to, :], sin_ref[to, :]).astype(bf16)
                    last = (a + 1) * size
                    probs = softmax_block(query, k_act[0:last, :], a, size, last, length)
                    ctx[at, column] = dot_nn(probs.astype(bf16), v_act[0:last, :]).astype(bf16)

            loop(groups, head)

        hand(3)
        for p in range(pairs):
            pair(p)
        qkv_copy.wait()

    pl.run_scoped(
        attention,
        pltpu.VMEM((span, width), bf16),
        pltpu.VMEM((span, qkv_width), f32),
        pltpu.VMEM((span, HD), bf16),
        pltpu.VMEM((span, HD), bf16),
    )
    ag.arrived(2)
    fetch((full_out, weights.at[:, pl.ds(0, out_width)]))
    step = 512

    class Scatter:
        def __init__(self, tile):
            self.tile = tile

        def half(self):
            flush()

            def one(n):
                half_out[:, rows(n, step)] = self.tile(2 * size, 2 * size, n).astype(bf16)

            loop(width // step, one)
            self.core = side.copy(half_out, half_in, 0, 1)

        def own(self):
            flush()

            def one(n):
                total[:, rows(n, step)] = self.tile(0, size, n)

            loop(width // step, one)

        def rest(self):
            flush()
            self.core.wait_recv()
            side.drain()

            def one(n):
                at = rows(n, step)
                part = self.tile(size, size, n) + half_in[pl.ds(size, size), at].astype(f32)
                cross_out[:, at] = part.astype(bf16)

            loop(width // step, one)
            self.other = side.copy(cross_out, cross_in, 1, 0)

            def add(i):
                at = rows(i, quarter)
                total[at, :] += half_in[at, :].astype(f32)

            loop(4, add)

        def done(self):
            flush()
            self.other.wait_recv()

    def out_tile(start, count, n):
        return dot_nt(ctx[pl.ds(start, count), :], weights[rows(n, step), pl.ds(0, out_width)])

    summed_out = Scatter(out_tile)
    summed_out.half()
    summed_out.own()
    hand(4)
    hand(5)
    summed_out.rest()
    summed_out.done()

    def second_norm(i):
        at = rows(i, quarter)
        value = tokens[at, :].astype(f32) + total[at, :] + cross_in[at, :].astype(f32)
        resid[at, :] = value
        mixed[at, :] = (value * row_scale(value) * gains[1:2, :]).astype(bf16)

    loop(4, second_norm)
    take_mixed = Gather(side, mixed.at[pl.ds(0, size)], mixed, size)
    hand(6)
    take_mixed.forward()
    take_mixed.done()
    hand(7)
    half = ff // 2
    tile = 256

    piece = max(block, HD)
    steps = depth * block // piece
    held = piece // block

    def staged(g, slot, to):
        return pltpu.make_async_copy(
            stage.at[slot, :, pl.ds(0, full[g].shape[1])], to, stage_sem.at[slot]
        )

    def part_of(ref, t):
        return ref.at[rows(t, piece)]

    def cross(g, t):
        return remote(
            part_of(away[g], t), part_of(got[g], t), rxs.at[g, t], rxr.at[g, t], place.far(0, 1)
        )

    def hand_over(g, k):
        return remote(
            home[g].at[rows(k, block)],
            come[g].at[rows(k - 1, block)],
            rzs.at[g, k],
            rzr.at[g, k],
            place.far(k, 0),
        )

    beside, beyond = 1 + 2 * ag.odd, 3 - 2 * ag.odd

    def lean_over(g):
        return remote(
            part_of(away[g], beside),
            aside,
            rxs.at[g, beside],
            rxr.at[g, depth],
            place.far(beside, 0),
        )

    def relay_over(g):
        return remote(
            part_of(home[g], beyond),
            relay[g],
            rzs.at[g, beyond],
            rzr.at[g, 0],
            place.far(depth - beyond, 0),
        )

    def add_to_stage(g, slot, src, made):
        wide_g = widths[g]
        made.wait_recv()
        more = pltpu.make_async_copy(src, arrived_tile.at[:, pl.ds(0, wide_g)], tile_sem)
        more.start()
        more.wait()
        stage[slot, :, 0:wide_g] = (
            stage[slot, :, 0:wide_g].astype(f32) + arrived_tile[:, 0:wide_g].astype(f32)
        ).astype(bf16)

    operands = {}
    turns = [0]
    gone = {g: 0 for g in range(5)}
    come_home = {g: 0 for g in range(5)}

    def known(t, value):
        return isinstance(t, int) and t == value

    def product(g, t):
        left, right = operands[g]
        return dot_tn(left[:, rows(t, piece)], right())

    def send(g, t, lean=False):
        wide_g = widths[g]
        made = product(g, steps + t)
        flush()
        slot = turns[0] % 2
        turns[0] += 1
        stage[slot, :, 0:wide_g] = made.astype(bf16)
        if lean and known(t, 0):
            add_to_stage(g, slot, aside, lean_over(g))
        staged(g, slot, part_of(away[g], t)).start()

        def finish():
            staged(g, slot, part_of(away[g], t)).wait()
            if lean and t is beside:
                lean_over(g).start()
            else:
                cross(g, t).start()

        waiting.append(finish)

    late = []
    in_stage = []

    def take(g, t, bare=False):
        wide_g = widths[g]
        slot = turns[0] % 2
        turns[0] += 1
        if bare:
            made = product(g, t)
            flush()
            stage[slot, :, 0:wide_g] = made.astype(bf16)
        else:
            if not late:
                flush()
            cross(g, t).wait_recv()
            get = pltpu.make_async_copy(
                part_of(got[g], t), arrived_tile.at[:, pl.ds(0, wide_g)], tile_sem
            )
            get.start()
            made = product(g, t)
            flush()
            get.wait()
            made = made + arrived_tile[:, 0:wide_g].astype(f32)
            stage[slot, :, 0:wide_g] = made.astype(bf16)
        if ag.near and known(t, 2):

            @pl.when((place.z == 1) | (place.z == 2))
            def _():
                add_to_stage(g, slot, relay[g], relay_over(g))

        if ag.near and g == 0 and known(t, 0):
            in_stage.append(slot)
            return
        staged(g, slot, part_of(home[g], t)).start()

        def finish():
            staged(g, slot, part_of(home[g], t)).wait()
            if ag.near:
                if t is beyond:
                    at_end = (place.z == 0) | (place.z == 3)

                    @pl.when(at_end)
                    def _():
                        relay_over(g).start()

                    @pl.when(jnp.logical_not(at_end))
                    def _():
                        hand_over(g, t).start()
                elif not known(t, 0):
                    hand_over(g, t).start()
                return
            for r in range(held):
                if t * held + r:
                    hand_over(g, t * held + r).start()

        waiting.append(finish)

    def away_step(g):
        i = gone[g]
        gone[g] += 1
        if not ag.near:
            for t in range(steps) if i == 0 else ():
                send(g, t)
            return
        lean = g == 4
        send(g, ((beside, beyond, 2, 0) if lean else (beyond, beside, 2, 0))[i], lean)

    def home_step(g, which):
        come_home[g] += 1
        if not ag.near:
            for t in tuple(range(1, steps)) + (0,) if come_home[g] == 4 else ():
                take(g, t)
            return
        lean = g == 4
        order = (beside, beyond, 2, 0) if lean else (beyond, beside, 2, 0)
        take(g, order[which], lean and which == 0)

    tokens_copy = keep(all_dyb, tokens)

    def feed_forward(gate, up):
        def feed(part):
            a = part * half
            fetch(
                (full_gate.at[:, pl.ds(a, half)], weights.at[:, pl.ds(0, half)]),
                (full_up.at[:, pl.ds(a, half)], weights.at[:, pl.ds(half, half)]),
            )

            def columns(n):
                def body(m):
                    at = rows(m, size)
                    left = mixed[at, :]
                    gate_part = dot_nn(left, weights[:, rows(n, tile)])
                    up_part = dot_nn(
                        left, weights[:, pl.ds(pl.multiple_of(half + n * tile, tile), tile)]
                    )
                    to = pl.ds(pl.multiple_of(a + n * tile, tile), tile)
                    gate[at, to] = gate_part
                    up[at, to] = up_part
                    hidden[at, to] = (gate_part * jax.nn.sigmoid(gate_part) * up_part).astype(bf16)

                loop(4, body)

            loop(half // tile, columns)

        ag.arrived(3)
        ag.arrived(4)
        feed(0)
        hand(8)
        ag.arrived(5)
        ag.arrived(6)
        feed(1)
        tokens_copy.wait()
        operands[4] = tokens, lambda: hidden[...]
        away_step(4)
        away_step(4)
        away_step(4)
        home_step(4, 0)
        flush()
        ag.arrived(7)
        ag.arrived(8)
        fetch((full_down, weights))

        def columns(n):
            def body(m):
                at = rows(m, size)
                to = rows(n, tile)
                grad = dot_nn(tokens[at, :], weights[:, to])
                gate_part = gate[at, to]
                up_part = up[at, to]
                sigma = jax.nn.sigmoid(gate_part)
                feed_grad[at, to] = (
                    grad * up_part * sigma * (1.0 + gate_part * (1.0 - sigma))
                ).astype(bf16)
                feed_grad[at, pl.ds(pl.multiple_of(ff + n * tile, tile), tile)] = (
                    grad * gate_part * sigma
                ).astype(bf16)

            loop(4, body)

        loop(ff // tile, columns)

    pl.run_scoped(feed_forward, pltpu.VMEM((span, ff), f32), pltpu.VMEM((span, ff), f32))

    operands[2] = mixed, lambda: feed_grad[:, pl.ds(0, ff)]
    operands[3] = mixed, lambda: feed_grad[:, pl.ds(ff, ff)]
    away_step(3)
    away_step(2)
    away_step(3)
    flush()

    def mixed_grad(both):
        fetch(
            (full_gate, both.at[:, pl.ds(0, ff)]),
            (full_up, both.at[:, pl.ds(ff, ff)]),
        )

        def mixed_tile(start, count, n):
            return dot_nt(feed_grad[pl.ds(start, count), :], both[rows(n, step), :])

        summed.append(Scatter(mixed_tile))
        summed[0].half()
        summed[0].own()
        summed[0].rest()

    summed = []
    pl.run_scoped(mixed_grad, pltpu.VMEM((width, 2 * ff), bf16))
    home_step(4, 1)
    home_step(2, 0)
    home_step(4, 2)
    away_step(2)
    away_step(4)
    away_step(2)
    home_step(3, 1)
    away_step(2)
    summed[0].done()
    sums[...] = jnp.zeros_like(sums)
    head_sums[...] = jnp.zeros_like(head_sums)

    def second_back(i):
        at = rows(i, quarter)
        value = resid[at, :]
        scale = row_scale(value)
        unit = value * scale
        grad = total[at, :] + cross_in[at, :].astype(f32)
        sums[1:2, :] += jnp.sum(grad * unit, axis=0, keepdims=True)
        back = norm_back(grad, unit, scale, gains[1:2, :])
        result = dyb_ref[at, :].astype(f32) + back
        grad_own[at, :] = result
        cross_out[at, :] = result.astype(bf16)

    side.drain()
    loop(4, second_back)
    take_dresb = Gather(side, cross_out, all_dresb, size)
    dresb_copy = keep(cross_out, all_dresb.at[pl.ds(0, size)])
    take_dresb.core.wait_recv()
    away_step(3)

    def down_tile(start, count, n):
        return dot_nt(hidden[pl.ds(start, count), :], weights[rows(n, step), :])

    summed_down = Scatter(down_tile)
    summed_down.half()
    home_step(2, 1)
    summed_down.own()
    home_step(4, 3)
    home_step(3, 0)
    flush()
    take_dresb.forward()
    dresb_copy.wait()
    summed_down.rest()
    pl.semaphore_signal(free_core, inc=1, device_id=place.side(0, 1), device_id_type=MESH)
    take_dresb.last.wait_recv()

    late.append(True)

    def attention_back(qkv_grad, qkv, k_act, v_act, ctx_grad, k_grad, v_grad):
        fetch(
            (all_dresb, tokens),
            (all_qkv, qkv),
            (full_out, weights.at[:, pl.ds(0, out_width)]),
        )

        operands[1] = tokens, lambda: ctx[...]

        def context_grad(m):
            ctx_grad[rows(m, size), :] = dot_nn(
                tokens[rows(m, size), :], weights[:, pl.ds(0, out_width)]
            ).astype(bf16)

        loop(4, context_grad)

        def head_back(raw, grad, gain, a):
            to = pl.ds(a * size, size)
            scale = row_scale(raw)
            unit = raw * scale
            turned = rope_back(grad, cos_ref[to, :], sin_ref[to, :])
            gain_part = jnp.sum(turned * unit, axis=0, keepdims=True)
            return norm_back(turned, unit, scale, gain).astype(bf16), gain_part

        def pair(p):
            keys_of(p, qkv, k_act, v_act)
            k_grad[...] = jnp.zeros_like(k_grad)
            v_grad[...] = jnp.zeros_like(v_grad)

            def head(g):
                column = pl.ds(pl.multiple_of((p * groups + g) * HD, HD), HD)
                for a in range(4):
                    at = rows(place.slot(a), size)
                    to = pl.ds(a * size, size)
                    last = (a + 1) * size
                    raw = qkv[at, column]
                    unit = raw * row_scale(raw) * head_gain[2:3, :]
                    query = rope(unit, cos_ref[to, :], sin_ref[to, :]).astype(bf16)
                    probs = softmax_block(query, k_act[0:last, :], a, size, last, length)
                    grad = ctx_grad[at, column]
                    probs_grad = dot_nt(grad, v_act[0:last, :])
                    v_grad[0:last, :] += dot_tn(probs.astype(bf16), grad)
                    delta = jnp.sum(probs * probs_grad, axis=-1, keepdims=True)
                    scores_grad = (probs * (probs_grad - delta)).astype(bf16)
                    query_grad = dot_nn(scores_grad, k_act[0:last, :]) * HD ** (-0.5)
                    k_grad[0:last, :] += dot_tn(scores_grad, query) * HD ** (-0.5)
                    made, gain_part = head_back(raw, query_grad, head_gain[2:3, :], a)
                    qkv_grad[at, column] = made
                    head_sums[0:1, :] += gain_part

            loop(groups, head)
            for a in range(4):
                at = rows(place.slot(a), size)
                to = pl.ds(a * size, size)
                column = pl.ds(pl.multiple_of((heads + p) * HD, HD), HD)
                made, gain_part = head_back(
                    qkv[at, column], k_grad[to, :], head_gain[3:4, :], a
                )
                qkv_grad[at, column] = made
                head_sums[1:2, :] += gain_part
                column = pl.ds(pl.multiple_of((heads + pairs + p) * HD, HD), HD)
                qkv_grad[at, column] = v_grad[to, :].astype(bf16)

        pair(0)
        home_step(2, 2)
        away_step(1)
        flush()
        summed_down.done()
        side.drain()

        def last_sum(i):
            at = rows(i, quarter)
            value = resid[at, :] + total[at, :] + cross_in[at, :].astype(f32)
            cross_out[at, :] = value.astype(bf16)

        loop(4, last_sum)
        results.extend(in_order(o_out, cross_out, out=True))
        pl.semaphore_signal(free_other, inc=1, device_id=place.side(1, 0), device_id_type=MESH)
        for p in range(1, pairs):
            pair(p)
        for made in results:
            made.wait()

    results = []

    def finish_back(qkv_grad, normed, come_v, home_v, sum_v, sum_t):
        normed_copy = keep(all_normed, normed)
        qkv_copy = keep(full_qkv, weights.at[:, pl.ds(0, qkv_width)])
        operands[0] = normed, lambda: qkv_grad[...]
        normed_copy.wait()
        away_step(0)
        away_step(0)
        away_step(1)
        flush()
        qkv_copy.wait()
        written = []

        def finals(g):
            flush()
            wide_g = widths[g]
            kept = in_stage if g == 0 else []
            if not kept:
                mine = keep(home[g].at[pl.ds(0, block)], home_v.at[:, pl.ds(0, wide_g)])

            def slot_of(k):
                return pl.ds((k - 1) * block, block)

            def bring(k):
                return pltpu.make_async_copy(
                    come[g].at[slot_of(k)], come_v.at[slot_of(k), pl.ds(0, wide_g)], come_sem.at[k]
                )

            def begin(k):
                hand_over(g, k).wait_recv()
                bring(k).start()

            def none(k):
                come_v[slot_of(k), 0:wide_g] = jnp.zeros((block, wide_g), bf16)

            for act, other in ((begin, none), (lambda k: bring(k).wait(), None)):
                for k in (1, 3, 2) if ag.near else range(1, depth):
                    if ag.near and k in (1, 3):
                        here = place.z != (0 if k == 1 else 3)
                        pl.when(here)(functools.partial(act, k))
                        if other is not None:
                            pl.when(jnp.logical_not(here))(functools.partial(other, k))
                    else:
                        act(k)
            if not kept:
                mine.wait()
            while written:
                written.pop().wait()

            def add(i):
                at = rows(i, block // 4)
                if kept:
                    value = stage[kept[0], at, 0:wide_g].astype(f32)
                else:
                    value = home_v[at, 0:wide_g].astype(f32)
                for k in range(1, depth):
                    more = pl.ds(
                        pl.multiple_of((k - 1) * block + i * (block // 4), block // 4), block // 4
                    )
                    value = value + come_v[more, 0:wide_g].astype(f32)
                sum_v[at, 0:wide_g] = value

            loop(4, add)
            if g in (1, 4):
                for i in range(wide_g // HD):
                    sum_t[pl.ds(i * HD, HD), :] = sum_v[:, i * HD : (i + 1) * HD].T
                ref = o_output if g == 1 else o_down
                written.append(keep(sum_t.at[pl.ds(0, wide_g)], ref))
            elif g == 0:
                ends = (o_query, o_keyval.at[0], o_keyval.at[1])
                columns = (heads * HD, pairs * HD, pairs * HD)
                at = 0
                for ref, count in zip(ends, columns, strict=True):
                    written.append(keep(sum_v.at[:, pl.ds(at, count)], ref))
                    at += count
            else:
                written.append(keep(sum_v.at[:, pl.ds(0, wide_g)], o_gateup.at[g - 2]))

        def normed_tile(start, count, n):
            return dot_nt(
                qkv_grad[pl.ds(start, count), :], weights[rows(n, step), pl.ds(0, qkv_width)]
            )

        summed_normed = Scatter(normed_tile)
        pl.semaphore_wait(free_core, 1)
        summed_normed.half()
        home_step(1, 0)
        summed_normed.own()
        home_step(3, 2)
        pl.semaphore_wait(free_other, 1)
        summed_normed.rest()
        x_again = in_order(x_in, half_out.at[pl.ds(0, size)])
        home_step(2, 3)
        away_step(0)
        away_step(1)
        finals(4)
        away_step(1)
        home_step(0, 1)
        finals(2)
        home_step(1, 1)
        away_step(3)
        home_step(0, 0)
        summed_normed.done()
        for made in x_again:
            made.wait()

        def first_back(i):
            at = rows(i, quarter)
            value = half_out[at, :].astype(f32)
            scale = row_scale(value)
            unit = value * scale
            grad = total[at, :] + cross_in[at, :].astype(f32)
            sums[0:1, :] += jnp.sum(grad * unit, axis=0, keepdims=True)
            grad_own[at, :] += norm_back(grad, unit, scale, gains[0:1, :])

        loop(4, first_back)
        grads = in_order(o_grad, grad_own, out=True)

        def trade(flip, dy, dc):
            return (
                side.copy(sums, sums_in.at[flip], dy, dc),
                side.copy(head_sums, head_sums_in.at[flip], dy, dc),
            )

        def add_trade(flip, made):
            flush()
            for one in made:
                one.wait_recv()
            side.drain()
            sums[...] += sums_in[flip]
            head_sums[...] += head_sums_in[flip]

        made = trade(0, 0, 1)
        home_step(1, 2)
        add_trade(0, made)
        made = trade(1, 1, 0)
        home_step(1, 3)
        away_step(0)
        home_step(0, 2)
        add_trade(1, made)
        for made in gain_copies:
            made.wait_send()
        for b in range(wide):
            slots[b, :, 0:block] = sums[:, b * block : (b + 1) * block]
        last = []
        for dx in (0, 1):
            for k in range(depth):
                if k or dx:
                    to = dx * depth + k
                    at = dx * depth + (depth - k) % depth
                    made = remote(
                        slots.at[to], last_norm.at[at], gs.at[at], gr.at[at], place.far(k, dx)
                    )
                    made.start()
                    last.append(made)
                    made = remote(
                        head_sums,
                        last_head.at[at],
                        gs.at[wide + at],
                        gr.at[wide + at],
                        place.far(k, dx),
                    )
                    made.start()
                    last.append(made)
        home_step(3, 3)
        finals(3)
        finals(1)
        home_step(0, 3)
        finals(0)
        for made in grads + written:
            made.wait()
        for made in last:
            made.wait_recv()
        norm_total = slots[0]
        head_total = head_sums[...]
        for b in range(1, wide):
            norm_total = norm_total + last_norm[b]
            head_total = head_total + last_head[b]
        o_norm[...] = norm_total
        o_head[...] = head_total
        for made in last:
            made.wait_send()

    def back(qkv_grad):
        pl.run_scoped(
            functools.partial(attention_back, qkv_grad),
            pltpu.VMEM((span, qkv_width), f32),
            pltpu.VMEM((span, HD), bf16),
            pltpu.VMEM((span, HD), bf16),
            pltpu.VMEM((span, out_width), bf16),
            pltpu.VMEM((span, HD), f32),
            pltpu.VMEM((span, HD), f32),
        )
        pl.run_scoped(
            functools.partial(finish_back, qkv_grad),
            pltpu.VMEM((span, width), bf16),
            pltpu.VMEM(((depth - 1) * block, max(widths)), bf16),
            pltpu.VMEM((block, max(widths)), bf16),
            pltpu.VMEM((block, max(widths)), f32),
            pltpu.VMEM((max(widths), block), f32),
        )

    pl.run_scoped(back, pltpu.VMEM((span, qkv_width), bf16))
    for g in range(5):
        for t in range(steps):
            cross(g, t).wait_send()
        for k in range(1, depth):
            hand_over(g, k).wait_send()
    side.drain()
    ag.drain()


def layer_call(lengths, norm_gains, head_gains, x, dy, weights, heads, pairs):
    wide = lax.axis_size("wide")
    depth = wide // 2
    size, width = x.shape
    span = 4 * size
    block = width // wide
    inside = block % HD == 0
    ff = weights[3].shape[-1]
    widths = [(heads + 2 * pairs) * HD, heads * HD, ff, ff, ff]
    lanes = max(HD, block)
    shape = jax.ShapeDtypeStruct
    anywhere = pl.BlockSpec(memory_space=pl.ANY)
    vmem = pl.BlockSpec(memory_space=pltpu.VMEM)
    smem = pl.BlockSpec(memory_space=pltpu.SMEM)
    count = len(chunks_of(widths))
    cosine, sine = rope_tables(span)
    outs = [
        shape((8, lanes), f32),
        shape((8, HD), f32),
        shape((size, width), bf16),
        shape((size, width), f32),
        shape((block, heads * HD), f32),
        shape((2, block, pairs * HD), f32),
        shape((heads * HD, block), f32),
        shape((2, block, ff), f32),
        shape((ff, block), f32),
    ]
    outs += [shape((width // 2, w), bf16) for w in widths]
    outs += [shape(((depth - 1) * block, w), bf16) for w in widths]
    outs += [shape((width, w), bf16) for w in widths]
    outs += [shape((width // 2, w), bf16) for w in widths] * 2
    outs += [shape((block, w), bf16) for w in widths]
    outs += [shape((block, ff), bf16)]
    outs += [
        shape((span, width), bf16),
        shape((span, width), bf16),
        shape((span, widths[0]), f32),
        shape((span, width), bf16),
    ]
    dma = pltpu.SemaphoreType.DMA
    if not inside:
        query, keyval, output, gateup, down = [w.astype(bf16) for w in weights]
        weights = [
            jnp.concatenate([query, keyval[0], keyval[1]], axis=1),
            output.T,
            gateup[0],
            gateup[1],
            down.T,
        ]
        owner, place = owners(wide), places(wide)
        x, dy = reorder(x, owner), reorder(dy, owner)
    results = pl.pallas_call(
        functools.partial(layer_kernel, wide, heads, pairs),
        out_shape=outs,
        in_specs=[smem] + [vmem] * 4 + [anywhere] * 7,
        out_specs=[vmem] * 2 + [anywhere] * (len(outs) - 2),
        scratch_shapes=[
            pltpu.VMEM((size, width), bf16),
            pltpu.VMEM((size, width), f32),
            pltpu.VMEM((8, lanes), f32),
            pltpu.VMEM((wide, 8, lanes), f32),
            pltpu.VMEM((8, width), f32),
            pltpu.VMEM((8, HD), f32),
            pltpu.VMEM((span, widths[1]), bf16),
            pltpu.VMEM((size, width), f32),
            pltpu.VMEM((size, width), f32),
            pltpu.VMEM((span, width), bf16),
            pltpu.VMEM((span, ff), bf16),
            pltpu.VMEM((width, ff), bf16),
            pltpu.VMEM((span, width), bf16),
            pltpu.VMEM((span, 2 * ff), bf16),
            pltpu.VMEM((2, max(block, HD), max(widths)), bf16),
            pltpu.VMEM((max(block, HD), max(widths)), bf16),
            pltpu.VMEM((2 * size, width), bf16),
            pltpu.VMEM((2 * size, width), bf16),
            pltpu.VMEM((size, width), bf16),
            pltpu.VMEM((size, width), bf16),
            pltpu.VMEM((8, width), f32),
            pltpu.VMEM((2, 8, width), f32),
            pltpu.VMEM((8, HD), f32),
            pltpu.VMEM((2, 8, HD), f32),
            pltpu.VMEM((wide, 8, lanes), f32),
            pltpu.VMEM((wide, 8, HD), f32),
            dma((count, 2 * depth)),
            dma((count, depth)),
            dma((count, depth)),
            dma((count, depth)),
            dma((40,)),
            dma((40,)),
            dma((2 * wide,)),
            dma((2 * wide,)),
            dma((160,)),
            dma((5, depth)),
            dma((5, depth + 1)),
            dma((5, depth)),
            dma((5, depth)),
            dma((2,)),
            dma,
            dma((depth,)),
            pltpu.SemaphoreType.REGULAR,
            pltpu.SemaphoreType.REGULAR,
        ],
        compiler_params=pltpu.CompilerParams(
            collective_id=0, has_side_effects=True, vmem_limit_bytes=63 * MIB
        ),
    )(lengths, norm_gains, head_gains, cosine, sine, x, dy, *weights)
    results = list(results[:9])
    if not inside:
        results[2] = reorder(results[2], place)
        results[3] = reorder(results[3], place)
    return results


def per_device(
    layer_input,
    out_grad,
    lengths,
    query_weight,
    query_mean,
    query_square,
    keyval_weight,
    keyval_mean,
    keyval_square,
    output_weight,
    output_mean,
    output_square,
    gateup_weight,
    gateup_mean,
    gateup_square,
    down_weight,
    down_mean,
    down_square,
    norm_gains,
    norm_mean,
    norm_square,
    head_gains,
    head_mean,
    head_square,
):
    wide = lax.axis_size("wide")
    w = lax.axis_index("wide")
    block = layer_input.shape[2] // wide
    heads = query_weight.shape[1] // HD
    pairs = keyval_weight.shape[2] // HD
    weights = [query_weight, keyval_weight, output_weight, gateup_weight, down_weight]
    results = layer_call(
        lengths, norm_gains, head_gains, layer_input[0], out_grad[0], weights, heads, pairs
    )
    norm_total = results[0][0:2, 0:block]
    part = HD // wide
    head_total = lax.dynamic_slice(results[1], (0, w * part), (2, part))
    layer_out, input_grad = results[2][None], results[3][None]
    query_total, keyval_total, output_total, gateup_total, down_total = results[4:]
    query = adamw(query_weight, query_mean, query_square, query_total, 0.04)
    keyval = adamw(keyval_weight, keyval_mean, keyval_square, keyval_total, 0.04)
    output = adamw(output_weight, output_mean, output_square, output_total, 0.3)
    gateup = adamw(gateup_weight, gateup_mean, gateup_square, gateup_total, 0.04)
    down = adamw(down_weight, down_mean, down_square, down_total, 0.025)
    norm = adamw(norm_gains, norm_mean, norm_square, norm_total, 0.4)
    head = adamw(head_gains, head_mean, head_square, head_total, 0.4)
    return (layer_out, input_grad, *query, *keyval, *output, *gateup, *down, *norm, *head)


def solution(mesh):
    tokens = P("wide", "narrow", None)
    down = [P("wide", "narrow")] * 3
    pair = [P(None, "wide", "narrow")] * 3
    across = [P("narrow", "wide")] * 3
    gain = [P(None, "wide")] * 3
    weights = down + pair + across + pair + across + gain + gain
    return jax.shard_map(
        per_device,
        mesh=mesh,
        in_specs=(tokens, tokens, P("wide"), *weights),
        out_specs=(tokens, tokens, *weights),
        check_vma=False,
    )
```
